32 devices in a mesh: fsdp: 2 (over core), heads: 4 (over y, x), tensor: 4 (over z).
Axes of the slice: x: 2, y: 2, z: 4, core: 2. Of those that a mesh axis runs over, the one named last changes fastest.
Arguments:
- tokens: bfloat16 [8192, 1024], P(('fsdp', 'heads'), 'tensor'), may hold values from -6 to 6
- cotangent: bfloat16 [8192, 1024], P(('fsdp', 'heads'), 'tensor'), may hold values from -6 to 6
- lengths: int32 [4], replicated, may hold values from 512 to 3584, as said below
- norm_gain: float32 [1024], replicated, may hold values from 0.5 to 1.5
- query_weight: bfloat16 [1024, 1024], P('fsdp', 'tensor'), may hold values from -0.1875 to 0.1875
- key_weight: bfloat16 [1024, 1024], P('fsdp', 'tensor'), may hold values from -0.1875 to 0.1875
- value_weight: bfloat16 [1024, 2048], P('fsdp', 'tensor'), may hold values from -0.1875 to 0.1875
- outgate_weight: bfloat16 [1024, 2048], P('fsdp', 'tensor'), may hold values from -0.1875 to 0.1875
- alpha_weight: bfloat16 [1024, 8], P('fsdp', 'tensor'), may hold values from -0.1875 to 0.1875
- beta_weight: bfloat16 [1024, 8], P('fsdp', 'tensor'), may hold values from -0.1875 to 0.1875
- output_weight: bfloat16 [2048, 1024], P('tensor', 'fsdp'), may hold values from -0.25 to 0.25
- conv_query: float32 [4, 1024], replicated, may hold values from -3 to 3
- conv_key: float32 [4, 1024], replicated, may hold values from -3 to 3
- conv_value: float32 [4, 2048], replicated, may hold values from -3 to 3
- log_rate: float32 [8], replicated, may hold values from 0 to 2.77
- step_bias: float32 [8], replicated, may hold values from -6.9 to -2.3
- out_gain: float32 [256], replicated, may hold values from 0.5 to 1.5
- ffn_gain: float32 [1024], replicated, may hold values from 0.5 to 1.5
- gate_weight: bfloat16 [1024, 2816], P('fsdp', 'tensor'), may hold values from -0.1875 to 0.1875
- up_weight: bfloat16 [1024, 2816], P('fsdp', 'tensor'), may hold values from -0.1875 to 0.1875
- down_weight: bfloat16 [2816, 1024], P('tensor', 'fsdp'), may hold values from -0.109375 to 0.109375
Outputs:
- output: bfloat16 [8192, 1024], P(('fsdp', 'heads'), 'tensor')
- grad_tokens: float32 [8192, 1024], P(('fsdp', 'heads'), 'tensor')
- grad_query_weight: float32 [1024, 1024], P(('fsdp', 'heads'), 'tensor')
- grad_key_weight: float32 [1024, 1024], P(('fsdp', 'heads'), 'tensor')
- grad_value_weight: float32 [1024, 2048], P(('fsdp', 'heads'), 'tensor')
- grad_outgate_weight: float32 [1024, 2048], P(('fsdp', 'heads'), 'tensor')
- grad_alpha_weight: float32 [1024, 8], P(('fsdp', 'heads'), 'tensor')
- grad_beta_weight: float32 [1024, 8], P(('fsdp', 'heads'), 'tensor')
- grad_output_weight: float32 [2048, 1024], P('tensor', ('fsdp', 'heads'))
- grad_gate_weight: float32 [1024, 2816], P(('fsdp', 'heads'), 'tensor')
- grad_up_weight: float32 [1024, 2816], P(('fsdp', 'heads'), 'tensor')
- grad_down_weight: float32 [2816, 1024], P('tensor', ('fsdp', 'heads'))
- grad_conv_query: float32 [4, 1024], replicated
- grad_conv_key: float32 [4, 1024], replicated
- grad_conv_value: float32 [4, 2048], replicated
- grad_log_rate: float32 [8], replicated
- grad_step_bias: float32 [8], replicated
- grad_out_gain: float32 [256], replicated
- grad_norm_gain: float32 [1024], replicated
- grad_ffn_gain: float32 [1024], replicated
The draws below stay inside these ranges and needn't reach their ends.
Inputs may be any that keep to these rules, and one draw needn't show every extreme that they name: `lengths`: lengths of the packed sequences in token order; each is a multiple of 64, they add up to 8192, and each is shorter than 4096.
All inputs are finite; a program needn't handle non-finite values.
Results may differ from the reference program's by a relative error of at most 0.02.
Values may be sent and summed in bfloat16 or wider, within the bound.
No kernel may reach another device: no remote copies, remote signals or barrier semaphores. Data moves between devices by JAX's collectives and lax.ppermute only.
A program may use at most 192 MiB of HBM per device.

```python
import jax
import jax.numpy as jnp
from jax import lax

D = 1024
HEADS = 8
DK = 128
DV = 256
FF = 2816
CONV = 4
GROUP = 64
TOK_DEV = 1024
TOKENS = 8192
NSEQ = 4


def draw_lengths(key, part):
    key = jax.random.fold_in(key, 11)
    span_count = NSEQ // 2
    per_span = 4 * TOK_DEV // GROUP
    first_key, second_key, third_key = jax.random.split(key, 3)
    cut_first = jax.random.randint(first_key, (span_count,), per_span // 8, 3 * per_span // 8 + 1)
    cut_second = jax.random.randint(second_key, (span_count,), 0, per_span // 8 + 1)
    chosen = jax.random.randint(third_key, (), 0, span_count - 1)
    span_index = jnp.arange(span_count, dtype=jnp.int32)
    cut_second = jnp.where(span_index == chosen, 0, cut_second)
    cut_first = jnp.where(span_index == chosen + 1, 3 * per_span // 8, cut_first)
    cut_first = jnp.where(span_index == 0, 0, cut_first)
    span_base = span_index * per_span
    starts = jnp.stack([span_base + cut_first, span_base + per_span // 2 + cut_second], axis=1).reshape(-1)
    finishes = jnp.concatenate([starts[1:], jnp.full((1,), span_count * per_span, starts.dtype)])
    return ((finishes - starts) * GROUP).astype(jnp.int32)


def levels(stream_key, shape, cuts, least, top_value):
    gain = 1.0
    for dim, parts in cuts:
        heights = jax.random.uniform(jax.random.fold_in(jax.random.fold_in(stream_key, 6), dim), (parts,), jnp.float32, least / len(cuts), top_value / len(cuts))
        gain = gain * jnp.repeat(jnp.exp(heights), shape[dim] // parts).reshape((-1,) + (1,) * (len(shape) - 1 - dim))
    return gain


def bell_draw(own_key, dims, width, limit, cuts=(), kind=jnp.bfloat16):
    level = levels(own_key, dims, cuts, -0.22, 0.18) if cuts else 1.0
    values = jax.random.normal(own_key, dims, jnp.float32) * width * level
    return jnp.minimum(jnp.maximum(values, -limit), limit).astype(kind)


def setup_inputs(seed: int = 0) -> dict:
    keys = jax.random.split(jax.random.key(seed), 22)
    tokens = bell_draw(keys[0], (TOKENS, D), 1.0, 6.0, ((0, 8), (1, 4)))
    cotangent = bell_draw(keys[1], (TOKENS, D), 1.0, 6.0, ((0, 8), (1, 4)))
    lengths = draw_lengths(jax.random.fold_in(keys[21], 71), 0)
    norm_gain = jnp.clip(1.0 + 0.1 * jax.random.normal(keys[3], (D,), jnp.float32), 0.5, 1.5)
    query_weight = bell_draw(keys[4], (D, HEADS * DK), D ** -0.5, 0.1875, ((0, 2), (1, 4)))
    key_weight = bell_draw(keys[5], (D, HEADS * DK), D ** -0.5, 0.1875, ((0, 2), (1, 4)))
    value_weight = bell_draw(keys[6], (D, HEADS * DV), D ** -0.5, 0.1875, ((0, 2), (1, 4)))
    outgate_weight = bell_draw(keys[7], (D, HEADS * DV), D ** -0.5, 0.1875, ((0, 2), (1, 4)))
    alpha_weight = bell_draw(keys[8], (D, HEADS), D ** -0.5, 0.1875, ((0, 2), (1, 4)))
    beta_weight = bell_draw(keys[9], (D, HEADS), D ** -0.5, 0.1875, ((0, 2), (1, 4)))
    output_weight = bell_draw(keys[10], (HEADS * DV, D), (HEADS * DV // 4) ** -0.5, 0.25, ((0, 4), (1, 2)))
    conv_query = bell_draw(keys[11], (CONV, HEADS * DK), CONV ** -0.5, 3.0, (), jnp.float32)
    conv_key = bell_draw(keys[12], (CONV, HEADS * DK), CONV ** -0.5, 3.0, (), jnp.float32)
    conv_value = bell_draw(keys[13], (CONV, HEADS * DV), CONV ** -0.5, 3.0, (), jnp.float32)
    log_rate = jnp.clip(jax.random.uniform(keys[14], (HEADS,), jnp.float32, 0.0, 2.77), 0.0, 2.77)
    step_bias = jnp.clip(jax.random.uniform(keys[15], (HEADS,), jnp.float32, -6.9, -2.3), -6.9, -2.3)
    out_gain = jnp.clip(1.0 + 0.1 * jax.random.normal(keys[16], (DV,), jnp.float32), 0.5, 1.5)
    ffn_gain = jnp.clip(1.0 + 0.1 * jax.random.normal(keys[17], (D,), jnp.float32), 0.5, 1.5)
    gate_weight = bell_draw(keys[18], (D, FF), D ** -0.5, 0.1875, ((0, 2), (1, 4)))
    up_weight = bell_draw(keys[19], (D, FF), D ** -0.5, 0.1875, ((0, 2), (1, 4)))
    down_weight = bell_draw(keys[20], (FF, D), FF ** -0.5, 0.109375, ((0, 4), (1, 2)))
    return {"tokens": tokens, "cotangent": cotangent, "lengths": lengths, "norm_gain": norm_gain, "query_weight": query_weight, "key_weight": key_weight, "value_weight": value_weight, "outgate_weight": outgate_weight, "alpha_weight": alpha_weight, "beta_weight": beta_weight, "output_weight": output_weight, "conv_query": conv_query, "conv_key": conv_key, "conv_value": conv_value, "log_rate": log_rate, "step_bias": step_bias, "out_gain": out_gain, "ffn_gain": ffn_gain, "gate_weight": gate_weight, "up_weight": up_weight, "down_weight": down_weight}


PRECISE = lax.Precision.HIGHEST
EPSILON = 1e-06

@jax.custom_vjp
def low(v):
    return lax.optimization_barrier(v.astype(jnp.bfloat16)).astype(jnp.float32)

@jax.custom_vjp
def low_back(v):
    return v

def low_keep(v):
    return (low(v), None)

def low_pass(kept, grad):
    return (grad,)

def back_keep(v):
    return (v, None)

def back_low(kept, grad):
    return (low(grad),)
low.defvjp(low_keep, low_pass)
low_back.defvjp(back_keep, back_low)

def matmul(left, right):
    return jnp.dot(left.astype(jnp.float32), right.astype(jnp.float32), precision=PRECISE, preferred_element_type=jnp.float32)

def rms_scale(values):
    return lax.rsqrt(lax.optimization_barrier(jnp.mean(values * values, axis=-1, keepdims=True)) + EPSILON)

def convolve(padded, kernel, valid_taps):
    row_count = valid_taps.shape[0]
    summed = padded[CONV - 1:] * kernel[CONV - 1] * valid_taps[:, CONV - 1:CONV]
    for offset in range(CONV - 1):
        summed = summed + padded[offset:offset + row_count] * kernel[offset] * valid_taps[:, offset:offset + 1]
    return summed

def delta_rule(queries, keys_in, values, decays, beta_rate, keep_flags, state_in):
    length, key_width = queries.shape
    value_width = values.shape[1]
    blocks = length // GROUP
    query_blocks = queries.reshape(blocks, GROUP, key_width)
    key_blocks = keys_in.reshape(blocks, GROUP, key_width)
    value_blocks = values.reshape(blocks, GROUP, value_width)
    beta_blocks = beta_rate.reshape(blocks, GROUP)
    cumulative = jnp.cumsum(decays.reshape(blocks, GROUP), axis=1)
    row_index = lax.broadcasted_iota(jnp.int32, (GROUP, GROUP), 0)
    col_index = lax.broadcasted_iota(jnp.int32, (GROUP, GROUP), 1)
    lower_mask = (row_index >= col_index).astype(queries.dtype)
    strict = (row_index > col_index).astype(queries.dtype)
    fading = jnp.exp((cumulative[:, :, None] - cumulative[:, None, :]) * lower_mask) * lower_mask
    key_gram = jnp.einsum('nid,njd->nij', key_blocks, key_blocks, precision=PRECISE)
    system = jnp.eye(GROUP, dtype=queries.dtype) + strict * fading * beta_blocks[:, :, None] * key_gram
    growth = jnp.exp(cumulative)
    keys_wy = lax.linalg.triangular_solve(system, (beta_blocks * growth)[:, :, None] * key_blocks, left_side=True, lower=True, unit_diagonal=True)
    values_wy = lax.linalg.triangular_solve(system, beta_blocks[:, :, None] * value_blocks, left_side=True, lower=True, unit_diagonal=True)
    scores = jnp.einsum('nid,njd->nij', query_blocks, key_blocks, precision=PRECISE) * fading
    query_grown = query_blocks * growth[:, :, None]
    key_tail = jnp.exp(cumulative[:, -1:] - cumulative)[:, :, None] * key_blocks
    block_decay = growth[:, -1]

    def advance(carried, pieces):
        wy_keys, wy_values, block_scores, grown, tail_keys, whole_decay, keep_flag = pieces
        carried = carried * keep_flag
        fresh = wy_values - jnp.dot(wy_keys, carried, precision=PRECISE)
        result = jnp.dot(grown, carried, precision=PRECISE) + jnp.dot(block_scores, fresh, precision=PRECISE)
        carried = whole_decay * carried + jnp.dot(tail_keys.T, fresh, precision=PRECISE)
        return (carried, result)
    final_state, results = lax.scan(jax.checkpoint(advance), state_in, (keys_wy, values_wy, scores, query_grown, key_tail, block_decay, keep_flags))
    return (results.reshape(length, value_width), final_state)

def reference(tokens, cotangent, lengths, norm_gain, query_weight, key_weight, value_weight, outgate_weight, alpha_weight, beta_weight, output_weight, conv_query, conv_key, conv_value, log_rate, step_bias, out_gain, ffn_gain, gate_weight, up_weight, down_weight):
    row_count = tokens.shape[0]
    starts = (jnp.cumsum(lengths) - lengths).astype(jnp.int32)
    places = jnp.arange(row_count, dtype=jnp.int32)
    latest = lax.optimization_barrier(jnp.max(jnp.where(starts[None, :] <= places[:, None], starts[None, :], 0), axis=1))
    tap_index = jnp.arange(CONV, dtype=jnp.int32)
    valid_taps = ((places - latest)[:, None] >= CONV - 1 - tap_index[None, :]).astype(jnp.float32)
    block_first = jnp.arange(row_count // GROUP, dtype=jnp.int32) * GROUP
    keep_flags = 1.0 - jnp.any(block_first[:, None] == starts[None, :], axis=1).astype(jnp.float32)
    half_width = DV // 2
    zero_state = jnp.zeros((DK, half_width), jnp.float32)

    def forward(tokens_in, query_w, key_w, value_w, outgate_w, alpha_w, beta_w, output_w, gate_w, up_w, down_w, conv_q, conv_k, conv_v, rate_log, bias_step, gain_out, gain_norm, gain_ffn):
        hidden_in = low(tokens_in * rms_scale(tokens_in) * gain_norm)
        query_pre = low_back(matmul(hidden_in, query_w))
        key_pre = low_back(matmul(hidden_in, key_w))
        value_pre = low_back(matmul(hidden_in, value_w))
        outgate_pre = low_back(matmul(hidden_in, outgate_w))
        alpha_pre = low_back(matmul(hidden_in, alpha_w))
        beta_pre = low_back(matmul(hidden_in, beta_w))
        joined = jnp.concatenate([query_pre, key_pre, value_pre], axis=1)
        kernel = jnp.concatenate([conv_q, conv_k, conv_v], axis=1)
        padded = jnp.concatenate([jnp.zeros((CONV - 1, joined.shape[1]), jnp.float32), joined], axis=0)
        active = jax.nn.silu(convolve(padded, kernel, valid_taps))
        query_act = active[:, :HEADS * DK].reshape(row_count, HEADS, DK)
        key_act = active[:, HEADS * DK:2 * HEADS * DK].reshape(row_count, HEADS, DK)
        value_act = active[:, 2 * HEADS * DK:].reshape(row_count, HEADS, DV)
        query_unit = low(query_act * lax.rsqrt(lax.optimization_barrier(jnp.sum(query_act * query_act, axis=2, keepdims=True)) + EPSILON) * DK ** (-0.5))
        key_unit = low(key_act * lax.rsqrt(lax.optimization_barrier(jnp.sum(key_act * key_act, axis=2, keepdims=True)) + EPSILON))
        value_low = low(value_act)
        decays = low(-jnp.exp(rate_log) * jax.nn.softplus(alpha_pre + bias_step))
        beta_rate = low(jax.nn.sigmoid(beta_pre))

        def per_head(pieces):
            query_head, key_head, value_head, decay_head, beta_head = pieces
            halves = []
            for half_index in range(2):
                value_half = value_head[:, half_index * half_width:(half_index + 1) * half_width]
                out_half, end_half = delta_rule(low_back(query_head), low_back(key_head), low_back(value_half), low_back(decay_head), low_back(beta_head), keep_flags, zero_state)
                halves.append(out_half)
            return jnp.concatenate(halves, axis=1)
        mixed_out = lax.map(per_head, (query_unit.transpose(1, 0, 2), key_unit.transpose(1, 0, 2), value_low.transpose(1, 0, 2), decays.T, beta_rate.T))
        mixed_out = low_back(low(mixed_out)).transpose(1, 0, 2)
        gate_rows = outgate_pre.reshape(row_count, HEADS, DV)
        normed = low((mixed_out * rms_scale(mixed_out) * gain_out * jax.nn.silu(gate_rows)).reshape(row_count, HEADS * DV))
        attended = low_back(matmul(normed, output_w))
        middle = tokens_in + attended
        hidden_mid = low(middle * rms_scale(middle) * gain_ffn)
        gate_act = low_back(matmul(hidden_mid, gate_w))
        up_act = low_back(matmul(hidden_mid, up_w))
        inner_act = low(jax.nn.silu(gate_act) * up_act)
        return middle + matmul(inner_act, down_w)
    result, pullback = jax.vjp(forward, tokens.astype(jnp.float32), query_weight.astype(jnp.float32), key_weight.astype(jnp.float32), value_weight.astype(jnp.float32), outgate_weight.astype(jnp.float32), alpha_weight.astype(jnp.float32), beta_weight.astype(jnp.float32), output_weight.astype(jnp.float32), gate_weight.astype(jnp.float32), up_weight.astype(jnp.float32), down_weight.astype(jnp.float32), conv_query, conv_key, conv_value, log_rate, step_bias, out_gain, norm_gain, ffn_gain)
    grads = pullback(cotangent.astype(jnp.float32))
    return (result.astype(jnp.bfloat16), grads[0], grads[1], grads[2], grads[3], grads[4], grads[5], grads[6], grads[7], grads[8], grads[9], grads[10], grads[11], grads[12], grads[13], grads[14], grads[15], grads[16], grads[17], grads[18])
```

```python
import functools

import jax
import jax.numpy as jnp
from jax import lax
from jax.experimental import pallas as pl
from jax.experimental.pallas import tpu as pltpu
from jax.sharding import PartitionSpec as P

CONV = 4
GROUP = 64
RIM = 16
PACK = 256
LANES = 128
LONGEST = 4096
EPSILON = 1e-06
FH = ("fsdp", "heads")
ALL = ("fsdp", "heads", "tensor")
BF = jnp.bfloat16
F32 = jnp.float32
VMEM_LIMIT = 56 * 1024 * 1024
INVERSE_PASSES = 1


def shifted(shard, axis, by):
    devices = lax.axis_size(axis)
    pairs = [(i, i + by) for i in range(devices) if 0 <= i + by < devices]
    return lax.ppermute(shard, axis, pairs)


def dot_on(left, right, left_dim, right_dim):
    return lax.dot_general(
        left.astype(BF),
        right.astype(BF),
        (((left_dim,), (right_dim,)), ((), ())),
        preferred_element_type=F32,
    )


def mm(left, right):
    return dot_on(left, right, 1, 0)


def mm_tn(left, right):
    return dot_on(left, right, 0, 0)


def mm_nt(left, right):
    return dot_on(left, right, 1, 1)


def mm_fine(left, right):
    if INVERSE_PASSES == 1:
        return mm(left, right)
    left_high, right_high = left.astype(BF), right.astype(BF)
    left_low = left - left_high.astype(F32)
    right_low = right - right_high.astype(F32)
    return mm(left_high, right_high) + mm(left_low, right_high) + mm(left_high, right_low)


def sigmoid(value):
    return 1.0 / (1.0 + jnp.exp(-value))


def softplus(value):
    return jnp.maximum(value, 0.0) + jnp.log(1.0 + jnp.exp(-jnp.abs(value)))


def window_taps(window, rows):
    total = window.shape[0]
    return [pltpu.roll(window, total - (RIM - CONV + 1 + j), 0)[:rows] for j in range(CONV)]


def pack_masks():
    row = lax.broadcasted_iota(jnp.int32, (PACK, PACK), 0)
    col = lax.broadcasted_iota(jnp.int32, (PACK, PACK), 1)
    apart = row ^ col
    same = apart < GROUP
    return row, col, apart, same, same & (row >= col), same & (row > col)


def packed_decay(decay, masks):
    row, col, apart, same, lower, strict = masks
    spread = jnp.broadcast_to(decay, (PACK, PACK))
    decay_row = jnp.sum(jnp.where(apart == 0, spread, 0.0), axis=0, keepdims=True)
    gam_row = jnp.sum(jnp.where(same & (row <= col), spread, 0.0), axis=0, keepdims=True)
    spread_row = jnp.broadcast_to(decay_row, (PACK, PACK))
    gam = jnp.sum(jnp.where(lower, spread_row, 0.0), axis=1, keepdims=True)
    last = jnp.sum(jnp.where(same, spread_row, 0.0), axis=1, keepdims=True)
    fading = jnp.where(lower, jnp.exp(jnp.where(lower, gam - gam_row, 0.0)), 0.0)
    return gam, last, fading


def rates_of(small, rate, bias):
    decay_tile = -jnp.exp(rate) * softplus(small + bias)
    return decay_tile, sigmoid(small)


def load_window(pre_ref, group, first, width, rows):
    start = group * PACK
    before = jnp.where(group == 0, rows, start - RIM)
    head = pre_ref[pl.ds(pl.multiple_of(before, RIM), RIM), first : first + width]
    body = pre_ref[pl.ds(pl.multiple_of(start, PACK), PACK), first : first + width]
    return jnp.concatenate([head, body], axis=0)


def active_of(window, taps_ref, valid, first, width):
    pieces = window_taps(window, PACK)
    conv = None
    for j in range(CONV):
        term = pieces[j] * taps_ref[j : j + 1, first : first + width] * valid[:, j : j + 1]
        conv = term if conv is None else conv + term
    return conv, pieces


def forward_kernel(
    keep_ref,
    pre_ref,
    small_ref,
    taps_ref,
    valid_ref,
    rate_ref,
    bias_ref,
    qkv_ref,
    inverse_ref,
    w_ref,
    u_ref,
    fold_ref,
    states_ref,
    local_ref,
    carry_ref,
    ends_ref,
    fresh_ref,
    start_ref,
    last_ref,
    joint_ref,
    *,
    heads,
    rows,
    key_width,
    value_width,
):
    groups = rows // PACK
    inner = PACK // GROUP
    key_cols = heads * key_width

    def prepare(group, _):
        start = pl.multiple_of(group * PACK, PACK)
        span = pl.ds(start, PACK)
        valid = valid_ref[span, :]
        for tile in range(2 * heads):
            first = tile * key_width
            window = load_window(pre_ref, group, first, key_width, rows)
            conv, _ = active_of(window, taps_ref, valid, first, key_width)
            act = conv * sigmoid(conv)
            scale = lax.rsqrt(jnp.sum(act * act, axis=1, keepdims=True) + EPSILON)
            if tile < heads:
                scale = scale * key_width ** (-0.5)
            qkv_ref[span, first : first + key_width] = (act * scale).astype(BF)
        for tile in range(heads):
            first = 2 * key_cols + tile * value_width
            window = load_window(pre_ref, group, first, value_width, rows)
            conv, _ = active_of(window, taps_ref, valid, first, value_width)
            qkv_ref[span, first : first + value_width] = (conv * sigmoid(conv)).astype(BF)
        return 0

    lax.fori_loop(0, groups, prepare, 0)

    def solve(group, _):
        masks = pack_masks()
        row, col, apart, same, lower, strict = masks
        start = pl.multiple_of(group * PACK, PACK)
        span = pl.ds(start, PACK)
        decay_tile, beta_tile = rates_of(small_ref[span, :], rate_ref[...], bias_ref[...])
        items = []
        for head in range(heads):
            decay = decay_tile[:, head : head + 1].astype(BF).astype(F32)
            beta = beta_tile[:, heads + head : heads + head + 1].astype(BF).astype(F32)
            key = qkv_ref[span, key_cols + head * key_width : key_cols + (head + 1) * key_width]
            gam, last, fading = packed_decay(decay, masks)
            gram = mm_nt(key, key)
            system = jnp.where(strict, fading * beta * gram, 0.0)
            inverse = jnp.where(apart == 0, 1.0, 0.0) - jnp.where(apart == 1, system, 0.0)
            items.append([decay, beta, key, gam, last, fading, system, inverse])
        level = 1
        while (1 << level) < GROUP:
            parts = [
                mm_fine(jnp.where((apart >> level) == 1, item[6], 0.0), item[7]) for item in items
            ]
            steps = [mm_fine(item[7], part) for item, part in zip(items, parts)]
            for item, step in zip(items, steps):
                item[7] = item[7] - step
            level += 1
        for head in range(heads):
            decay, beta, key, gam, last, fading, system, inverse = items[head]
            query = qkv_ref[span, head * key_width : (head + 1) * key_width]
            first = 2 * key_cols + head * value_width
            value = qkv_ref[span, first : first + value_width]
            key_f = key.astype(F32)
            growth = jnp.exp(gam)
            inverse_low = inverse.astype(BF)
            inverse_ref[group * heads + head] = inverse_low
            w = mm(inverse_low, beta * growth * key_f)
            u = mm(inverse_low, beta * value.astype(F32))
            w_low, u_low = w.astype(BF), u.astype(BF)
            w_ref[span, head * key_width : (head + 1) * key_width] = w_low
            u_ref[span, head * value_width : (head + 1) * value_width] = u_low
            scores = (mm_nt(query, key) * fading).astype(BF)
            query_w = growth * query.astype(F32) - mm(scores, w_low)
            start_ref[span, head * value_width : (head + 1) * value_width] = mm(scores, u_low)
            tail = jnp.exp(last - gam) * key_f
            block_of = lax.broadcasted_iota(jnp.int32, (PACK, 1), 0) // GROUP
            whole = jnp.exp(last)
            for b in range(inner):
                index = (group * inner + b) * heads + head
                tail_b = jnp.where(block_of == b, tail, 0.0).astype(BF)
                fold_ref[index, :key_width, :] = mm_tn(tail_b, w_low).astype(BF)
                fold_ref[index, key_width:, :] = query_w[b * GROUP : (b + 1) * GROUP].astype(BF)
                fresh_ref[index] = mm_tn(tail_b, u_low)
                last_ref[index] = jnp.broadcast_to(
                    whole[b * GROUP : b * GROUP + 1], (8, LANES)
                )
        return 0

    lax.fori_loop(0, groups, solve, 0)

    unit = jnp.where(
        lax.broadcasted_iota(jnp.int32, (key_width, key_width), 0)
        == lax.broadcasted_iota(jnp.int32, (key_width, key_width), 1),
        1.0,
        0.0,
    )
    for head in range(heads):
        joint_ref[head, :, :value_width] = jnp.zeros((key_width, value_width), F32)
        joint_ref[head, :, value_width:] = unit
    for block in range(rows // GROUP):
        span = slice(block * GROUP, (block + 1) * GROUP)
        for head in range(heads):
            index = block * heads + head
            joint = joint_ref[head] * keep_ref[block]
            joint_low = joint.astype(BF)
            states_ref[index] = joint_low
            moved = mm(fold_ref[index], joint_low)
            whole = last_ref[index, 0:1, 0:1]
            fresh = whole * joint - moved[:key_width]
            joint_ref[head, :, :value_width] = fresh[:, :value_width] + fresh_ref[index]
            joint_ref[head, :, value_width:] = fresh[:, value_width:]
            cols = slice(head * value_width, (head + 1) * value_width)
            local_ref[span, cols] = moved[key_width:, :value_width] + start_ref[span, cols]
            carry_ref[span, head * key_width : (head + 1) * key_width] = moved[
                key_width:, value_width:
            ].astype(BF)
    ends_ref[...] = joint_ref[...].astype(BF)


def mixer_forward(pre, keep, taps, valid, rate, bias, heads, key_width, value_width):
    rows = pre.shape[0] - RIM
    wide = heads * (2 * key_width + value_width)
    gate_wide = heads * value_width
    count = rows // GROUP
    packs = rows // PACK
    joint_width = key_width + value_width
    whole = lambda shape: pl.BlockSpec(shape, lambda i: (0,) * len(shape))
    outs = [
        ((rows, wide), BF),
        ((packs * heads, PACK, PACK), BF),
        ((rows, heads * key_width), BF),
        ((rows, heads * value_width), BF),
        ((count * heads, key_width + GROUP, key_width), BF),
        ((count * heads, key_width, joint_width), BF),
        ((rows, heads * value_width), F32),
        ((rows, heads * key_width), BF),
        ((heads, key_width, joint_width), BF),
    ]
    return pl.pallas_call(
        functools.partial(
            forward_kernel, heads=heads, rows=rows, key_width=key_width, value_width=value_width
        ),
        grid=(1,),
        in_specs=[
            pl.BlockSpec(memory_space=pltpu.SMEM),
            pl.BlockSpec((rows + RIM, wide), lambda i: (0, 0)),
            pl.BlockSpec((rows + RIM, LANES), lambda i: (0, (wide + gate_wide) // LANES)),
            whole(taps.shape),
            whole(valid.shape),
            whole(rate.shape),
            whole(bias.shape),
        ],
        out_specs=[whole(shape) for shape, _ in outs],
        out_shape=[jax.ShapeDtypeStruct(shape, kind) for shape, kind in outs],
        scratch_shapes=[
            pltpu.VMEM((count * heads, key_width, value_width), F32),
            pltpu.VMEM((rows, heads * value_width), F32),
            pltpu.VMEM((count * heads, 8, LANES), F32),
            pltpu.VMEM((heads, key_width, joint_width), F32),
        ],
        compiler_params=pltpu.CompilerParams(vmem_limit_bytes=VMEM_LIMIT),
        name="mixer_forward",
    )(keep, pre, pre, taps, valid, rate, bias)


def output_kernel(
    place_ref,
    local_ref,
    carry_ref,
    end1_ref,
    end2_ref,
    end3_ref,
    end4_ref,
    gate_ref,
    gain_ref,
    weight_ref,
    mixed_ref,
    normed_ref,
    partial_ref,
    enter_ref,
    *,
    heads,
    key_width,
    value_width,
):
    @pl.when(pl.program_id(0) == 0)
    def _():
        for head in range(heads):
            state = end4_ref[0, head, :, :value_width].astype(F32)
            for end in (end3_ref, end2_ref, end1_ref):
                state = end[0, head, :, :value_width].astype(F32) + mm(
                    end[0, head, :, value_width:], state
                )
            enter_ref[head] = state.astype(BF)

    for head in range(heads):
        cols = slice(head * value_width, (head + 1) * value_width)
        mixed = local_ref[:, cols] + mm(
            carry_ref[:, head * key_width : (head + 1) * key_width], enter_ref[head]
        )
        mixed_low = mixed.astype(BF)
        mixed_ref[:, cols] = mixed_low
        mixed = mixed_low.astype(F32)
        scale = lax.rsqrt(jnp.mean(mixed * mixed, axis=1, keepdims=True) + EPSILON)
        gate = gate_ref[:, cols]
        normed = mixed * scale * gain_ref[...] * (gate * sigmoid(gate))
        normed_ref[:, cols] = normed.astype(BF)
    partial_ref[...] = mm(normed_ref[...], weight_ref[...]).astype(BF)


def mixer_output(local, carry, ends, place, pre, gain, weight, key_width, value_width):
    rows, cols = local.shape
    heads = cols // value_width
    width = weight.shape[1]
    gate_block = heads * (2 * key_width + value_width) // cols
    end_shape = (1,) + ends.shape[1:]

    def end_spec(step):
        return pl.BlockSpec(end_shape, lambda i, at: (jnp.maximum(at[0] - step, 0), 0, 0, 0))

    return pl.pallas_call(
        functools.partial(
            output_kernel, heads=heads, key_width=key_width, value_width=value_width
        ),
        grid_spec=pltpu.PrefetchScalarGridSpec(
            num_scalar_prefetch=1,
            grid=(rows // PACK,),
            in_specs=[
                pl.BlockSpec((PACK, cols), lambda i, at: (i, 0)),
                pl.BlockSpec((PACK, carry.shape[1]), lambda i, at: (i, 0)),
                end_spec(1),
                end_spec(2),
                end_spec(3),
                end_spec(4),
                pl.BlockSpec((PACK, cols), lambda i, at: (i, gate_block)),
                pl.BlockSpec(gain.shape, lambda i, at: (0, 0)),
                pl.BlockSpec(weight.shape, lambda i, at: (0, 0)),
            ],
            out_specs=[
                pl.BlockSpec((PACK, cols), lambda i, at: (i, 0)),
                pl.BlockSpec((PACK, cols), lambda i, at: (i, 0)),
                pl.BlockSpec((PACK, width), lambda i, at: (i, 0)),
                pl.BlockSpec((heads, key_width, value_width), lambda i, at: (0, 0, 0)),
            ],
        ),
        out_shape=[
            jax.ShapeDtypeStruct((rows, cols), BF),
            jax.ShapeDtypeStruct((rows, cols), BF),
            jax.ShapeDtypeStruct((rows, width), BF),
            jax.ShapeDtypeStruct((heads, key_width, value_width), BF),
        ],
        compiler_params=pltpu.CompilerParams(vmem_limit_bytes=VMEM_LIMIT),
        name="mixer_output",
    )(place, local, carry, ends, ends, ends, ends, pre, gain, weight)


def gate_back_kernel(
    grad_ref,
    weight_ref,
    mixed_ref,
    gate_ref,
    gain_ref,
    fold_ref,
    states_ref,
    mixed_grad_ref,
    gate_grad_ref,
    gain_grad_ref,
    source_ref,
    enter_grad_ref,
    *,
    heads,
    key_width,
    value_width,
):
    inner = PACK // GROUP

    @pl.when(pl.program_id(0) == 0)
    def _():
        gain_grad_ref[...] = jnp.zeros_like(gain_grad_ref)
        enter_grad_ref[...] = jnp.zeros_like(enter_grad_ref)

    normed_grad = mm_nt(grad_ref[...], weight_ref[...])
    gain = gain_ref[...]
    for head in range(heads):
        cols = slice(head * value_width, (head + 1) * value_width)
        grad = normed_grad[:, cols]
        mixed = mixed_ref[:, cols].astype(F32)
        scale = lax.rsqrt(jnp.mean(mixed * mixed, axis=1, keepdims=True) + EPSILON)
        gate = gate_ref[:, cols]
        sig = sigmoid(gate)
        silu = gate * sig
        unit = mixed * scale
        scaled = grad * unit
        gate_grad_ref[:, cols] = (scaled * gain * (sig * (1.0 + gate * (1.0 - sig)))).astype(BF)
        gain_grad_ref[0:1, :] += jnp.sum(scaled * silu, axis=0, keepdims=True)
        unit_grad = grad * gain * silu
        mixed_grad = scale * (unit_grad - unit * jnp.mean(unit_grad * unit, axis=1, keepdims=True))
        mixed_grad = mixed_grad.astype(BF)
        mixed_grad_ref[:, cols] = mixed_grad
        total = enter_grad_ref[head]
        for b in range(inner):
            index = b * heads + head
            source = mm_tn(
                fold_ref[index, key_width:, :], mixed_grad[b * GROUP : (b + 1) * GROUP]
            )
            source_ref[index] = source
            total = total + mm_tn(states_ref[index, :, value_width:], source)
        enter_grad_ref[head] = total


def gate_back(grad, weight, mixed, pre, gain, fold, states, key_width, value_width):
    rows, width = grad.shape
    cols = weight.shape[0]
    heads = cols // value_width
    gate_block = heads * (2 * key_width + value_width) // cols
    step = PACK // GROUP * heads
    return pl.pallas_call(
        functools.partial(
            gate_back_kernel, heads=heads, key_width=key_width, value_width=value_width
        ),
        grid=(rows // PACK,),
        in_specs=[
            pl.BlockSpec((PACK, width), lambda i: (i, 0)),
            pl.BlockSpec(weight.shape, lambda i: (0, 0)),
            pl.BlockSpec((PACK, cols), lambda i: (i, 0)),
            pl.BlockSpec((PACK, cols), lambda i: (i, gate_block)),
            pl.BlockSpec(gain.shape, lambda i: (0, 0)),
            pl.BlockSpec((step,) + fold.shape[1:], lambda i: (i, 0, 0)),
            pl.BlockSpec((step,) + states.shape[1:], lambda i: (i, 0, 0)),
        ],
        out_specs=[
            pl.BlockSpec((PACK, cols), lambda i: (i, 0)),
            pl.BlockSpec((PACK, cols), lambda i: (i, 0)),
            pl.BlockSpec((8, value_width), lambda i: (0, 0)),
            pl.BlockSpec((step, key_width, value_width), lambda i: (i, 0, 0)),
            pl.BlockSpec((heads, key_width, value_width), lambda i: (0, 0, 0)),
        ],
        out_shape=[
            jax.ShapeDtypeStruct((rows, cols), BF),
            jax.ShapeDtypeStruct((rows, cols), BF),
            jax.ShapeDtypeStruct((8, value_width), F32),
            jax.ShapeDtypeStruct((rows // GROUP * heads, key_width, value_width), F32),
            jax.ShapeDtypeStruct((heads, key_width, value_width), F32),
        ],
        compiler_params=pltpu.CompilerParams(vmem_limit_bytes=VMEM_LIMIT),
        name="gate_back",
    )(grad, weight, mixed, pre, gain, fold, states)


def backward_kernel(
    place_ref,
    keep_ref,
    flag_ref,
    pre_ref,
    small_ref,
    taps_ref,
    valid_ref,
    rate_ref,
    bias_ref,
    qkv_ref,
    inverse_ref,
    w_ref,
    u_ref,
    fold_ref,
    states_ref,
    enter_ref,
    mixed_grad_ref,
    source_ref,
    next1_ref,
    next2_ref,
    next3_ref,
    next4_ref,
    end1_ref,
    end2_ref,
    end3_ref,
    pre_grad_ref,
    small_grad_ref,
    taps_grad_ref,
    rate_grad_ref,
    later_ref,
    whole_ref,
    conv_grad_ref,
    flow_ref,
    *,
    heads,
    rows,
    key_width,
    value_width,
):
    groups = rows // PACK
    inner = PACK // GROUP
    key_cols = heads * key_width
    wide = heads * (2 * key_width + value_width)
    taps_grad_ref[...] = jnp.zeros_like(taps_grad_ref)
    rate_grad_ref[...] = jnp.zeros_like(rate_grad_ref)
    conv_grad_ref[0:RIM, :] = jnp.zeros((RIM, wide), F32)
    conv_grad_ref[RIM + rows :, :] = jnp.zeros((RIM, wide), F32)
    small_grad_ref[rows:, :] = jnp.zeros((RIM, LANES), BF)

    def lasts(group, _):
        masks = pack_masks()
        span = pl.ds(pl.multiple_of(group * PACK, PACK), PACK)
        decay_tile, _ = rates_of(small_ref[span, :], rate_ref[...], bias_ref[...])
        for head in range(heads):
            decay = decay_tile[:, head : head + 1].astype(BF).astype(F32)
            for b in range(inner):
                total = jnp.sum(decay[b * GROUP : (b + 1) * GROUP], axis=0, keepdims=True)
                whole_ref[(group * inner + b) * heads + head] = jnp.broadcast_to(
                    jnp.exp(total), (8, LANES)
                )
        return 0

    lax.fori_loop(0, groups, lasts, 0)

    for head in range(heads):
        flow = flag_ref[3] * next4_ref[0, head].astype(F32)
        flow = flag_ref[2] * (
            next3_ref[0, head].astype(F32) + mm_tn(end3_ref[0, head, :, value_width:], flow)
        )
        flow = flag_ref[1] * (
            next2_ref[0, head].astype(F32) + mm_tn(end2_ref[0, head, :, value_width:], flow)
        )
        flow = flag_ref[0] * (
            next1_ref[0, head].astype(F32) + mm_tn(end1_ref[0, head, :, value_width:], flow)
        )
        flow_ref[head] = flow
    for block in reversed(range(rows // GROUP)):
        for head in range(heads):
            index = block * heads + head
            flow = flow_ref[head]
            flow_low = flow.astype(BF)
            later_ref[index] = flow_low
            moved = mm_tn(fold_ref[index, :key_width, :], flow_low)
            flow_ref[head] = keep_ref[block] * (
                whole_ref[index, 0:1, 0:1] * flow - moved + source_ref[index]
            )

    def back(group, _):
        masks = pack_masks()
        row, col, apart, same, lower, strict = masks
        span = pl.ds(pl.multiple_of(group * PACK, PACK), PACK)
        small = small_ref[span, :]
        valid = valid_ref[pl.ds(pl.multiple_of(group * PACK + RIM, RIM), PACK), :]
        decay_tile, beta_tile = rates_of(small, rate_ref[...], bias_ref[...])
        lane = lax.broadcasted_iota(jnp.int32, (PACK, LANES), 1)
        small_rows = jnp.zeros((PACK, LANES), F32)
        for head in range(heads):
            decay = decay_tile[:, head : head + 1].astype(BF).astype(F32)
            beta = beta_tile[:, heads + head : heads + head + 1].astype(BF).astype(F32)
            query_at = head * key_width
            key_at = key_cols + head * key_width
            value_at = 2 * key_cols + head * value_width
            query = qkv_ref[span, query_at : query_at + key_width]
            key = qkv_ref[span, key_at : key_at + key_width]
            value = qkv_ref[span, value_at : value_at + value_width]
            key_f = key.astype(F32)
            gam, last, fading = packed_decay(decay, masks)
            growth = jnp.exp(gam)
            rest = jnp.exp(last - gam)
            gram = mm_nt(key, key)
            scores = mm_nt(query, key) * fading
            system = jnp.where(strict, fading * beta * gram, 0.0)
            tail = (rest * key_f).astype(BF)
            w = w_ref[span, query_at : query_at + key_width]
            u = u_ref[span, head * value_width : (head + 1) * value_width]
            out_grad = mixed_grad_ref[span, head * value_width : (head + 1) * value_width]
            renewed, renewed_grad, state_lows, flows, drops = [], [], [], [], []
            for b in range(inner):
                index = (group * inner + b) * heads + head
                part = slice(b * GROUP, (b + 1) * GROUP)
                state = states_ref[index, :, :value_width].astype(F32) + mm(
                    states_ref[index, :, value_width:], enter_ref[head]
                )
                state_low = state.astype(BF)
                flow = later_ref[index]
                state_lows.append(state_low)
                flows.append(flow)
                renewed.append(u[part].astype(F32) - mm(w[part], state_low))
                renewed_grad.append(mm(tail[part], flow))
                shared = jnp.sum(
                    jnp.sum(state * flow.astype(F32), axis=1, keepdims=True), axis=0, keepdims=True
                )
                drops.append(
                    jnp.broadcast_to(shared * whole_ref[index, 0:1, 0:1], (GROUP, 1))
                )
            renewed = jnp.concatenate(renewed, axis=0).astype(BF)
            renewed_grad = mm_tn(scores, out_grad) + jnp.concatenate(renewed_grad, axis=0)
            renewed_low = renewed_grad.astype(BF)
            scores_grad = jnp.where(lower, mm_nt(out_grad, renewed), 0.0)
            grown_grad, tail_grad, w_grad = [], [], []
            for b in range(inner):
                part = slice(b * GROUP, (b + 1) * GROUP)
                grown_grad.append(mm_nt(out_grad[part], state_lows[b]))
                tail_grad.append(mm_nt(renewed[part], flows[b]))
                w_grad.append(mm_nt(renewed_low[part], state_lows[b]))
            grown_grad = jnp.concatenate(grown_grad, axis=0)
            tail_grad = jnp.concatenate(tail_grad, axis=0)
            w_grad = -jnp.concatenate(w_grad, axis=0)
            inverse = inverse_ref[group * heads + head]
            keys_grad = mm_tn(inverse, w_grad)
            values_grad = mm_tn(inverse, renewed_low)
            system_grad = jnp.where(strict, -(mm_nt(keys_grad, w) + mm_nt(values_grad, u)), 0.0)
            gram_beta = system_grad * fading
            gram_grad = (gram_beta * beta).astype(BF)
            pair_grad = (scores_grad * fading).astype(BF)
            changes = system_grad * system + scores_grad * scores
            query_f = query.astype(F32)
            query_grad = mm(pair_grad, key) + growth * grown_grad
            key_grad = (
                mm(gram_grad, key)
                + mm_tn(gram_grad, key)
                + mm_tn(pair_grad, query)
                + beta * growth * keys_grad
                + rest * tail_grad
            )
            value_grad = beta * values_grad
            keys_dot = growth * jnp.sum(keys_grad * key_f, axis=1, keepdims=True)
            beta_grad = (
                keys_dot
                + jnp.sum(values_grad * value.astype(F32), axis=1, keepdims=True)
                + jnp.sum(gram_beta * gram, axis=1, keepdims=True)
            )
            tail_dot = rest * jnp.sum(tail_grad * key_f, axis=1, keepdims=True)
            column = jnp.sum(changes, axis=0, keepdims=True)
            column = jnp.sum(
                jnp.where(apart == 0, jnp.broadcast_to(column, (PACK, PACK)), 0.0),
                axis=1,
                keepdims=True,
            )
            gam_grad = (
                beta * keys_dot
                + jnp.sum(changes, axis=1, keepdims=True)
                - column
                + growth * jnp.sum(grown_grad * query_f, axis=1, keepdims=True)
                - tail_dot
            )
            gam_grad_row = jnp.sum(
                jnp.where(apart == 0, jnp.broadcast_to(gam_grad, (PACK, PACK)), 0.0),
                axis=0,
                keepdims=True,
            )
            tail_row = jnp.sum(
                jnp.where(apart == 0, jnp.broadcast_to(tail_dot, (PACK, PACK)), 0.0),
                axis=0,
                keepdims=True,
            )
            decay_grad = (
                jnp.sum(
                    jnp.where(same & (col >= row), gam_grad_row, 0.0)
                    + jnp.where(same, tail_row, 0.0),
                    axis=1,
                    keepdims=True,
                )
                + jnp.concatenate(drops, axis=0)
            )
            small_rows = jnp.where(lane == head, decay_grad, small_rows)
            small_rows = jnp.where(lane == heads + head, beta_grad, small_rows)

            for first, width, unit_grad, factor in (
                (query_at, key_width, query_grad, key_width ** (-0.5)),
                (key_at, key_width, key_grad, 1.0),
                (value_at, value_width, value_grad, None),
            ):
                window = load_window(pre_ref, group, first, width, rows)
                conv, pieces = active_of(window, taps_ref, valid, first, width)
                sig = sigmoid(conv)
                act_grad = unit_grad
                if factor is not None:
                    act = conv * sig
                    scale = lax.rsqrt(jnp.sum(act * act, axis=1, keepdims=True) + EPSILON)
                    along = jnp.sum(unit_grad * act, axis=1, keepdims=True)
                    act_grad = factor * scale * (unit_grad - act * (scale * scale * along))
                conv_grad = act_grad * (sig * (1.0 + conv * (1.0 - sig)))
                conv_grad_ref[
                    pl.ds(pl.multiple_of(group * PACK + RIM, RIM), PACK), first : first + width
                ] = conv_grad
                for j in range(CONV):
                    taps_grad_ref[j : j + 1, first : first + width] += jnp.sum(
                        conv_grad * valid[:, j : j + 1] * pieces[j], axis=0, keepdims=True
                    )

        raw = small + bias_ref[...]
        slope = -jnp.exp(rate_ref[...]) * sigmoid(raw)
        small_grad = jnp.where(
            lane < heads, small_rows * slope, small_rows * beta_tile * (1.0 - beta_tile)
        )
        small_grad = jnp.where(lane < 2 * heads, small_grad, 0.0)
        small_grad_ref[span, :] = small_grad.astype(BF)
        rate_grad_ref[0:1, :] += jnp.sum(small_rows * decay_tile, axis=0, keepdims=True)
        rate_grad_ref[1:2, :] += jnp.sum(small_grad, axis=0, keepdims=True)
        return 0

    lax.fori_loop(0, groups, back, 0)

    def convolve_back(start, target, count, first):
        cols = slice(first, first + LANES)
        window = conv_grad_ref[pl.ds(start, count + RIM), cols]
        flags = valid_ref[pl.ds(start, count + RIM), :]
        total = None
        for j in range(CONV):
            term = window * (flags[:, j : j + 1] * taps_ref[j : j + 1, cols])
            shift = CONV - 1 - j
            if shift:
                term = pltpu.roll(term, count + RIM - shift, 0)
            total = term if total is None else total + term
        pre_grad_ref[pl.ds(target, count), cols] = total[:count].astype(BF)

    def spread(group, _):
        base = pl.multiple_of(group * PACK, PACK)
        for first in range(0, wide, LANES):
            convolve_back(pl.multiple_of(base + RIM, RIM), base, PACK, first)
        return 0

    lax.fori_loop(0, groups, spread, 0)
    for first in range(0, wide, LANES):
        convolve_back(0, rows, RIM, first)


def mixer_backward(
    place,
    keep,
    flags,
    pre,
    taps,
    valid,
    rate,
    bias,
    qkv,
    inverse,
    w,
    u,
    fold,
    states,
    enter,
    mixed_grad,
    source,
    enter_grads,
    ends,
    heads,
    key_width,
    value_width,
):
    rows = pre.shape[0] - RIM
    wide = heads * (2 * key_width + value_width)
    gate_wide = heads * value_width
    count = rows // GROUP
    devices = ends.shape[0]

    def whole(shape):
        return pl.BlockSpec(shape, lambda i, at: (0,) * len(shape))

    def next_spec(shape, step):
        return pl.BlockSpec(
            (1,) + shape[1:], lambda i, at: (jnp.minimum(at[0] + step, devices - 1), 0, 0, 0)
        )

    smem = pl.BlockSpec(memory_space=pltpu.SMEM)
    return pl.pallas_call(
        functools.partial(
            backward_kernel, heads=heads, rows=rows, key_width=key_width, value_width=value_width
        ),
        grid_spec=pltpu.PrefetchScalarGridSpec(
            num_scalar_prefetch=1,
            grid=(1,),
            in_specs=[
                smem,
                smem,
                pl.BlockSpec((rows + RIM, wide), lambda i, at: (0, 0)),
                pl.BlockSpec((rows + RIM, LANES), lambda i, at: (0, (wide + gate_wide) // LANES)),
                whole(taps.shape),
                whole(valid.shape),
                whole(rate.shape),
                whole(bias.shape),
                whole(qkv.shape),
                whole(inverse.shape),
                whole(w.shape),
                whole(u.shape),
                whole(fold.shape),
                whole(states.shape),
                whole(enter.shape),
                whole(mixed_grad.shape),
                whole(source.shape),
                next_spec(enter_grads.shape, 1),
                next_spec(enter_grads.shape, 2),
                next_spec(enter_grads.shape, 3),
                next_spec(enter_grads.shape, 4),
                next_spec(ends.shape, 1),
                next_spec(ends.shape, 2),
                next_spec(ends.shape, 3),
            ],
            out_specs=[
                whole((rows + RIM, wide)),
                whole((rows + RIM, LANES)),
                whole((8, wide)),
                whole((8, LANES)),
            ],
            scratch_shapes=[
                pltpu.VMEM((count * heads, key_width, value_width), BF),
                pltpu.VMEM((count * heads, 8, LANES), F32),
                pltpu.VMEM((rows + 2 * RIM, wide), F32),
                pltpu.VMEM((heads, key_width, value_width), F32),
            ],
        ),
        out_shape=[
            jax.ShapeDtypeStruct((rows + RIM, wide), BF),
            jax.ShapeDtypeStruct((rows + RIM, LANES), BF),
            jax.ShapeDtypeStruct((8, wide), F32),
            jax.ShapeDtypeStruct((8, LANES), F32),
        ],
        compiler_params=pltpu.CompilerParams(vmem_limit_bytes=VMEM_LIMIT),
        name="mixer_backward",
    )(
        place,
        keep,
        flags,
        pre,
        pre,
        taps,
        valid,
        rate,
        bias,
        qkv,
        inverse,
        w,
        u,
        fold,
        states,
        enter,
        mixed_grad,
        source,
        enter_grads,
        enter_grads,
        enter_grads,
        enter_grads,
        ends,
        ends,
        ends,
    )


def product(left, right):
    return jnp.dot(left, right, preferred_element_type=F32)


def transposed_left(left, right):
    return lax.dot_general(left, right, (((0,), (0,)), ((), ())), preferred_element_type=F32)


def transposed_right(left, right):
    return lax.dot_general(left, right, (((1,), (1,)), ((), ())), preferred_element_type=F32)


def full_rows(row_block):
    return lax.all_gather(row_block, "tensor", axis=1, tiled=True)


def tensor_total(terms):
    return lax.psum_scatter(terms.astype(BF), "tensor", scatter_dimension=1, tiled=True)


def owners(grad):
    return lax.psum_scatter(grad.astype(BF), FH, scatter_dimension=0, tiled=True).astype(F32)


def spread_into(piece, whole_shape, start, axis_number):
    return lax.dynamic_update_slice_in_dim(jnp.zeros(whole_shape, F32), piece, start, axis_number)


def lane_row(values):
    return jnp.pad(values, (0, LANES - values.shape[0]))[None, :]


def per_device(
    tokens,
    cotangent,
    lengths,
    norm_gain,
    query_weight,
    key_weight,
    value_weight,
    outgate_weight,
    alpha_weight,
    beta_weight,
    output_weight,
    conv_query,
    conv_key,
    conv_value,
    log_rate,
    step_bias,
    out_gain,
    ffn_gain,
    gate_weight,
    up_weight,
    down_weight,
):
    rows, slice_width = tokens.shape
    full_width = slice_width * lax.axis_size("tensor")
    tensor_place = lax.axis_index("tensor")
    place = lax.axis_index(FH)
    devices = lax.axis_size(FH)
    key_cols = query_weight.shape[1]
    value_cols = value_weight.shape[1]
    heads = alpha_weight.shape[1]
    key_width = key_cols // heads
    value_width = value_cols // heads
    wide = 2 * key_cols + value_cols
    hidden = gate_weight.shape[1]

    rim_slice = shifted(tokens[rows - RIM :], FH, 1)
    token_rows = full_rows(tokens)
    rim_rows = full_rows(rim_slice)
    small_shard = jnp.pad(
        jnp.concatenate([alpha_weight, beta_weight], axis=1), ((0, 0), (0, LANES - 2 * heads))
    )
    in_shard = jnp.concatenate(
        [query_weight, key_weight, value_weight, outgate_weight, small_shard], axis=1
    )
    in_full = lax.all_gather(in_shard, "fsdp", axis=0, tiled=True)
    output_full = lax.all_gather(output_weight, "fsdp", axis=1, tiled=True)
    ffn_full = lax.all_gather(jnp.stack([gate_weight, up_weight]), "fsdp", axis=1, tiled=True)
    down_full = lax.all_gather(down_weight, "fsdp", axis=1, tiled=True)
    cot_rows = full_rows(cotangent)

    starts = jnp.cumsum(lengths) - lengths
    places = place * rows + jnp.arange(rows, dtype=jnp.int32)
    latest = jnp.max(jnp.where(starts[None, :] <= places[:, None], starts[None, :], 0), axis=1)
    tap_index = jnp.arange(8, dtype=jnp.int32)
    valid = ((places - latest)[:, None] >= CONV - 1 - tap_index[None, :]).astype(F32)
    valid_padded = jnp.pad(valid, ((RIM, RIM), (0, 0)))
    block_first = place * rows + jnp.arange(rows // GROUP, dtype=jnp.int32) * GROUP
    keep = 1.0 - jnp.any(block_first[:, None] == starts[None, :], axis=1).astype(F32)
    following = place + 1 + jnp.arange(4, dtype=jnp.int32)
    flags = (following < devices).astype(F32)
    place_array = place.astype(jnp.int32)[None]
    taps = jnp.concatenate(
        [
            lax.dynamic_slice_in_dim(conv_query, tensor_place * key_cols, key_cols, 1),
            lax.dynamic_slice_in_dim(conv_key, tensor_place * key_cols, key_cols, 1),
            lax.dynamic_slice_in_dim(conv_value, tensor_place * value_cols, value_cols, 1),
        ],
        axis=1,
    )
    rate = lane_row(lax.dynamic_slice_in_dim(log_rate, tensor_place * heads, heads))
    bias = lane_row(lax.dynamic_slice_in_dim(step_bias, tensor_place * heads, heads))
    gain_row = out_gain[None, :]

    token_all = jnp.concatenate([token_rows, rim_rows], axis=0).astype(F32)
    scale_all = lax.rsqrt(jnp.mean(token_all * token_all, axis=1, keepdims=True) + EPSILON)
    hidden_in = (token_all * scale_all * norm_gain).astype(BF)
    pre = product(hidden_in, in_full)

    qkv, inverse, w, u, fold, states, local, carry, end = mixer_forward(
        pre, keep, taps, valid, rate, bias, heads, key_width, value_width
    )
    ends = lax.all_gather(end, FH, axis=0, tiled=False)
    mixed, normed, attn_terms, enter = mixer_output(
        local, carry, ends, place_array, pre, gain_row, output_full, key_width, value_width
    )
    attn = full_rows(tensor_total(attn_terms))

    middle = token_rows.astype(F32) + attn.astype(F32)
    scale_mid = lax.rsqrt(jnp.mean(middle * middle, axis=1, keepdims=True) + EPSILON)
    hidden_mid = (middle * scale_mid * ffn_gain).astype(BF)
    gate_act = product(hidden_mid, ffn_full[0])
    up_act = product(hidden_mid, ffn_full[1])
    gate_sig = jax.nn.sigmoid(gate_act)
    inner_act = (gate_act * gate_sig * up_act).astype(BF)
    inner_grad = transposed_right(cot_rows, down_full)
    gate_grad = (inner_grad * up_act * gate_sig * (1.0 + gate_act * (1.0 - gate_sig))).astype(BF)
    up_grad = (inner_grad * gate_act * gate_sig).astype(BF)
    mid_terms = transposed_right(gate_grad, ffn_full[0]) + transposed_right(up_grad, ffn_full[1])
    ffn_gain_grad = jnp.sum(mid_terms * (middle * scale_mid), axis=0)
    mid_grad = full_rows(tensor_total(mid_terms))
    output_terms = tensor_total(product(inner_act, down_full))
    middle_own = lax.dynamic_slice_in_dim(middle, tensor_place * slice_width, slice_width, 1)
    output_rows = (middle_own + output_terms.astype(F32)).astype(BF)

    scaled_mid = mid_grad.astype(F32) * ffn_gain
    mid_dot = jnp.sum(scaled_mid * middle, axis=1, keepdims=True)
    middle_grad = (
        cot_rows.astype(F32)
        + scale_mid * scaled_mid
        - middle * (scale_mid * scale_mid * scale_mid * mid_dot / full_width)
    )
    attn_grad = middle_grad.astype(BF)

    mixed_grad, outgate_grad, out_gain_grad, source, enter_grad = gate_back(
        attn_grad, output_full, mixed, pre, gain_row, fold, states, key_width, value_width
    )
    enter_grads = lax.all_gather(enter_grad.astype(BF), FH, axis=0, tiled=False)
    ffn_grads = owners(
        jnp.concatenate(
            [
                transposed_left(hidden_mid, gate_grad).astype(BF),
                transposed_left(hidden_mid, up_grad).astype(BF),
                transposed_left(cot_rows, inner_act).astype(BF),
            ],
            axis=1,
        )
    )
    out_grads = owners(
        jnp.concatenate(
            [
                transposed_left(attn_grad, normed).astype(BF),
                transposed_left(hidden_in[:rows], outgate_grad).astype(BF),
            ],
            axis=1,
        )
    )
    pre_grad, small_grad, taps_grad, rate_grad = mixer_backward(
        place_array,
        keep,
        flags,
        pre,
        taps,
        valid_padded,
        rate,
        bias,
        qkv,
        inverse,
        w,
        u,
        fold,
        states,
        enter,
        mixed_grad,
        source,
        enter_grads,
        ends,
        heads,
        key_width,
        value_width,
    )

    gate_terms = transposed_right(outgate_grad, in_full[:, wide : wide + value_cols])
    main_terms = transposed_right(pre_grad, in_full[:, :wide]) + transposed_right(
        small_grad, in_full[:, wide + value_cols :]
    )
    rim_terms = shifted(main_terms[rows:], FH, -1)
    in_terms = main_terms[:rows] + gate_terms
    norm_gain_grad = jnp.sum(in_terms * (token_all * scale_all)[:rows], axis=0) + jnp.sum(
        main_terms[rows:] * (token_all * scale_all)[rows:], axis=0
    )
    in_terms = in_terms + jnp.pad(rim_terms, ((rows - RIM, 0), (0, 0)))
    in_dot = lax.psum(jnp.sum(in_terms * (token_all[:rows] * norm_gain), axis=1), "tensor")
    in_grad = tensor_total(in_terms).astype(F32)
    late_grads = owners(
        jnp.concatenate(
            [
                transposed_left(hidden_in, pre_grad).astype(BF),
                transposed_left(hidden_in, small_grad).astype(BF),
            ],
            axis=1,
        )
    )
    norm_slice = lax.dynamic_slice_in_dim(norm_gain, tensor_place * slice_width, slice_width)
    middle_grad_own = lax.dynamic_slice_in_dim(
        middle_grad, tensor_place * slice_width, slice_width, 1
    )
    scale_in = scale_all[:rows]
    tokens_grad = (
        middle_grad_own
        + scale_in * (in_grad * norm_slice)
        - tokens.astype(F32) * (scale_in * scale_in * scale_in * in_dot[:, None] / full_width)
    )

    pieces = (
        spread_into(taps_grad[:CONV, :key_cols], conv_query.shape, tensor_place * key_cols, 1),
        spread_into(
            taps_grad[:CONV, key_cols : 2 * key_cols], conv_key.shape, tensor_place * key_cols, 1
        ),
        spread_into(
            taps_grad[:CONV, 2 * key_cols :], conv_value.shape, tensor_place * value_cols, 1
        ),
        spread_into(rate_grad[0, :heads], log_rate.shape, tensor_place * heads, 0),
        spread_into(rate_grad[1, :heads], step_bias.shape, tensor_place * heads, 0),
        out_gain_grad[0],
        norm_gain_grad,
        ffn_gain_grad,
    )
    joined = lax.psum(jnp.concatenate([piece.reshape(-1) for piece in pieces]), ALL)
    small, at = [], 0
    for piece in pieces:
        small.append(joined[at : at + piece.size].reshape(piece.shape))
        at += piece.size

    return (
        output_rows,
        tokens_grad,
        late_grads[:, :key_cols],
        late_grads[:, key_cols : 2 * key_cols],
        late_grads[:, 2 * key_cols : wide],
        out_grads[:, value_cols:],
        late_grads[:, wide : wide + heads],
        late_grads[:, wide + heads : wide + 2 * heads],
        out_grads[:, :value_cols].T,
        ffn_grads[:, :hidden],
        ffn_grads[:, hidden : 2 * hidden],
        ffn_grads[:, 2 * hidden :].T,
        *small,
    )


def solution(mesh):
    in_specs = (
        P(FH, "tensor"),
        P(FH, "tensor"),
        P(),
        P(),
        P("fsdp", "tensor"),
        P("fsdp", "tensor"),
        P("fsdp", "tensor"),
        P("fsdp", "tensor"),
        P("fsdp", "tensor"),
        P("fsdp", "tensor"),
        P("tensor", "fsdp"),
        P(),
        P(),
        P(),
        P(),
        P(),
        P(),
        P(),
        P("fsdp", "tensor"),
        P("fsdp", "tensor"),
        P("tensor", "fsdp"),
    )
    out_specs = (
        P(FH, "tensor"),
        P(FH, "tensor"),
        P(FH, "tensor"),
        P(FH, "tensor"),
        P(FH, "tensor"),
        P(FH, "tensor"),
        P(FH, "tensor"),
        P(FH, "tensor"),
        P("tensor", FH),
        P(FH, "tensor"),
        P(FH, "tensor"),
        P("tensor", FH),
        P(),
        P(),
        P(),
        P(),
        P(),
        P(),
        P(),
        P(),
    )
    return jax.shard_map(
        per_device, mesh=mesh, in_specs=in_specs, out_specs=out_specs, check_vma=False
    )
```

```python
import functools

import jax
import jax.numpy as jnp
from jax import lax
from jax.experimental import pallas as pl
from jax.experimental.pallas import tpu as pltpu
from jax.sharding import PartitionSpec as P

CONV = 4
GROUP = 64
RIM = 16
PACK = 256
LANES = 128
LONGEST = 4096
EPSILON = 1e-06
FH = ("fsdp", "heads")
ALL = ("fsdp", "heads", "tensor")
BF = jnp.bfloat16
F32 = jnp.float32
VMEM_LIMIT = 56 * 1024 * 1024
INVERSE_PASSES = 1
CHUNKS = 2


def cost(micros):
    return pl.CostEstimate(flops=int(micros * 1e9), bytes_accessed=int(micros * 3e6), transcendentals=0)


def shifted(shard, axis, by):
    devices = lax.axis_size(axis)
    pairs = [(i, i + by) for i in range(devices) if 0 <= i + by < devices]
    return lax.ppermute(shard, axis, pairs)


def dot_on(left, right, left_dim, right_dim):
    return lax.dot_general(
        left.astype(BF),
        right.astype(BF),
        (((left_dim,), (right_dim,)), ((), ())),
        preferred_element_type=F32,
    )


def mm(left, right):
    return dot_on(left, right, 1, 0)


def mm_tn(left, right):
    return dot_on(left, right, 0, 0)


def mm_nt(left, right):
    return dot_on(left, right, 1, 1)


def mm_fine(left, right):
    if INVERSE_PASSES == 1:
        return mm(left, right)
    left_high, right_high = left.astype(BF), right.astype(BF)
    left_low = left - left_high.astype(F32)
    right_low = right - right_high.astype(F32)
    return mm(left_high, right_high) + mm(left_low, right_high) + mm(left_high, right_low)


def sigmoid(value):
    return 1.0 / (1.0 + jnp.exp(-value))


def softplus(value):
    return jnp.maximum(value, 0.0) + jnp.log(1.0 + jnp.exp(-jnp.abs(value)))


def window_taps(window, rows):
    total = window.shape[0]
    return [pltpu.roll(window, total - (RIM - CONV + 1 + j), 0)[:rows] for j in range(CONV)]


def pack_masks():
    row = lax.broadcasted_iota(jnp.int32, (PACK, PACK), 0)
    col = lax.broadcasted_iota(jnp.int32, (PACK, PACK), 1)
    apart = row ^ col
    same = apart < GROUP
    return row, col, apart, same, same & (row >= col), same & (row > col)


def packed_decay(decay, masks):
    row, col, apart, same, lower, strict = masks
    spread = jnp.broadcast_to(decay, (PACK, PACK))
    decay_row = jnp.sum(jnp.where(apart == 0, spread, 0.0), axis=0, keepdims=True)
    gam_row = jnp.sum(jnp.where(same & (row <= col), spread, 0.0), axis=0, keepdims=True)
    spread_row = jnp.broadcast_to(decay_row, (PACK, PACK))
    gam = jnp.sum(jnp.where(lower, spread_row, 0.0), axis=1, keepdims=True)
    last = jnp.sum(jnp.where(same, spread_row, 0.0), axis=1, keepdims=True)
    fading = jnp.where(lower, jnp.exp(jnp.where(lower, gam - gam_row, 0.0)), 0.0)
    return gam, last, fading


def rates_of(small, rate, bias):
    decay_tile = -jnp.exp(rate) * softplus(small + bias)
    return decay_tile, sigmoid(small)


def load_window(pre_ref, group, first, width, rows):
    start = group * PACK
    before = jnp.where(group == 0, rows, start - RIM)
    head = pre_ref[pl.ds(pl.multiple_of(before, RIM), RIM), first : first + width]
    body = pre_ref[pl.ds(pl.multiple_of(start, PACK), PACK), first : first + width]
    return jnp.concatenate([head, body], axis=0)


def active_of(window, taps_ref, valid, first, width):
    pieces = window_taps(window, PACK)
    conv = None
    for j in range(CONV):
        term = pieces[j] * taps_ref[j : j + 1, first : first + width] * valid[:, j : j + 1]
        conv = term if conv is None else conv + term
    return conv, pieces


def net_of(changes, apart):
    column = jnp.sum(changes, axis=0, keepdims=True)
    column = jnp.where(apart == 0, jnp.broadcast_to(column, changes.shape), 0.0)
    return jnp.sum(changes - column, axis=1, keepdims=True)


def column_of(tile, lane):
    return tile[:, lane : lane + 1].astype(BF).astype(F32)


def forward_kernel(
    keep_ref,
    pre_ref,
    small_ref,
    taps_ref,
    valid_ref,
    rate_ref,
    bias_ref,
    keys_ref,
    inverse_ref,
    w_ref,
    u_ref,
    fold_ref,
    states_ref,
    ends_ref,
    fresh_ref,
    last_ref,
    joint_ref,
    *,
    heads,
    rows,
    key_width,
    value_width,
):
    groups = rows // PACK
    inner = PACK // GROUP
    key_cols = heads * key_width

    def solve(group, _):
        masks = pack_masks()
        row, col, apart, same, lower, strict = masks
        start = pl.multiple_of(group * PACK, PACK)
        span = pl.ds(start, PACK)
        valid = valid_ref[span, :]
        decay_tile, beta_tile = rates_of(small_ref[span, :], rate_ref[...], bias_ref[...])
        items = []
        for head in range(heads):
            decay = column_of(decay_tile, head)
            beta = column_of(beta_tile, heads + head)
            first = key_cols + head * key_width
            window = load_window(pre_ref, group, first, key_width, rows)
            conv, _ = active_of(window, taps_ref, valid, first, key_width)
            act = conv * sigmoid(conv)
            scale = lax.rsqrt(jnp.sum(act * act, axis=1, keepdims=True) + EPSILON)
            key = (act * scale).astype(BF)
            keys_ref[span, head * key_width : (head + 1) * key_width] = key
            gam, last, fading = packed_decay(decay, masks)
            gram = mm_nt(key, key)
            system = jnp.where(strict, fading * beta * gram, 0.0)
            inverse = jnp.where(apart == 0, 1.0, 0.0) - jnp.where(apart == 1, system, 0.0)
            items.append([beta, key, gam, last, system, inverse])
        level = 1
        while (1 << level) < GROUP:
            parts = [
                mm_fine(jnp.where((apart >> level) == 1, item[4], 0.0), item[5]) for item in items
            ]
            steps = [mm_fine(item[5], part) for item, part in zip(items, parts)]
            for item, step in zip(items, steps):
                item[5] = item[5] - step
            level += 1
        for head in range(heads):
            beta, key, gam, last, system, inverse = items[head]
            cols = slice(head * value_width, (head + 1) * value_width)
            first = 2 * key_cols + head * value_width
            window = load_window(pre_ref, group, first, value_width, rows)
            conv, _ = active_of(window, taps_ref, valid, first, value_width)
            value = (conv * sigmoid(conv)).astype(BF)
            keys_ref[span, key_cols + head * value_width : key_cols + (head + 1) * value_width] = (
                value
            )
            key_f = key.astype(F32)
            inverse_low = inverse.astype(BF)
            inverse_ref[group * heads + head] = inverse_low
            w_low = mm(inverse_low, beta * jnp.exp(gam) * key_f).astype(BF)
            u_low = mm(inverse_low, beta * value.astype(F32)).astype(BF)
            w_ref[span, head * key_width : (head + 1) * key_width] = w_low
            u_ref[span, cols] = u_low
            tail = jnp.exp(last - gam) * key_f
            block_of = lax.broadcasted_iota(jnp.int32, (PACK, 1), 0) // GROUP
            whole = jnp.exp(last)
            for b in range(inner):
                index = (group * inner + b) * heads + head
                tail_b = jnp.where(block_of == b, tail, 0.0).astype(BF)
                fold_ref[index] = mm_tn(tail_b, w_low).astype(BF)
                fresh_ref[index] = mm_tn(tail_b, u_low)
                last_ref[index] = jnp.broadcast_to(
                    whole[b * GROUP : b * GROUP + 1], (8, LANES)
                )
        return 0

    lax.fori_loop(0, groups, solve, 0)

    unit = jnp.where(
        lax.broadcasted_iota(jnp.int32, (key_width, key_width), 0)
        == lax.broadcasted_iota(jnp.int32, (key_width, key_width), 1),
        1.0,
        0.0,
    )
    for head in range(heads):
        joint_ref[head, :, :value_width] = jnp.zeros((key_width, value_width), F32)
        joint_ref[head, :, value_width:] = unit
    for block in range(rows // GROUP):
        for head in range(heads):
            index = block * heads + head
            joint = joint_ref[head] * keep_ref[block]
            joint_low = joint.astype(BF)
            states_ref[index] = joint_low
            fresh = last_ref[index, 0:1, 0:1] * joint - mm(fold_ref[index], joint_low)
            joint_ref[head, :, :value_width] = fresh[:, :value_width] + fresh_ref[index]
            joint_ref[head, :, value_width:] = fresh[:, value_width:]
    ends_ref[...] = joint_ref[...].astype(BF)


def mixer_forward(pre, keep, taps, valid, rate, bias, heads, key_width, value_width):
    rows = pre.shape[0] - RIM
    wide = heads * (2 * key_width + value_width)
    gate_wide = heads * value_width
    count = rows // GROUP
    packs = rows // PACK
    joint_width = key_width + value_width
    whole = lambda shape: pl.BlockSpec(shape, lambda i: (0,) * len(shape))
    outs = [
        ((rows, wide - heads * key_width), BF),
        ((packs * heads, PACK, PACK), BF),
        ((rows, heads * key_width), BF),
        ((rows, heads * value_width), BF),
        ((count * heads, key_width, key_width), BF),
        ((count * heads, key_width, joint_width), BF),
        ((heads, key_width, joint_width), BF),
    ]
    return pl.pallas_call(
        functools.partial(
            forward_kernel, heads=heads, rows=rows, key_width=key_width, value_width=value_width
        ),
        grid=(1,),
        in_specs=[
            pl.BlockSpec(memory_space=pltpu.SMEM),
            pl.BlockSpec((rows + RIM, wide), lambda i: (0, 0)),
            pl.BlockSpec((rows + RIM, LANES), lambda i: (0, (wide + gate_wide) // LANES)),
            whole(taps.shape),
            whole(valid.shape),
            whole(rate.shape),
            whole(bias.shape),
        ],
        out_specs=[whole(shape) for shape, _ in outs],
        out_shape=[jax.ShapeDtypeStruct(shape, kind) for shape, kind in outs],
        scratch_shapes=[
            pltpu.VMEM((count * heads, key_width, value_width), F32),
            pltpu.VMEM((count * heads, 8, LANES), F32),
            pltpu.VMEM((heads, key_width, joint_width), F32),
        ],
        compiler_params=pltpu.CompilerParams(vmem_limit_bytes=VMEM_LIMIT),
        cost_estimate=cost(20),
        name="mixer_forward",
    )(keep, pre, pre, taps, valid, rate, bias)


def query_kernel(
    pre_ref,
    small_ref,
    taps_ref,
    valid_ref,
    rate_ref,
    bias_ref,
    keys_ref,
    w_ref,
    u_ref,
    states_ref,
    queries_ref,
    query_w_ref,
    local_ref,
    carry_ref,
    *,
    heads,
    rows,
    key_width,
    value_width,
):
    inner = PACK // GROUP

    def ask(group, _):
        masks = pack_masks()
        span = pl.ds(pl.multiple_of(group * PACK, PACK), PACK)
        valid = valid_ref[span, :]
        decay_tile, _ = rates_of(small_ref[span, :], rate_ref[...], bias_ref[...])
        for head in range(heads):
            cols = slice(head * key_width, (head + 1) * key_width)
            value_at = slice(head * value_width, (head + 1) * value_width)
            window = load_window(pre_ref, group, head * key_width, key_width, rows)
            conv, _ = active_of(window, taps_ref, valid, head * key_width, key_width)
            act = conv * sigmoid(conv)
            scale = lax.rsqrt(jnp.sum(act * act, axis=1, keepdims=True) + EPSILON)
            query = (act * (scale * key_width ** (-0.5))).astype(BF)
            queries_ref[span, cols] = query
            gam, last, fading = packed_decay(column_of(decay_tile, head), masks)
            scores = (mm_nt(query, keys_ref[span, cols]) * fading).astype(BF)
            query_w = (
                jnp.exp(gam) * query.astype(F32) - mm(scores, w_ref[span, cols])
            ).astype(BF)
            start = mm(scores, u_ref[span, value_at])
            local, carry = [], []
            for b in range(inner):
                index = (group * inner + b) * heads + head
                part = slice(b * GROUP, (b + 1) * GROUP)
                query_w_ref[index] = query_w[part]
                moved = mm(query_w[part], states_ref[index])
                local.append(moved[:, :value_width])
                carry.append(moved[:, value_width:])
            local_ref[span, value_at] = start + jnp.concatenate(local, axis=0)
            carry_ref[span, cols] = jnp.concatenate(carry, axis=0).astype(BF)
        return 0

    lax.fori_loop(0, rows // PACK, ask, 0)


def mixer_query(pre, taps, valid, rate, bias, keys, w, u, states, heads, key_width, value_width):
    rows = pre.shape[0] - RIM
    wide = heads * (2 * key_width + value_width)
    gate_wide = heads * value_width
    whole = lambda shape: pl.BlockSpec(shape, lambda i: (0,) * len(shape))
    outs = [
        ((rows, heads * key_width), BF),
        ((rows // GROUP * heads, GROUP, key_width), BF),
        ((rows, heads * value_width), F32),
        ((rows, heads * key_width), BF),
    ]
    return pl.pallas_call(
        functools.partial(
            query_kernel, heads=heads, rows=rows, key_width=key_width, value_width=value_width
        ),
        grid=(1,),
        in_specs=[
            pl.BlockSpec((rows + RIM, heads * key_width), lambda i: (0, 0)),
            pl.BlockSpec((rows + RIM, LANES), lambda i: (0, (wide + gate_wide) // LANES)),
            whole(taps.shape),
            whole(valid.shape),
            whole(rate.shape),
            whole(bias.shape),
            pl.BlockSpec((rows, heads * key_width), lambda i: (0, 0)),
            whole(w.shape),
            whole(u.shape),
            whole(states.shape),
        ],
        out_specs=[whole(shape) for shape, _ in outs],
        out_shape=[jax.ShapeDtypeStruct(shape, kind) for shape, kind in outs],
        compiler_params=pltpu.CompilerParams(vmem_limit_bytes=VMEM_LIMIT),
        cost_estimate=cost(10),
        name="mixer_query",
    )(pre, pre, taps, valid, rate, bias, keys, w, u, states)


def rotated(shard, axis, by):
    devices = lax.axis_size(axis)
    return lax.ppermute(shard, axis, [(i, (i + by) % devices) for i in range(devices)])


def rotations(shard, axis):
    return [shard] + [rotated(shard, axis, by) for by in range(1, lax.axis_size(axis))]


def scattered(pieces, axis):
    total = pieces[0].astype(F32)
    for by in range(1, lax.axis_size(axis)):
        total = total + rotated(pieces[by], axis, by).astype(F32)
    return total


def axis_total(values, axis):
    return scattered([values] * lax.axis_size(axis), axis)


def exchanged(parts):
    return rotations(scattered(parts, "tensor").astype(BF), "tensor")


def swapped(shard):
    return lax.ppermute(shard, "fsdp", [(0, 1), (1, 0)])


def weight_rows(shard, axis):
    return lax.all_gather(shard, "fsdp", axis=axis, tiled=True)


def owners(grad):
    return lax.psum_scatter(grad, FH, scatter_dimension=0, tiled=True).astype(F32)


def owners_by_steps(grad):
    if lax.axis_size("fsdp") != 2:
        return owners(grad)
    half = grad.shape[0] // 2
    core = lax.axis_index("fsdp")
    mine = lax.dynamic_slice_in_dim(grad, core * half, half)
    other = swapped(lax.dynamic_slice_in_dim(grad, (1 - core) * half, half))
    grad = (mine.astype(F32) + other.astype(F32)).astype(BF)
    count = lax.axis_size("heads")
    rows = half // count
    spot = lax.axis_index("heads")
    return scattered(
        [
            lax.dynamic_slice_in_dim(grad, lax.rem(spot + by, count) * rows, rows)
            for by in range(count)
        ],
        "heads",
    )


def padded(width):
    return -(-width // LANES) * LANES


def weight_kernel(*refs, rows):
    out_ref = refs[-1]
    at = 0
    for index, many in enumerate(rows):
        left, right = refs[2 * index], refs[2 * index + 1]
        width = right.shape[1]
        part = mm_tn(left[...], right[...]).astype(BF)
        out_ref[:, at : at + width] = part
        if width < padded(width):
            out_ref[:, at + width : at + padded(width)] = jnp.zeros(
                (part.shape[0], padded(width) - width), BF
            )
        at += padded(width)


def weight_grads(*pairs):
    features = pairs[0][0].shape[1]
    total = sum(padded(right.shape[1]) for _, right in pairs)
    specs, args = [], []
    for left, right in pairs:
        many = right.shape[0]
        specs.append(pl.BlockSpec((many, PACK), lambda i: (0, i)))
        specs.append(pl.BlockSpec(right.shape, lambda i: (0, 0)))
        args += [left, right]
    return pl.pallas_call(
        functools.partial(weight_kernel, rows=[right.shape[0] for _, right in pairs]),
        grid=(features // PACK,),
        in_specs=specs,
        out_specs=pl.BlockSpec((PACK, total), lambda i: (i, 0)),
        out_shape=jax.ShapeDtypeStruct((features, total), BF),
        compiler_params=pltpu.CompilerParams(vmem_limit_bytes=VMEM_LIMIT),
        cost_estimate=cost(5),
        name="weight_grads",
    )(*args)


def total_batches(values):
    if lax.axis_size("fsdp") == 2:
        values = values + swapped(values)
    else:
        values = lax.psum(values, "fsdp")
    return axis_total(values, "heads")


def feature_blocks(pieces, place, whole_ref):
    count = len(pieces)
    width = whole_ref.shape[1] // count
    for by, piece in enumerate(pieces):
        at = lax.rem(place + count - by, count) * width
        whole_ref[:, pl.ds(pl.multiple_of(at, width), width)] = piece


def project_kernel(place_ref, *refs, count):
    pieces = refs[:count]
    gain_ref, weight_ref, token_ref, hidden_ref, scale_ref, pre_ref = refs[count:]
    rows = pieces[0].shape[0] - RIM

    @pl.when(pl.program_id(0) == 0)
    def _():
        feature_blocks([piece[...] for piece in pieces], place_ref[0], token_ref)

        def norm(start, many):
            span = pl.ds(start, many)
            values = token_ref[span, :].astype(F32)
            scale = lax.rsqrt(jnp.mean(values * values, axis=1, keepdims=True) + EPSILON)
            hidden_ref[span, :] = (values * scale * gain_ref[...]).astype(BF)
            scale_ref[span, :] = jnp.broadcast_to(scale, (many, LANES))

        for start in range(0, rows, PACK):
            norm(start, PACK)
        norm(rows, RIM)

    pre_ref[...] = mm(hidden_ref[...], weight_ref[...])


def project(tensor_place, pieces, gain, weight):
    total = pieces[0].shape[0]
    features, outs = weight.shape
    count = len(pieces)
    tile = 2 * LANES
    whole = lambda shape: pl.BlockSpec(shape, lambda i, at: (0,) * len(shape))
    return pl.pallas_call(
        functools.partial(project_kernel, count=count),
        grid_spec=pltpu.PrefetchScalarGridSpec(
            num_scalar_prefetch=1,
            grid=(outs // tile,),
            in_specs=[whole(piece.shape) for piece in pieces]
            + [whole(gain.shape), pl.BlockSpec((features, tile), lambda i, at: (0, i))],
            out_specs=[
                whole((total, features)),
                whole((total, features)),
                whole((total, LANES)),
                pl.BlockSpec((total, tile), lambda i, at: (0, i)),
            ],
        ),
        out_shape=[
            jax.ShapeDtypeStruct((total, features), BF),
            jax.ShapeDtypeStruct((total, features), BF),
            jax.ShapeDtypeStruct((total, LANES), F32),
            jax.ShapeDtypeStruct((total, outs), F32),
        ],
        compiler_params=pltpu.CompilerParams(vmem_limit_bytes=VMEM_LIMIT),
        cost_estimate=cost(8),
        name="project",
    )(tensor_place, *pieces, gain, weight)


def output_kernel(
    place_ref,
    local_ref,
    carry_ref,
    end1_ref,
    end2_ref,
    end3_ref,
    end4_ref,
    gate_ref,
    gain_ref,
    weight_ref,
    mixed_ref,
    normed_ref,
    enter_ref,
    *partial_refs,
    heads,
    key_width,
    value_width,
    chunks,
):
    step = pl.program_id(0)

    @pl.when(step == 0)
    def _():
        for head in range(heads):
            state = end4_ref[head, :, :value_width].astype(F32)
            for end in (end3_ref, end2_ref, end1_ref):
                state = end[head, :, :value_width].astype(F32) + mm(
                    end[head, :, value_width:], state
                )
            enter_ref[head] = state.astype(BF)

    for head in range(heads):
        cols = slice(head * value_width, (head + 1) * value_width)
        mixed = local_ref[:, cols] + mm(
            carry_ref[:, head * key_width : (head + 1) * key_width], enter_ref[head]
        )
        mixed_low = mixed.astype(BF)
        mixed_ref[:, cols] = mixed_low
        mixed = mixed_low.astype(F32)
        scale = lax.rsqrt(jnp.mean(mixed * mixed, axis=1, keepdims=True) + EPSILON)
        gate = gate_ref[:, cols]
        normed = mixed * scale * gain_ref[...] * (gate * sigmoid(gate))
        normed_ref[:, cols] = normed.astype(BF)
    count = len(partial_refs) // chunks
    width = weight_ref.shape[1] // count
    steps = pl.num_programs(0) // chunks
    for by in range(count):
        at = lax.rem(place_ref[0] + by, count) * width
        part = mm(normed_ref[...], weight_ref[:, pl.ds(pl.multiple_of(at, width), width)])
        for chunk in range(chunks):

            @pl.when(step // steps == chunk)
            def _():
                partial_refs[chunk * count + by][...] = part.astype(BF)


def mixer_output(
    local, carry, ends, tensor_place, pre, gain, weight, key_width, value_width, chunks, count
):
    rows, cols = local.shape
    heads = cols // value_width
    width = weight.shape[1] // count
    gate_block = heads * (2 * key_width + value_width) // cols
    steps = rows // PACK // chunks
    whole = lambda shape: pl.BlockSpec(shape, lambda i, at: (0,) * len(shape))

    def part_spec(chunk):
        return pl.BlockSpec(
            (PACK, width), lambda i, at: (jnp.clip(i - chunk * steps, 0, steps - 1), 0)
        )

    outs = pl.pallas_call(
        functools.partial(
            output_kernel,
            heads=heads,
            key_width=key_width,
            value_width=value_width,
            chunks=chunks,
        ),
        grid_spec=pltpu.PrefetchScalarGridSpec(
            num_scalar_prefetch=1,
            grid=(rows // PACK,),
            in_specs=[
                pl.BlockSpec((PACK, cols), lambda i, at: (i, 0)),
                pl.BlockSpec((PACK, carry.shape[1]), lambda i, at: (i, 0)),
                whole(ends[0].shape),
                whole(ends[0].shape),
                whole(ends[0].shape),
                whole(ends[0].shape),
                pl.BlockSpec((PACK, cols), lambda i, at: (i, gate_block)),
                whole(gain.shape),
                whole((cols, weight.shape[1])),
            ],
            out_specs=[
                pl.BlockSpec((PACK, cols), lambda i, at: (i, 0)),
                pl.BlockSpec((PACK, cols), lambda i, at: (i, 0)),
                whole((heads, key_width, value_width)),
            ]
            + [part_spec(chunk) for chunk in range(chunks) for _ in range(count)],
        ),
        out_shape=[
            jax.ShapeDtypeStruct((rows, cols), BF),
            jax.ShapeDtypeStruct((rows, cols), BF),
            jax.ShapeDtypeStruct((heads, key_width, value_width), BF),
        ]
        + [jax.ShapeDtypeStruct((rows // chunks, width), BF)] * (chunks * count),
        compiler_params=pltpu.CompilerParams(vmem_limit_bytes=VMEM_LIMIT),
        cost_estimate=cost(7),
        name="mixer_output",
    )(tensor_place, local, carry, *ends, pre, gain, weight)
    parts = outs[3:]
    return outs[0], outs[1], outs[2], [parts[c * count : (c + 1) * count] for c in range(chunks)]


def feed_kernel(place_ref, *refs, count, aliased):
    attn = refs[:count]
    cot_ref, token_ref, gain_ref, gate_ref, up_ref, down_ref = refs[count : count + 6]
    outs = refs[count + 6 + aliased :]
    middle_ref, hidden_ref, inner_ref, gate_grad_ref, up_grad_ref = outs[:5]
    out_refs, mid_refs = outs[5 : 5 + count], outs[5 + count : 5 + 2 * count]
    whole_ref = outs[5 + 2 * count]
    first = down_ref.shape[0] - inner_ref.shape[1]
    place = place_ref[0]
    feature_blocks([piece[...] for piece in attn], place, whole_ref)
    middle = token_ref[...].astype(F32) + whole_ref[...].astype(F32)
    middle_ref[...] = middle
    scale = lax.rsqrt(jnp.mean(middle * middle, axis=1, keepdims=True) + EPSILON)
    hidden = (middle * scale * gain_ref[...]).astype(BF)
    hidden_ref[...] = hidden
    many = inner_ref.shape[1]
    gate = mm(hidden, gate_ref[:, :many])
    up = mm(hidden, up_ref[:, :many])
    inner_grad = mm_nt(cot_ref[...], down_ref[first:, :])
    sig = sigmoid(gate)
    silu = gate * sig
    inner_ref[...] = (silu * up).astype(BF)
    gate_grad_ref[...] = (inner_grad * up * (sig * (1.0 + gate * (1.0 - sig)))).astype(BF)
    up_grad_ref[...] = (inner_grad * silu).astype(BF)
    width = whole_ref.shape[1] // count
    for by in range(count):
        at = lax.rem(place + by, count) * width
        span = pl.ds(pl.multiple_of(at, width), width)
        mid_refs[by][...] = (
            mm_nt(gate_grad_ref[...], gate_ref[span, :many])
            + mm_nt(up_grad_ref[...], up_ref[span, :many])
        ).astype(BF)
        out_refs[by][...] = mm(inner_ref[...], down_ref[first:, span]).astype(BF)


def feed_forward(chunk, chunks, tensor_place, attn, cot, token, gain, feed, down, hidden, before):
    rows, features = cot.shape
    count = len(attn)
    width = features // count
    steps = rows // PACK // chunks
    first = chunk * steps
    whole = lambda shape: pl.BlockSpec(shape, lambda i, at: (0,) * len(shape))
    rows_at = lambda size: pl.BlockSpec((PACK, size), lambda i, at: (first + i, 0))
    part = pl.BlockSpec((PACK, width), lambda i, at: (i, 0))
    inputs = [*attn, cot, token, gain, feed, feed, down]
    kept = [
        (features, F32),
        (features, BF),
        (hidden, BF),
        (hidden, BF),
        (hidden, BF),
    ] + [(width, BF)] * count
    outs = pl.pallas_call(
        functools.partial(feed_kernel, count=count, aliased=len(before)),
        grid_spec=pltpu.PrefetchScalarGridSpec(
            num_scalar_prefetch=1,
            grid=(steps,),
            in_specs=[part] * count
            + [rows_at(features)] * 2
            + [
                whole(gain.shape),
                pl.BlockSpec((features, feed.shape[1] // 2), lambda i, at: (0, 0)),
                pl.BlockSpec((features, feed.shape[1] // 2), lambda i, at: (0, 1)),
                whole(down.shape),
            ]
            + [pl.BlockSpec(memory_space=pl.ANY)] * len(before),
            out_specs=[rows_at(size) for size, _ in kept] + [part] * count,
            scratch_shapes=[pltpu.VMEM((PACK, features), BF)],
        ),
        out_shape=[jax.ShapeDtypeStruct((rows, size), kind) for size, kind in kept]
        + [jax.ShapeDtypeStruct((rows // chunks, width), BF)] * count,
        input_output_aliases={1 + len(inputs) + i: i for i in range(len(before))},
        compiler_params=pltpu.CompilerParams(vmem_limit_bytes=VMEM_LIMIT),
        cost_estimate=cost(10),
        name="feed_forward",
    )(tensor_place, *inputs, *before)
    return outs[: 5 + count], outs[5 + count :]


def gate_back_kernel(
    place_ref, *refs, count, aliased, heads, key_width, value_width
):
    pieces = refs[:count]
    (
        middle_ref,
        cot_ref,
        ffn_gain_ref,
        weight_ref,
        mixed_ref,
        gate_ref,
        gain_ref,
        query_w_ref,
        states_ref,
    ) = refs[count : count + 9]
    (
        attn_grad_ref,
        mixed_grad_ref,
        gate_grad_ref,
        source_ref,
        own_ref,
        ffn_gain_grad_ref,
        gain_grad_ref,
        enter_grad_ref,
        whole_ref,
        middle_grad_ref,
    ) = refs[count + 9 + aliased :]
    inner = PACK // GROUP

    @pl.when(pl.program_id(0) == 0)
    def _():
        gain_grad_ref[...] = jnp.zeros_like(gain_grad_ref)
        ffn_gain_grad_ref[...] = jnp.zeros_like(ffn_gain_grad_ref)
        enter_grad_ref[...] = jnp.zeros_like(enter_grad_ref)

    feature_blocks([piece[...] for piece in pieces], place_ref[0], whole_ref)
    middle = middle_ref[...]
    scale_mid = lax.rsqrt(jnp.mean(middle * middle, axis=1, keepdims=True) + EPSILON)
    hidden_grad = whole_ref[...].astype(F32)
    unit_mid = middle * scale_mid
    ffn_gain_grad_ref[0:1, :] += jnp.sum(hidden_grad * unit_mid, axis=0, keepdims=True)
    scaled_mid = hidden_grad * ffn_gain_ref[...]
    along = jnp.mean(scaled_mid * unit_mid, axis=1, keepdims=True)
    middle_grad = cot_ref[...].astype(F32) + scale_mid * (scaled_mid - unit_mid * along)
    middle_grad_ref[...] = middle_grad
    width = own_ref.shape[1]
    own_ref[...] = middle_grad_ref[
        :, pl.ds(pl.multiple_of(place_ref[0] * width, width), width)
    ]
    attn_grad = middle_grad.astype(BF)
    attn_grad_ref[...] = attn_grad
    normed_grad = mm_nt(attn_grad, weight_ref[...])
    gain = gain_ref[...]
    for head in range(heads):
        cols = slice(head * value_width, (head + 1) * value_width)
        grad = normed_grad[:, cols]
        mixed = mixed_ref[:, cols].astype(F32)
        scale = lax.rsqrt(jnp.mean(mixed * mixed, axis=1, keepdims=True) + EPSILON)
        gate = gate_ref[:, cols]
        sig = sigmoid(gate)
        silu = gate * sig
        unit = mixed * scale
        scaled = grad * unit
        gate_grad_ref[:, cols] = (scaled * gain * (sig * (1.0 + gate * (1.0 - sig)))).astype(BF)
        gain_grad_ref[0:1, :] += jnp.sum(scaled * silu, axis=0, keepdims=True)
        unit_grad = grad * gain * silu
        mixed_grad = scale * (unit_grad - unit * jnp.mean(unit_grad * unit, axis=1, keepdims=True))
        mixed_grad = mixed_grad.astype(BF)
        mixed_grad_ref[:, cols] = mixed_grad
        total = enter_grad_ref[head]
        for b in range(inner):
            index = b * heads + head
            source = mm_tn(
                query_w_ref[index], mixed_grad[b * GROUP : (b + 1) * GROUP]
            )
            source_ref[index] = source
            total = total + mm_tn(states_ref[index, :, value_width:], source)
        enter_grad_ref[head] = total


def gate_back(
    chunk,
    chunks,
    tensor_place,
    pieces,
    middle,
    cot,
    ffn_gain,
    weight,
    mixed,
    pre,
    gain,
    query_w,
    states,
    before,
    key_width,
    value_width,
):
    rows, features = middle.shape
    width = pieces[0].shape[1]
    cols = mixed.shape[1]
    heads = cols // value_width
    gate_block = heads * (2 * key_width + value_width) // cols
    step = PACK // GROUP * heads
    steps = rows // PACK // chunks
    first = chunk * steps
    whole = lambda shape: pl.BlockSpec(shape, lambda i, at: (0,) * len(shape))
    rows_at = lambda size, col=0: pl.BlockSpec((PACK, size), lambda i, at: (first + i, col))
    blocks_at = lambda shape: pl.BlockSpec((step,) + shape, lambda i, at: (first + i, 0, 0))
    inputs = [*pieces, middle, cot, ffn_gain, weight, mixed, pre, gain, query_w, states]
    outs = pl.pallas_call(
        functools.partial(
            gate_back_kernel,
            count=len(pieces),
            aliased=len(before),
            heads=heads,
            key_width=key_width,
            value_width=value_width,
        ),
        grid_spec=pltpu.PrefetchScalarGridSpec(
            num_scalar_prefetch=1,
            grid=(steps,),
            in_specs=[pl.BlockSpec((PACK, width), lambda i, at: (i, 0))] * len(pieces)
            + [
                rows_at(features),
                rows_at(features),
                whole(ffn_gain.shape),
                whole((cols, features)),
                rows_at(cols),
                rows_at(cols, gate_block),
                whole(gain.shape),
                blocks_at(query_w.shape[1:]),
                blocks_at(states.shape[1:]),
            ]
            + [pl.BlockSpec(memory_space=pl.ANY)] * len(before),
            out_specs=[
                rows_at(features),
                rows_at(cols),
                rows_at(cols),
                blocks_at((key_width, value_width)),
                rows_at(width),
                whole((8, features)),
                whole((8, value_width)),
                whole((heads, key_width, value_width)),
            ],
            scratch_shapes=[pltpu.VMEM((PACK, features), BF), pltpu.VMEM((PACK, features), F32)],
        ),
        out_shape=[
            jax.ShapeDtypeStruct((rows, features), BF),
            jax.ShapeDtypeStruct((rows, cols), BF),
            jax.ShapeDtypeStruct((rows, cols), BF),
            jax.ShapeDtypeStruct((rows // GROUP * heads, key_width, value_width), F32),
            jax.ShapeDtypeStruct((rows, width), F32),
            jax.ShapeDtypeStruct((8, features), F32),
            jax.ShapeDtypeStruct((8, value_width), F32),
            jax.ShapeDtypeStruct((heads, key_width, value_width), F32),
        ],
        input_output_aliases={1 + len(inputs) + i: i for i in range(len(before))},
        compiler_params=pltpu.CompilerParams(vmem_limit_bytes=VMEM_LIMIT),
        cost_estimate=cost(7),
        name="gate_back",
    )(tensor_place, *inputs, *before)
    return outs[:5], outs[5:]


def input_kernel(
    place_ref,
    pre_grad_ref,
    small_grad_ref,
    gate_grad_ref,
    weight_ref,
    token_ref,
    scale_ref,
    gain_ref,
    dot_ref,
    gain_grad_ref,
    rim_ref,
    part_ref,
    terms_ref,
):
    rows = gate_grad_ref.shape[0]
    wide = pre_grad_ref.shape[1]
    gate_wide = gate_grad_ref.shape[1]
    small_wide = small_grad_ref.shape[1]
    width = token_ref.shape[1]
    step = pl.program_id(0)

    @pl.when(step == 0)
    def _():
        dot_ref[...] = jnp.zeros_like(dot_ref)

    terms = mm_nt(pre_grad_ref[...], weight_ref[:, :wide])
    terms = terms + mm_nt(
        small_grad_ref[...], weight_ref[:, wide + gate_wide : wide + gate_wide + small_wide]
    )
    terms_ref[...] = terms
    terms_ref[:rows, :] += mm_nt(gate_grad_ref[...], weight_ref[:, wide : wide + gate_wide])
    rim_ref[...] = terms_ref[rows:, :]
    terms = terms_ref[...]
    product = terms * token_ref[...].astype(F32)
    dot_ref[...] += jnp.sum(product * gain_ref[...], axis=1, keepdims=True)
    total = jnp.sum(product * scale_ref[:, 0:1], axis=0, keepdims=True)
    gain_grad_ref[...] = jnp.broadcast_to(total, gain_grad_ref.shape)
    part_ref[...] = terms[:rows].astype(BF)


def input_terms(tensor_place, pre_grad, small_grad, gate_grad, weight, token, scale, gain, count):
    total, wide = pre_grad.shape
    rows, gate_wide = gate_grad.shape
    features, outs = weight.shape
    width = features // count
    whole = lambda shape: pl.BlockSpec(shape, lambda i, at: (0,) * len(shape))
    spot = lambda i, at: lax.rem(at[0] + i, count)
    found = pl.pallas_call(
        input_kernel,
        grid_spec=pltpu.PrefetchScalarGridSpec(
            num_scalar_prefetch=1,
            grid=(count,),
            in_specs=[
                whole(pre_grad.shape),
                whole(small_grad.shape),
                whole(gate_grad.shape),
                pl.BlockSpec((width, outs), lambda i, at: (spot(i, at), 0)),
                pl.BlockSpec((total, width), lambda i, at: (0, spot(i, at))),
                whole(scale.shape),
                pl.BlockSpec((1, width), lambda i, at: (0, spot(i, at))),
            ],
            out_specs=[
                whole((total, LANES)),
                pl.BlockSpec((8, width), lambda i, at: (0, spot(i, at))),
                pl.BlockSpec((RIM, width), lambda i, at: (0, spot(i, at))),
                pl.BlockSpec((rows, width), lambda i, at: (0, spot(i, at))),
            ],
            scratch_shapes=[pltpu.VMEM((total, width), F32)],
        ),
        out_shape=[
            jax.ShapeDtypeStruct((total, LANES), F32),
            jax.ShapeDtypeStruct((8, features), F32),
            jax.ShapeDtypeStruct((RIM, features), F32),
            jax.ShapeDtypeStruct((rows, features), BF),
        ],
        compiler_params=pltpu.CompilerParams(vmem_limit_bytes=VMEM_LIMIT),
        cost_estimate=cost(8),
        name="input_terms",
    )(tensor_place, pre_grad, small_grad, gate_grad, weight, token, scale, gain)
    return found


def conv_back(unit_grad, window, taps_ref, valid, first, width, factor, taps_grad_ref):
    conv, pieces = active_of(window, taps_ref, valid, first, width)
    sig = sigmoid(conv)
    act_grad = unit_grad
    if factor is not None:
        act = conv * sig
        scale = lax.rsqrt(jnp.sum(act * act, axis=1, keepdims=True) + EPSILON)
        along = jnp.sum(unit_grad * act, axis=1, keepdims=True)
        act_grad = (factor * scale) * (unit_grad - act * (scale * scale * along))
    conv_grad = act_grad * (sig * (1.0 + conv * (1.0 - sig)))
    for j in range(CONV):
        taps_grad_ref[j : j + 1, first : first + width] += jnp.sum(
            conv_grad * valid[:, j : j + 1] * pieces[j], axis=0, keepdims=True
        )
    return conv_grad


def ready_kernel(
    pre_ref,
    small_ref,
    taps_ref,
    valid_ref,
    rate_ref,
    bias_ref,
    queries_ref,
    keys_ref,
    w_ref,
    u_ref,
    states_ref,
    enter_ref,
    mixed_grad_ref,
    true_ref,
    whole_ref,
    renewed_ref,
    base_ref,
    key_part_ref,
    conv_grad_ref,
    taps_grad_ref,
    along_ref,
    *,
    heads,
    rows,
    key_width,
    value_width,
):
    groups = rows // PACK
    inner = PACK // GROUP
    taps_grad_ref[...] = jnp.zeros_like(taps_grad_ref)
    def ready(group, _):
        masks = pack_masks()
        row, col, apart, same, lower, strict = masks
        span = pl.ds(pl.multiple_of(group * PACK, PACK), PACK)
        valid = valid_ref[pl.ds(pl.multiple_of(group * PACK + RIM, RIM), PACK), :]
        decay_tile, _ = rates_of(small_ref[span, :], rate_ref[...], bias_ref[...])
        lane = lax.broadcasted_iota(jnp.int32, (PACK, LANES), 1)
        along = jnp.zeros((PACK, LANES), F32)
        for head in range(heads):
            cols = slice(head * key_width, (head + 1) * key_width)
            value_at = slice(head * value_width, (head + 1) * value_width)
            query = queries_ref[span, cols]
            key = keys_ref[span, cols]
            gam, last, fading = packed_decay(column_of(decay_tile, head), masks)
            whole = jnp.exp(last)
            scores = mm_nt(query, key) * fading
            w = w_ref[span, cols]
            u = u_ref[span, value_at]
            out_grad = mixed_grad_ref[span, value_at]
            renewed, grown_grad = [], []
            for b in range(inner):
                index = (group * inner + b) * heads + head
                part = slice(b * GROUP, (b + 1) * GROUP)
                whole_ref[index] = jnp.broadcast_to(whole[b * GROUP : b * GROUP + 1], (8, LANES))
                state = (
                    states_ref[index, :, :value_width].astype(F32)
                    + mm(states_ref[index, :, value_width:], enter_ref[head])
                ).astype(BF)
                true_ref[index] = state
                renewed.append(u[part].astype(F32) - mm(w[part], state))
                grown_grad.append(mm_nt(out_grad[part], state))
            renewed = jnp.concatenate(renewed, axis=0).astype(BF)
            renewed_ref[span, value_at] = renewed
            base_ref[span, value_at] = mm_tn(scores, out_grad)
            scores_grad = jnp.where(lower, mm_nt(out_grad, renewed), 0.0)
            pair_grad = (scores_grad * fading).astype(BF)
            grown_grad = jnp.exp(gam) * jnp.concatenate(grown_grad, axis=0)
            query_grad = mm(pair_grad, key) + grown_grad
            along = jnp.where(
                lane == head,
                net_of(scores_grad * scores, apart)
                + jnp.sum(grown_grad * query.astype(F32), axis=1, keepdims=True),
                along,
            )
            key_part_ref[span, cols] = mm_tn(pair_grad, query)
            window = load_window(pre_ref, group, head * key_width, key_width, rows)
            conv_grad_ref[span, cols] = conv_back(
                query_grad,
                window,
                taps_ref,
                valid,
                head * key_width,
                key_width,
                key_width ** (-0.5),
                taps_grad_ref,
            )
        along_ref[span, :] = along
        return 0

    lax.fori_loop(0, groups, ready, 0)


def mixer_ready(
    pre,
    taps,
    valid,
    rate,
    bias,
    queries,
    keys,
    w,
    u,
    states,
    enter,
    mixed_grad,
    heads,
    key_width,
    value_width,
):
    rows = pre.shape[0] - RIM
    wide = heads * (2 * key_width + value_width)
    gate_wide = heads * value_width
    count = rows // GROUP
    key_cols = heads * key_width
    whole = lambda shape: pl.BlockSpec(shape, lambda i: (0,) * len(shape))
    outs = [
        ((count * heads, key_width, value_width), BF),
        ((count * heads, 8, LANES), F32),
        ((rows, heads * value_width), BF),
        ((rows, heads * value_width), F32),
        ((rows, key_cols), F32),
        ((rows, key_cols), F32),
        ((8, key_cols), F32),
        ((rows, LANES), F32),
    ]
    return pl.pallas_call(
        functools.partial(
            ready_kernel, heads=heads, rows=rows, key_width=key_width, value_width=value_width
        ),
        grid=(1,),
        in_specs=[
            pl.BlockSpec((rows + RIM, key_cols), lambda i: (0, 0)),
            pl.BlockSpec((rows + RIM, LANES), lambda i: (0, (wide + gate_wide) // LANES)),
            whole(taps.shape),
            whole(valid.shape),
            whole(rate.shape),
            whole(bias.shape),
            whole(queries.shape),
            pl.BlockSpec((rows, key_cols), lambda i: (0, 0)),
            whole(w.shape),
            whole(u.shape),
            whole(states.shape),
            whole(enter.shape),
            whole(mixed_grad.shape),
        ],
        out_specs=[whole(shape) for shape, _ in outs],
        out_shape=[jax.ShapeDtypeStruct(shape, kind) for shape, kind in outs],
        compiler_params=pltpu.CompilerParams(vmem_limit_bytes=VMEM_LIMIT),
        cost_estimate=cost(14),
        name="mixer_ready",
    )(
        pre,
        pre,
        taps,
        valid,
        rate,
        bias,
        queries,
        keys,
        w,
        u,
        states,
        enter,
        mixed_grad,
    )


def backward_kernel(
    keep_ref,
    pre_ref,
    small_ref,
    taps_ref,
    valid_ref,
    rate_ref,
    bias_ref,
    keys_ref,
    inverse_ref,
    w_ref,
    u_ref,
    fold_ref,
    source_ref,
    true_ref,
    whole_ref,
    renewed_ref,
    base_ref,
    key_part_ref,
    query_conv_ref,
    query_taps_ref,
    along_ref,
    next1_ref,
    next2_ref,
    next3_ref,
    next4_ref,
    pre_grad_ref,
    small_grad_ref,
    taps_grad_ref,
    rate_grad_ref,
    later_ref,
    conv_grad_ref,
    flow_ref,
    *,
    heads,
    rows,
    key_width,
    value_width,
):
    groups = rows // PACK
    inner = PACK // GROUP
    key_cols = heads * key_width
    wide = heads * (2 * key_width + value_width)
    taps_grad_ref[...] = jnp.zeros_like(taps_grad_ref)
    taps_grad_ref[:, :key_cols] = query_taps_ref[...]
    rate_grad_ref[...] = jnp.zeros_like(rate_grad_ref)
    conv_grad_ref[0:RIM, :] = jnp.zeros((RIM, wide), F32)
    conv_grad_ref[RIM + rows :, :] = jnp.zeros((RIM, wide), F32)
    conv_grad_ref[RIM : RIM + rows, :key_cols] = query_conv_ref[...]
    small_grad_ref[rows:, :] = jnp.zeros((RIM, LANES), BF)

    for head in range(heads):
        flow = next4_ref[head, :, :value_width].astype(F32)
        for near in (next3_ref, next2_ref, next1_ref):
            flow = near[head, :, :value_width].astype(F32) + mm_tn(
                near[head, :, value_width:], flow
            )
        flow_ref[head] = flow
    for block in reversed(range(rows // GROUP)):
        for head in range(heads):
            index = block * heads + head
            flow = flow_ref[head]
            flow_low = flow.astype(BF)
            later_ref[index] = flow_low
            flow_ref[head] = keep_ref[block] * (
                whole_ref[index, 0:1, 0:1] * flow
                - mm_tn(fold_ref[index], flow_low)
                + source_ref[index]
            )

    def back(group, _):
        masks = pack_masks()
        row, col, apart, same, lower, strict = masks
        span = pl.ds(pl.multiple_of(group * PACK, PACK), PACK)
        small = small_ref[span, :]
        valid = valid_ref[pl.ds(pl.multiple_of(group * PACK + RIM, RIM), PACK), :]
        decay_tile, beta_tile = rates_of(small, rate_ref[...], bias_ref[...])
        lane = lax.broadcasted_iota(jnp.int32, (PACK, LANES), 1)
        small_rows = jnp.zeros((PACK, LANES), F32)
        for head in range(heads):
            decay = column_of(decay_tile, head)
            beta = column_of(beta_tile, heads + head)
            cols = slice(head * key_width, (head + 1) * key_width)
            value_at = slice(head * value_width, (head + 1) * value_width)
            key = keys_ref[span, cols]
            value = keys_ref[span, key_cols + head * value_width : key_cols + (head + 1) * value_width]
            key_f = key.astype(F32)
            gam, last, fading = packed_decay(decay, masks)
            growth = jnp.exp(gam)
            rest = jnp.exp(last - gam)
            gram = mm_nt(key, key)
            tail = (rest * key_f).astype(BF)
            w = w_ref[span, cols]
            u = u_ref[span, value_at]
            renewed = renewed_ref[span, value_at]
            renewed_grad, drops = [], []
            for b in range(inner):
                index = (group * inner + b) * heads + head
                flow = later_ref[index]
                renewed_grad.append(mm(tail[b * GROUP : (b + 1) * GROUP], flow))
                shared = true_ref[index].astype(F32) * flow.astype(F32)
                shared = jnp.sum(jnp.sum(shared, axis=1, keepdims=True), axis=0, keepdims=True)
                drops.append(
                    jnp.broadcast_to(shared * whole_ref[index, 0:1, 0:1], (GROUP, 1))
                )
            renewed_low = (base_ref[span, value_at] + jnp.concatenate(renewed_grad, axis=0)).astype(
                BF
            )
            tail_grad, w_grad = [], []
            for b in range(inner):
                index = (group * inner + b) * heads + head
                part = slice(b * GROUP, (b + 1) * GROUP)
                tail_grad.append(mm_nt(renewed[part], later_ref[index]))
                w_grad.append(mm_nt(renewed_low[part], true_ref[index]))
            tail_grad = jnp.concatenate(tail_grad, axis=0)
            w_grad = -jnp.concatenate(w_grad, axis=0)
            inverse = inverse_ref[group * heads + head]
            keys_grad = mm_tn(inverse, w_grad)
            values_grad = mm_tn(inverse, renewed_low)
            system_grad = jnp.where(strict, -(mm_nt(keys_grad, w) + mm_nt(values_grad, u)), 0.0)
            gram_beta = system_grad * fading
            gram_grad = (gram_beta * beta).astype(BF)
            key_grad = (
                mm(gram_grad, key)
                + mm_tn(gram_grad, key)
                + key_part_ref[span, cols]
                + beta * growth * keys_grad
                + rest * tail_grad
            )
            value_grad = beta * values_grad
            keys_dot = growth * jnp.sum(keys_grad * key_f, axis=1, keepdims=True)
            beta_grad = (
                keys_dot
                + jnp.sum(values_grad * value.astype(F32), axis=1, keepdims=True)
                + jnp.sum(gram_beta * gram, axis=1, keepdims=True)
            )
            tail_dot = rest * jnp.sum(tail_grad * key_f, axis=1, keepdims=True)
            system = jnp.where(strict, fading * beta * gram, 0.0)
            gam_grad = (
                along_ref[span, head : head + 1]
                + beta * keys_dot
                + net_of(system_grad * system, apart)
            )
            gam_grad_row = jnp.sum(
                jnp.where(apart == 0, jnp.broadcast_to(gam_grad, (PACK, PACK)), 0.0),
                axis=0,
                keepdims=True,
            )
            tail_row = jnp.sum(
                jnp.where(apart == 0, jnp.broadcast_to(tail_dot, (PACK, PACK)), 0.0),
                axis=0,
                keepdims=True,
            )
            decay_grad = jnp.sum(
                jnp.where(same, jnp.where(col >= row, gam_grad_row, tail_row), 0.0),
                axis=1,
                keepdims=True,
            ) + jnp.concatenate(drops, axis=0)
            small_rows = jnp.where(lane == head, decay_grad, small_rows)
            small_rows = jnp.where(lane == heads + head, beta_grad, small_rows)

            for first, width, unit_grad, factor in (
                (key_cols + head * key_width, key_width, key_grad, 1.0),
                (2 * key_cols + head * value_width, value_width, value_grad, None),
            ):
                window = load_window(pre_ref, group, first, width, rows)
                conv_grad_ref[
                    pl.ds(pl.multiple_of(group * PACK + RIM, RIM), PACK), first : first + width
                ] = conv_back(
                    unit_grad, window, taps_ref, valid, first, width, factor, taps_grad_ref
                )

        raw = small + bias_ref[...]
        slope = -jnp.exp(rate_ref[...]) * sigmoid(raw)
        small_grad = jnp.where(
            lane < heads, small_rows * slope, small_rows * beta_tile * (1.0 - beta_tile)
        )
        small_grad = jnp.where(lane < 2 * heads, small_grad, 0.0)
        small_grad_ref[span, :] = small_grad.astype(BF)
        rate_grad_ref[0:1, :] += jnp.sum(small_rows * decay_tile, axis=0, keepdims=True)
        rate_grad_ref[1:2, :] += jnp.sum(small_grad, axis=0, keepdims=True)
        return 0

    lax.fori_loop(0, groups, back, 0)

    def convolve_back(start, target, count, first):
        cols = slice(first, first + LANES)
        window = conv_grad_ref[pl.ds(start, count + RIM), cols]
        flags = valid_ref[pl.ds(start, count + RIM), :]
        total = None
        for j in range(CONV):
            term = window * (flags[:, j : j + 1] * taps_ref[j : j + 1, cols])
            shift = CONV - 1 - j
            if shift:
                term = pltpu.roll(term, count + RIM - shift, 0)
            total = term if total is None else total + term
        pre_grad_ref[pl.ds(target, count), cols] = total[:count].astype(BF)

    def spread(group, _):
        base = pl.multiple_of(group * PACK, PACK)
        for first in range(0, wide, LANES):
            convolve_back(pl.multiple_of(base + RIM, RIM), base, PACK, first)
        return 0

    lax.fori_loop(0, groups, spread, 0)
    for first in range(0, wide, LANES):
        convolve_back(0, rows, RIM, first)


def mixer_backward(
    keep,
    pre,
    taps,
    valid,
    rate,
    bias,
    keys,
    inverse,
    w,
    u,
    fold,
    source,
    found,
    nexts,
    heads,
    key_width,
    value_width,
):
    rows = pre.shape[0] - RIM
    wide = heads * (2 * key_width + value_width)
    gate_wide = heads * value_width
    count = rows // GROUP
    whole = lambda shape: pl.BlockSpec(shape, lambda i: (0,) * len(shape))
    outs = [
        ((rows + RIM, wide), BF),
        ((rows + RIM, LANES), BF),
        ((8, wide), F32),
        ((8, LANES), F32),
    ]
    given = [taps, valid, rate, bias, keys, inverse, w, u, fold, source, *found, *nexts]
    return pl.pallas_call(
        functools.partial(
            backward_kernel, heads=heads, rows=rows, key_width=key_width, value_width=value_width
        ),
        grid=(1,),
        in_specs=[
            pl.BlockSpec(memory_space=pltpu.SMEM),
            pl.BlockSpec((rows + RIM, wide), lambda i: (0, 0)),
            pl.BlockSpec((rows + RIM, LANES), lambda i: (0, (wide + gate_wide) // LANES)),
        ]
        + [whole(array.shape) for array in given],
        out_specs=[whole(shape) for shape, _ in outs],
        out_shape=[jax.ShapeDtypeStruct(shape, kind) for shape, kind in outs],
        scratch_shapes=[
            pltpu.VMEM((count * heads, key_width, value_width), BF),
            pltpu.VMEM((rows + 2 * RIM, wide), F32),
            pltpu.VMEM((heads, key_width, value_width), F32),
        ],
        compiler_params=pltpu.CompilerParams(vmem_limit_bytes=VMEM_LIMIT),
        cost_estimate=cost(25),
        name="mixer_backward",
    )(keep, pre, pre, *given)


def spread_into(piece, whole_shape, start, axis_number):
    return lax.dynamic_update_slice_in_dim(jnp.zeros(whole_shape, F32), piece, start, axis_number)


def lane_row(values):
    return jnp.pad(values, (0, LANES - values.shape[0]))[None, :]


def per_device(
    tokens,
    cotangent,
    lengths,
    norm_gain,
    query_weight,
    key_weight,
    value_weight,
    outgate_weight,
    alpha_weight,
    beta_weight,
    output_weight,
    conv_query,
    conv_key,
    conv_value,
    log_rate,
    step_bias,
    out_gain,
    ffn_gain,
    gate_weight,
    up_weight,
    down_weight,
):
    rows, slice_width = tokens.shape
    count = lax.axis_size("tensor")
    full_width = slice_width * count
    tensor_place = lax.axis_index("tensor")
    tensor_array = tensor_place.astype(jnp.int32)[None]
    place = lax.axis_index(FH)
    key_cols = query_weight.shape[1]
    value_cols = value_weight.shape[1]
    heads = alpha_weight.shape[1]
    key_width = key_cols // heads
    value_width = value_cols // heads
    wide = 2 * key_cols + value_cols
    reach = LONGEST // rows

    rim_slice = shifted(tokens[rows - RIM :], FH, 1)
    token_pieces = rotations(jnp.concatenate([tokens, rim_slice], axis=0), "tensor")
    small_shard = jnp.pad(
        jnp.concatenate([alpha_weight, beta_weight], axis=1), ((0, 0), (0, 2 * LANES - 2 * heads))
    )
    in_full = weight_rows(
        jnp.concatenate(
            [query_weight, key_weight, value_weight, outgate_weight, small_shard], axis=1
        ),
        0,
    )
    hidden = gate_weight.shape[1]
    room = ((0, 0), (0, padded(hidden) - hidden))
    down_full = weight_rows(jnp.concatenate([output_weight, down_weight], axis=0), 1)
    feed_full = weight_rows(
        jnp.concatenate([jnp.pad(gate_weight, room), jnp.pad(up_weight, room)], axis=1), 0
    )

    starts = jnp.cumsum(lengths) - lengths
    places = place * rows + jnp.arange(rows, dtype=jnp.int32)
    latest = jnp.max(jnp.where(starts[None, :] <= places[:, None], starts[None, :], 0), axis=1)
    tap_index = jnp.arange(8, dtype=jnp.int32)
    valid = ((places - latest)[:, None] >= CONV - 1 - tap_index[None, :]).astype(F32)
    valid_padded = jnp.pad(valid, ((RIM, RIM), (0, 0)))
    block_first = place * rows + jnp.arange(rows // GROUP, dtype=jnp.int32) * GROUP
    keep = 1.0 - jnp.any(block_first[:, None] == starts[None, :], axis=1).astype(F32)
    taps = jnp.concatenate(
        [
            lax.dynamic_slice_in_dim(conv_query, tensor_place * key_cols, key_cols, 1),
            lax.dynamic_slice_in_dim(conv_key, tensor_place * key_cols, key_cols, 1),
            lax.dynamic_slice_in_dim(conv_value, tensor_place * value_cols, value_cols, 1),
        ],
        axis=1,
    )
    rate = lane_row(lax.dynamic_slice_in_dim(log_rate, tensor_place * heads, heads))
    bias = lane_row(lax.dynamic_slice_in_dim(step_bias, tensor_place * heads, heads))
    gain_row = out_gain[None, :]
    norm_row = norm_gain[None, :]
    ffn_row = ffn_gain[None, :]

    token_rows, hidden_in, scale_in, pre = project(
        tensor_array, token_pieces, norm_row, in_full
    )
    cot_held, *_ = lax.optimization_barrier((cotangent, *token_pieces[1:]))
    cot_rows = lax.all_gather(cot_held, "tensor", axis=1, tiled=True)

    keys, inverse, w, u, fold, states, end = mixer_forward(
        pre, keep, taps, valid, rate, bias, heads, key_width, value_width
    )
    queries, query_w, local, carry = mixer_query(
        pre, taps, valid, rate, bias, keys, w, u, states, heads, key_width, value_width
    )
    ends = [shifted(end, FH, by) for by in range(1, reach + 1)]
    ends[0], cot_rows = lax.optimization_barrier((ends[0], cot_rows))
    mixed, normed, enter, attn_parts = mixer_output(
        local,
        carry,
        ends,
        tensor_array,
        pre,
        gain_row,
        down_full,
        key_width,
        value_width,
        CHUNKS,
        count,
    )

    kept, mid_parts = (), []
    attn_chunks = [exchanged(parts) for parts in attn_parts]
    for chunk in range(CHUNKS):
        kept, mid = feed_forward(
            chunk,
            CHUNKS,
            tensor_array,
            attn_chunks[chunk],
            cot_rows,
            token_rows,
            ffn_row,
            feed_full,
            down_full,
            hidden,
            kept,
        )
        mid_parts.append(mid)
    middle, hidden_mid, inner_act, gate_grad, up_grad, *out_parts = kept
    back_kept, sums = (), []
    mid_chunks = [exchanged(parts) for parts in mid_parts]
    inner_held = lax.optimization_barrier((inner_act, mid_chunks[0][0]))[0]
    feed_local = weight_grads(
        (hidden_mid, gate_grad), (hidden_mid, up_grad), (cot_rows, inner_held)
    )
    feed_grads = owners(feed_local)
    mid_chunks[0][0] = lax.optimization_barrier((mid_chunks[0][0], feed_local))[0]
    for chunk in range(CHUNKS):
        back_kept, found = gate_back(
            chunk,
            CHUNKS,
            tensor_array,
            mid_chunks[chunk],
            middle,
            cot_rows,
            ffn_row,
            down_full,
            mixed,
            pre,
            gain_row,
            query_w,
            states,
            back_kept,
            key_width,
            value_width,
        )
        sums.append(found)
    attn_grad, mixed_grad, outgate_grad, source, middle_grad_own = back_kept
    ffn_gain_grad, out_gain_grad, enter_grad = [sum(group[1:], group[0]) for group in zip(*sums)]

    enter_low = jnp.concatenate([enter_grad.astype(BF), end[:, :, value_width:]], axis=2)
    nexts = [shifted(enter_low, FH, -by) for by in range(1, reach + 1)]
    attn_held, feed_grads = lax.optimization_barrier((attn_grad, feed_grads))
    out_local = weight_grads((attn_held, normed), (hidden_in, outgate_grad))
    out_grads = owners(out_local)
    mixed_held, out_held = lax.optimization_barrier((mixed_grad, out_parts, out_local))[:2]
    found = mixer_ready(
        pre,
        taps,
        valid_padded,
        rate,
        bias,
        queries,
        keys,
        w,
        u,
        states,
        enter,
        mixed_held,
        heads,
        key_width,
        value_width,
    )
    output_terms = scattered(out_held, "tensor")
    middle_own = lax.dynamic_slice_in_dim(middle, tensor_place * slice_width, slice_width, 1)
    output_rows = (middle_own + output_terms).astype(BF)
    pre_grad, small_grad, taps_grad, rate_grad = mixer_backward(
        keep,
        pre,
        taps,
        valid_padded,
        rate,
        bias,
        keys,
        inverse,
        w,
        u,
        fold,
        source,
        found,
        nexts,
        heads,
        key_width,
        value_width,
    )

    pre_grad, out_grads = lax.optimization_barrier((pre_grad, out_grads))
    in_dot, norm_gain_grad, rim_terms, in_part = input_terms(
        tensor_array, pre_grad, small_grad, outgate_grad, in_full, token_rows, scale_in, norm_row, count
    )
    in_grad = lax.psum_scatter(in_part, "tensor", scatter_dimension=1, tiled=True).astype(F32)
    late_held = lax.optimization_barrier((pre_grad, in_part))[0]
    late_grads = owners_by_steps(weight_grads((hidden_in, late_held), (hidden_in, small_grad)))
    rim = shifted(jnp.concatenate([rim_terms, in_dot[rows:]], axis=1), FH, -1)
    in_dot = in_dot[:rows, 0] + jnp.pad(rim[:, full_width], (rows - RIM, 0))
    rim_blocks = [
        lax.dynamic_slice_in_dim(
            rim, lax.rem(tensor_place + by, count) * slice_width, slice_width, 1
        ).reshape(-1)
        for by in range(count)
    ]

    own_gain_grad = lax.dynamic_slice_in_dim(
        ffn_gain_grad[0], tensor_place * slice_width, slice_width
    )
    pieces = (
        spread_into(taps_grad[:CONV, :key_cols], conv_query.shape, tensor_place * key_cols, 1),
        spread_into(
            taps_grad[:CONV, key_cols : 2 * key_cols], conv_key.shape, tensor_place * key_cols, 1
        ),
        spread_into(
            taps_grad[:CONV, 2 * key_cols :], conv_value.shape, tensor_place * value_cols, 1
        ),
        out_gain_grad[0],
        norm_gain_grad[0],
        spread_into(own_gain_grad, ffn_gain.shape, tensor_place * slice_width, 0),
        spread_into(rate_grad[0, :heads], log_rate.shape, tensor_place * heads, 0),
        spread_into(rate_grad[1, :heads], step_bias.shape, tensor_place * heads, 0),
    )
    flat = jnp.concatenate([piece.reshape(-1) for piece in pieces])
    flat = jnp.pad(flat, (0, -flat.size % (8 * LANES))).reshape(-1, LANES)
    flat = total_batches(flat).reshape(-1)
    joined = scattered(
        [jnp.concatenate([flat, in_dot, block]).reshape(-1, LANES) for block in rim_blocks], "tensor"
    ).reshape(-1)
    small, at = [], 0
    for piece in pieces:
        small.append(joined[at : at + piece.size].reshape(piece.shape))
        at += piece.size
    in_dot = joined[flat.size : flat.size + rows]
    rim_grad = joined[flat.size + rows :].reshape(RIM, slice_width)

    norm_slice = lax.dynamic_slice_in_dim(norm_gain, tensor_place * slice_width, slice_width)
    in_grad = in_grad + jnp.pad(rim_grad, ((rows - RIM, 0), (0, 0)))
    scale = scale_in[:rows, :1]
    tokens_grad = (
        middle_grad_own
        + scale * (in_grad * norm_slice)
        - tokens.astype(F32) * (scale * scale * scale * in_dot[:, None] / full_width)
    )

    return (
        output_rows,
        tokens_grad,
        late_grads[:, :key_cols],
        late_grads[:, key_cols : 2 * key_cols],
        late_grads[:, 2 * key_cols : wide],
        out_grads[:, value_cols:],
        late_grads[:, wide : wide + heads],
        late_grads[:, wide + heads : wide + 2 * heads],
        out_grads[:, :value_cols].T,
        feed_grads[:, :hidden],
        feed_grads[:, padded(hidden) : padded(hidden) + hidden],
        feed_grads[:, 2 * padded(hidden) : 2 * padded(hidden) + hidden].T,
        small[0],
        small[1],
        small[2],
        small[6],
        small[7],
        small[3],
        small[4],
        small[5],
    )


def solution(mesh):
    in_specs = (
        P(FH, "tensor"),
        P(FH, "tensor"),
        P(),
        P(),
        P("fsdp", "tensor"),
        P("fsdp", "tensor"),
        P("fsdp", "tensor"),
        P("fsdp", "tensor"),
        P("fsdp", "tensor"),
        P("fsdp", "tensor"),
        P("tensor", "fsdp"),
        P(),
        P(),
        P(),
        P(),
        P(),
        P(),
        P(),
        P("fsdp", "tensor"),
        P("fsdp", "tensor"),
        P("tensor", "fsdp"),
    )
    out_specs = (
        P(FH, "tensor"),
        P(FH, "tensor"),
        P(FH, "tensor"),
        P(FH, "tensor"),
        P(FH, "tensor"),
        P(FH, "tensor"),
        P(FH, "tensor"),
        P(FH, "tensor"),
        P("tensor", FH),
        P(FH, "tensor"),
        P(FH, "tensor"),
        P("tensor", FH),
        P(),
        P(),
        P(),
        P(),
        P(),
        P(),
        P(),
        P(),
    )
    return jax.shard_map(
        per_device, mesh=mesh, in_specs=in_specs, out_specs=out_specs, check_vma=False
    )
```

```python
import functools

import jax
import jax.numpy as jnp
from jax import lax
from jax.experimental import pallas as pl
from jax.experimental.pallas import tpu as pltpu
from jax.sharding import PartitionSpec as P

CONV = 4
GROUP = 64
RIM = 16
PACK = 256
LANES = 128
LONGEST = 4096
EPSILON = 1e-06
FH = ("fsdp", "heads")
ALL = ("fsdp", "heads", "tensor")
BF = jnp.bfloat16
F32 = jnp.float32
VMEM_LIMIT = 56 * 1024 * 1024
INVERSE_PASSES = 1
CHUNKS = 2
SIDES = 2


def cost(micros):
    return pl.CostEstimate(flops=int(micros * 1e9), bytes_accessed=int(micros * 3e6), transcendentals=0)


def shifted(shard, axis, by):
    devices = lax.axis_size(axis)
    pairs = [(i, i + by) for i in range(devices) if 0 <= i + by < devices]
    return lax.ppermute(shard, axis, pairs)


def dot_on(left, right, left_dim, right_dim):
    return lax.dot_general(
        left.astype(BF),
        right.astype(BF),
        (((left_dim,), (right_dim,)), ((), ())),
        preferred_element_type=F32,
    )


def mm(left, right):
    return dot_on(left, right, 1, 0)


def mm_tn(left, right):
    return dot_on(left, right, 0, 0)


def mm_nt(left, right):
    return dot_on(left, right, 1, 1)


def mm_fine(left, right):
    if INVERSE_PASSES == 1:
        return mm(left, right)
    left_high, right_high = left.astype(BF), right.astype(BF)
    left_low = left - left_high.astype(F32)
    right_low = right - right_high.astype(F32)
    return mm(left_high, right_high) + mm(left_low, right_high) + mm(left_high, right_low)


def sigmoid(value):
    return 1.0 / (1.0 + jnp.exp(-value))


def softplus(value):
    return jnp.maximum(value, 0.0) + jnp.log(1.0 + jnp.exp(-jnp.abs(value)))


def window_taps(window, rows):
    total = window.shape[0]
    return [pltpu.roll(window, total - (RIM - CONV + 1 + j), 0)[:rows] for j in range(CONV)]


def pack_masks():
    row = lax.broadcasted_iota(jnp.int32, (PACK, PACK), 0)
    col = lax.broadcasted_iota(jnp.int32, (PACK, PACK), 1)
    apart = row ^ col
    same = apart < GROUP
    return row, col, apart, same, same & (row >= col), same & (row > col)


def packed_decay(decay, masks):
    row, col, apart, same, lower, strict = masks
    spread = jnp.broadcast_to(decay, (PACK, PACK))
    decay_row = jnp.sum(jnp.where(apart == 0, spread, 0.0), axis=0, keepdims=True)
    gam_row = jnp.sum(jnp.where(same & (row <= col), spread, 0.0), axis=0, keepdims=True)
    spread_row = jnp.broadcast_to(decay_row, (PACK, PACK))
    gam = jnp.sum(jnp.where(lower, spread_row, 0.0), axis=1, keepdims=True)
    last = jnp.sum(jnp.where(same, spread_row, 0.0), axis=1, keepdims=True)
    fading = jnp.where(lower, jnp.exp(jnp.where(lower, gam - gam_row, 0.0)), 0.0)
    return gam, last, fading


def rates_of(small, rate, bias):
    decay_tile = -jnp.exp(rate) * softplus(small + bias)
    return decay_tile, sigmoid(small)


def load_window(pre_ref, group, first, width, rows):
    start = group * PACK
    before = jnp.where(group == 0, rows, start - RIM)
    head = pre_ref[pl.ds(pl.multiple_of(before, RIM), RIM), first : first + width]
    body = pre_ref[pl.ds(pl.multiple_of(start, PACK), PACK), first : first + width]
    return jnp.concatenate([head, body], axis=0)


def active_of(window, taps_ref, valid, first, width):
    pieces = window_taps(window, PACK)
    conv = None
    for j in range(CONV):
        term = pieces[j] * taps_ref[j : j + 1, first : first + width] * valid[:, j : j + 1]
        conv = term if conv is None else conv + term
    return conv, pieces


def net_of(changes, apart):
    column = jnp.sum(changes, axis=0, keepdims=True)
    column = jnp.where(apart == 0, jnp.broadcast_to(column, changes.shape), 0.0)
    return jnp.sum(changes - column, axis=1, keepdims=True)


def column_of(tile, lane):
    return tile[:, lane : lane + 1].astype(BF).astype(F32)


def forward_kernel(
    keep_ref,
    pre_ref,
    small_ref,
    taps_ref,
    valid_ref,
    rate_ref,
    bias_ref,
    keys_ref,
    inverse_ref,
    w_ref,
    u_ref,
    fold_ref,
    states_ref,
    ends_ref,
    fresh_ref,
    last_ref,
    joint_ref,
    *,
    heads,
    rows,
    key_width,
    value_width,
):
    groups = rows // PACK
    inner = PACK // GROUP
    key_cols = heads * key_width

    def solve(step, _):
        masks = pack_masks()
        row, col, apart, same, lower, strict = masks
        items = []
        for side in range(SIDES):
            group = step * SIDES + side
            span = pl.ds(pl.multiple_of(group * PACK, PACK), PACK)
            valid = valid_ref[span, :]
            decay_tile, beta_tile = rates_of(small_ref[span, :], rate_ref[...], bias_ref[...])
            for head in range(heads):
                decay = column_of(decay_tile, head)
                beta = column_of(beta_tile, heads + head)
                first = key_cols + head * key_width
                window = load_window(pre_ref, group, first, key_width, rows)
                conv, _ = active_of(window, taps_ref, valid, first, key_width)
                act = conv * sigmoid(conv)
                scale = lax.rsqrt(jnp.sum(act * act, axis=1, keepdims=True) + EPSILON)
                key = (act * scale).astype(BF)
                gam, last, fading = packed_decay(decay, masks)
                gram = mm_nt(key, key)
                system = jnp.where(strict, fading * beta * gram, 0.0)
                inverse = jnp.where(apart == 0, 1.0, 0.0) - jnp.where(apart == 1, system, 0.0)
                items.append([beta, key, gam, last, system, inverse, group, span, valid, head])
        level = 1
        while (1 << level) < GROUP:
            parts = [
                mm_fine(jnp.where((apart >> level) == 1, item[4], 0.0), item[5]) for item in items
            ]
            steps = [mm_fine(item[5], part) for item, part in zip(items, parts)]
            for item, step_of in zip(items, steps):
                item[5] = item[5] - step_of
            level += 1
        for beta, key, gam, last, system, inverse, group, span, valid, head in items:
            keys_ref[span, head * key_width : (head + 1) * key_width] = key
            cols = slice(head * value_width, (head + 1) * value_width)
            first = 2 * key_cols + head * value_width
            window = load_window(pre_ref, group, first, value_width, rows)
            conv, _ = active_of(window, taps_ref, valid, first, value_width)
            value = (conv * sigmoid(conv)).astype(BF)
            keys_ref[span, key_cols + head * value_width : key_cols + (head + 1) * value_width] = (
                value
            )
            key_f = key.astype(F32)
            inverse_low = inverse.astype(BF)
            inverse_ref[group * heads + head] = inverse_low
            w_low = mm(inverse_low, beta * jnp.exp(gam) * key_f).astype(BF)
            u_low = mm(inverse_low, beta * value.astype(F32)).astype(BF)
            w_ref[span, head * key_width : (head + 1) * key_width] = w_low
            u_ref[span, cols] = u_low
            tail = jnp.exp(last - gam) * key_f
            block_of = lax.broadcasted_iota(jnp.int32, (PACK, 1), 0) // GROUP
            whole = jnp.exp(last)
            for b in range(inner):
                index = (group * inner + b) * heads + head
                tail_b = jnp.where(block_of == b, tail, 0.0).astype(BF)
                fold_ref[index] = mm_tn(tail_b, w_low).astype(BF)
                fresh_ref[index] = mm_tn(tail_b, u_low)
                last_ref[index] = jnp.broadcast_to(
                    whole[b * GROUP : b * GROUP + 1], (8, LANES)
                )
        return 0

    lax.fori_loop(0, groups // SIDES, solve, 0)

    unit = jnp.where(
        lax.broadcasted_iota(jnp.int32, (key_width, key_width), 0)
        == lax.broadcasted_iota(jnp.int32, (key_width, key_width), 1),
        1.0,
        0.0,
    )
    for head in range(heads):
        joint_ref[head, :, :value_width] = jnp.zeros((key_width, value_width), F32)
        joint_ref[head, :, value_width:] = unit
    for block in range(rows // GROUP):
        for head in range(heads):
            index = block * heads + head
            joint = joint_ref[head] * keep_ref[block]
            joint_low = joint.astype(BF)
            states_ref[index] = joint_low
            fresh = last_ref[index, 0:1, 0:1] * joint - mm(fold_ref[index], joint_low)
            joint_ref[head, :, :value_width] = fresh[:, :value_width] + fresh_ref[index]
            joint_ref[head, :, value_width:] = fresh[:, value_width:]
    ends_ref[...] = joint_ref[...].astype(BF)


def mixer_forward(pre, keep, taps, valid, rate, bias, heads, key_width, value_width):
    rows = pre.shape[0] - RIM
    wide = heads * (2 * key_width + value_width)
    gate_wide = heads * value_width
    count = rows // GROUP
    packs = rows // PACK
    joint_width = key_width + value_width
    whole = lambda shape: pl.BlockSpec(shape, lambda i: (0,) * len(shape))
    outs = [
        ((rows, wide - heads * key_width), BF),
        ((packs * heads, PACK, PACK), BF),
        ((rows, heads * key_width), BF),
        ((rows, heads * value_width), BF),
        ((count * heads, key_width, key_width), BF),
        ((count * heads, key_width, joint_width), BF),
        ((heads, key_width, joint_width), BF),
    ]
    return pl.pallas_call(
        functools.partial(
            forward_kernel, heads=heads, rows=rows, key_width=key_width, value_width=value_width
        ),
        grid=(1,),
        in_specs=[
            pl.BlockSpec(memory_space=pltpu.SMEM),
            pl.BlockSpec((rows + RIM, wide), lambda i: (0, 0)),
            pl.BlockSpec((rows + RIM, LANES), lambda i: (0, (wide + gate_wide) // LANES)),
            whole(taps.shape),
            whole(valid.shape),
            whole(rate.shape),
            whole(bias.shape),
        ],
        out_specs=[whole(shape) for shape, _ in outs],
        out_shape=[jax.ShapeDtypeStruct(shape, kind) for shape, kind in outs],
        scratch_shapes=[
            pltpu.VMEM((count * heads, key_width, value_width), F32),
            pltpu.VMEM((count * heads, 8, LANES), F32),
            pltpu.VMEM((heads, key_width, joint_width), F32),
        ],
        compiler_params=pltpu.CompilerParams(vmem_limit_bytes=VMEM_LIMIT),
        cost_estimate=cost(20),
        name="mixer_forward",
    )(keep, pre, pre, taps, valid, rate, bias)


def query_kernel(
    head_ref,
    pre_ref,
    small_ref,
    taps_ref,
    valid_ref,
    rate_ref,
    bias_ref,
    keys_ref,
    w_ref,
    u_ref,
    states_ref,
    queries_ref,
    query_w_ref,
    local_ref,
    carry_ref,
    *,
    heads,
    rows,
    key_width,
    value_width,
):
    inner = PACK // GROUP

    masks = pack_masks()
    span = slice(0, PACK)
    valid = valid_ref[span, :]
    decay_tile, _ = rates_of(small_ref[span, :], rate_ref[...], bias_ref[...])
    for head in range(heads):
        cols = slice(head * key_width, (head + 1) * key_width)
        value_at = slice(head * value_width, (head + 1) * value_width)
        window = jnp.concatenate([head_ref[:, cols], pre_ref[:, cols]], axis=0)
        conv, _ = active_of(window, taps_ref, valid, head * key_width, key_width)
        act = conv * sigmoid(conv)
        scale = lax.rsqrt(jnp.sum(act * act, axis=1, keepdims=True) + EPSILON)
        query = (act * (scale * key_width ** (-0.5))).astype(BF)
        queries_ref[span, cols] = query
        gam, last, fading = packed_decay(column_of(decay_tile, head), masks)
        scores = (mm_nt(query, keys_ref[span, cols]) * fading).astype(BF)
        query_w = (
            jnp.exp(gam) * query.astype(F32) - mm(scores, w_ref[span, cols])
        ).astype(BF)
        start = mm(scores, u_ref[span, value_at])
        local, carry = [], []
        for b in range(inner):
            index = b * heads + head
            part = slice(b * GROUP, (b + 1) * GROUP)
            query_w_ref[index] = query_w[part]
            moved = mm(query_w[part], states_ref[index])
            local.append(moved[:, :value_width])
            carry.append(moved[:, value_width:])
        local_ref[span, value_at] = start + jnp.concatenate(local, axis=0)
        carry_ref[span, cols] = jnp.concatenate(carry, axis=0).astype(BF)


def mixer_query(pre, taps, valid, rate, bias, keys, w, u, states, heads, key_width, value_width):
    rows = pre.shape[0] - RIM
    wide = heads * (2 * key_width + value_width)
    gate_wide = heads * value_width
    whole = lambda shape: pl.BlockSpec(shape, lambda i: (0,) * len(shape))
    outs = [
        ((rows, heads * key_width), BF),
        ((rows // GROUP * heads, GROUP, key_width), BF),
        ((rows, heads * value_width), F32),
        ((rows, heads * key_width), BF),
    ]
    rows_at = lambda width: pl.BlockSpec((PACK, width), lambda i: (i, 0))
    blocks_at = lambda shape: pl.BlockSpec(
        (PACK // GROUP * heads,) + shape, lambda i: (i, 0, 0)
    )
    head_at = lambda i: jnp.where(i == 0, rows // RIM, i * (PACK // RIM) - 1)
    return pl.pallas_call(
        functools.partial(
            query_kernel, heads=heads, rows=rows, key_width=key_width, value_width=value_width
        ),
        grid=(rows // PACK,),
        in_specs=[
            pl.BlockSpec((RIM, heads * key_width), lambda i: (head_at(i), 0)),
            rows_at(heads * key_width),
            pl.BlockSpec((PACK, LANES), lambda i: (i, (wide + gate_wide) // LANES)),
            whole(taps.shape),
            rows_at(valid.shape[1]),
            whole(rate.shape),
            whole(bias.shape),
            rows_at(heads * key_width),
            rows_at(w.shape[1]),
            rows_at(u.shape[1]),
            blocks_at(states.shape[1:]),
        ],
        out_specs=[
            blocks_at(shape[1:]) if len(shape) == 3 else rows_at(shape[1]) for shape, _ in outs
        ],
        out_shape=[jax.ShapeDtypeStruct(shape, kind) for shape, kind in outs],
        compiler_params=pltpu.CompilerParams(vmem_limit_bytes=VMEM_LIMIT),
        cost_estimate=cost(10),
        name="mixer_query",
    )(pre, pre, pre, taps, valid, rate, bias, keys, w, u, states)


def rotated(shard, axis, by):
    devices = lax.axis_size(axis)
    return lax.ppermute(shard, axis, [(i, (i + by) % devices) for i in range(devices)])


def rotations(shard, axis):
    moved = [rotated(shard, axis, by) for by in reversed(range(1, lax.axis_size(axis)))]
    return [shard] + moved[::-1]


def scattered(pieces, axis):
    total = pieces[0].astype(F32)
    for by in range(1, lax.axis_size(axis)):
        total = total + rotated(pieces[by], axis, by).astype(F32)
    return total


def axis_total(values, axis):
    return scattered([values] * lax.axis_size(axis), axis)


def paired(shard, by):
    devices = lax.axis_size("tensor")
    return lax.ppermute(shard, "tensor", [(i, i ^ by) for i in range(devices)])


def pair_half(kept, sent, beside=None):
    width = kept.shape[1] // 2
    near = paired(sent, 1)
    if beside is not None:
        near = lax.optimization_barrier((near, beside))[0]
    other = (kept[:, width:].astype(F32) + near[:, width:].astype(F32)).astype(BF)
    return kept[:, :width].astype(F32) + near[:, :width].astype(F32), other


def pair_rest(own, other):
    return own + paired(other, 2).astype(F32)


def pair_gather(total):
    far = paired(total, 2)
    return [total, far, paired(jnp.concatenate([total, far], axis=1), 1)]


def pair_blocks(pieces, place, whole_ref):
    own, far, near = pieces
    width = whole_ref.shape[1] // 4
    for by, piece in ((0, own), (2, far), (1, near[:, :width]), (3, near[:, width:])):
        whole_ref[:, pl.ds(pl.multiple_of((place ^ by) * width, width), width)] = piece


def pair_parts(place, whole_width, compute, kept_ref, sent_ref):
    width = whole_width // 4
    for by, ref, col in ((1, sent_ref, 0), (3, sent_ref, 1), (0, kept_ref, 0), (2, kept_ref, 1)):
        span = pl.ds(pl.multiple_of((place ^ by) * width, width), width)
        ref[:, col * width : (col + 1) * width] = compute(span).astype(BF)


def swapped(shard):
    return lax.ppermute(shard, "fsdp", [(0, 1), (1, 0)])


def weight_rows(shard, axis):
    return lax.all_gather(shard, "fsdp", axis=axis, tiled=True)


def owners(grad):
    return lax.psum_scatter(grad, FH, scatter_dimension=0, tiled=True).astype(F32)


def owners_by_steps(grad):
    if lax.axis_size("fsdp") != 2:
        return grad, owners(grad)
    half = grad.shape[0] // 2
    core = lax.axis_index("fsdp")
    mine = lax.dynamic_slice_in_dim(grad, core * half, half)
    other = swapped(lax.dynamic_slice_in_dim(grad, (1 - core) * half, half))
    grad = (mine.astype(F32) + other.astype(F32)).astype(BF)
    count = lax.axis_size("heads")
    rows = half // count
    spot = lax.axis_index("heads")
    return grad, scattered(
        [
            lax.dynamic_slice_in_dim(grad, lax.rem(spot + by, count) * rows, rows)
            for by in range(count)
        ],
        "heads",
    )


def padded(width):
    return -(-width // LANES) * LANES


def weight_kernel(*refs, rows):
    out_ref = refs[-1]
    at = 0
    for index, many in enumerate(rows):
        left, right = refs[2 * index], refs[2 * index + 1]
        width = right.shape[1]
        part = mm_tn(left[...], right[...]).astype(BF)
        out_ref[:, at : at + width] = part
        if width < padded(width):
            out_ref[:, at + width : at + padded(width)] = jnp.zeros(
                (part.shape[0], padded(width) - width), BF
            )
        at += padded(width)


def weight_grads(*pairs):
    features = pairs[0][0].shape[1]
    total = sum(padded(right.shape[1]) for _, right in pairs)
    specs, args = [], []
    for left, right in pairs:
        many = right.shape[0]
        specs.append(pl.BlockSpec((many, PACK), lambda i: (0, i)))
        specs.append(pl.BlockSpec(right.shape, lambda i: (0, 0)))
        args += [left, right]
    return pl.pallas_call(
        functools.partial(weight_kernel, rows=[right.shape[0] for _, right in pairs]),
        grid=(features // PACK,),
        in_specs=specs,
        out_specs=pl.BlockSpec((PACK, total), lambda i: (i, 0)),
        out_shape=jax.ShapeDtypeStruct((features, total), BF),
        compiler_params=pltpu.CompilerParams(vmem_limit_bytes=VMEM_LIMIT),
        cost_estimate=cost(5),
        name="weight_grads",
    )(*args)


def total_batches(values):
    if lax.axis_size("fsdp") == 2:
        values = values + swapped(values)
    else:
        values = lax.psum(values, "fsdp")
    return axis_total(values, "heads")


def feature_blocks(pieces, place, whole_ref):
    count = len(pieces)
    width = whole_ref.shape[1] // count
    for by, piece in enumerate(pieces):
        at = lax.rem(place + count - by, count) * width
        whole_ref[:, pl.ds(pl.multiple_of(at, width), width)] = piece


def project_kernel(place_ref, *refs, count):
    pieces = refs[:count]
    gain_ref, weight_ref, token_ref, hidden_ref, scale_ref, pre_ref = refs[count:]
    rows = pieces[0].shape[0] - RIM

    @pl.when(pl.program_id(0) == 0)
    def _():
        feature_blocks([piece[...] for piece in pieces], place_ref[0], token_ref)

        def norm(start, many):
            span = pl.ds(start, many)
            values = token_ref[span, :].astype(F32)
            scale = lax.rsqrt(jnp.mean(values * values, axis=1, keepdims=True) + EPSILON)
            hidden_ref[span, :] = (values * scale * gain_ref[...]).astype(BF)
            scale_ref[span, :] = jnp.broadcast_to(scale, (many, LANES))

        for start in range(0, rows, PACK):
            norm(start, PACK)
        norm(rows, RIM)

    pre_ref[...] = mm(hidden_ref[...], weight_ref[...])


def project(tensor_place, pieces, gain, weight):
    total = pieces[0].shape[0]
    features, outs = weight.shape
    count = len(pieces)
    tile = 2 * LANES
    whole = lambda shape: pl.BlockSpec(shape, lambda i, at: (0,) * len(shape))
    return pl.pallas_call(
        functools.partial(project_kernel, count=count),
        grid_spec=pltpu.PrefetchScalarGridSpec(
            num_scalar_prefetch=1,
            grid=(outs // tile,),
            in_specs=[whole(piece.shape) for piece in pieces]
            + [whole(gain.shape), pl.BlockSpec((features, tile), lambda i, at: (0, i))],
            out_specs=[
                whole((total, features)),
                whole((total, features)),
                whole((total, LANES)),
                pl.BlockSpec((total, tile), lambda i, at: (0, i)),
            ],
        ),
        out_shape=[
            jax.ShapeDtypeStruct((total, features), BF),
            jax.ShapeDtypeStruct((total, features), BF),
            jax.ShapeDtypeStruct((total, LANES), F32),
            jax.ShapeDtypeStruct((total, outs), F32),
        ],
        compiler_params=pltpu.CompilerParams(vmem_limit_bytes=VMEM_LIMIT),
        cost_estimate=cost(8),
        name="project",
    )(tensor_place, *pieces, gain, weight)


def output_kernel(
    place_ref,
    local_ref,
    carry_ref,
    end1_ref,
    end2_ref,
    end3_ref,
    end4_ref,
    gate_ref,
    gain_ref,
    weight_ref,
    mixed_ref,
    normed_ref,
    enter_ref,
    *partial_refs,
    heads,
    key_width,
    value_width,
    chunks,
):
    step = pl.program_id(0)

    @pl.when(step == 0)
    def _():
        for head in range(heads):
            state = end4_ref[head, :, :value_width].astype(F32)
            for end in (end3_ref, end2_ref, end1_ref):
                state = end[head, :, :value_width].astype(F32) + mm(
                    end[head, :, value_width:], state
                )
            enter_ref[head] = state.astype(BF)

    for head in range(heads):
        cols = slice(head * value_width, (head + 1) * value_width)
        mixed = local_ref[:, cols] + mm(
            carry_ref[:, head * key_width : (head + 1) * key_width], enter_ref[head]
        )
        mixed_low = mixed.astype(BF)
        mixed_ref[:, cols] = mixed_low
        mixed = mixed_low.astype(F32)
        scale = lax.rsqrt(jnp.mean(mixed * mixed, axis=1, keepdims=True) + EPSILON)
        gate = gate_ref[:, cols]
        normed = mixed * scale * gain_ref[...] * (gate * sigmoid(gate))
        normed_ref[:, cols] = normed.astype(BF)
    steps = pl.num_programs(0) // chunks
    for chunk in range(chunks):

        @pl.when(step // steps == chunk)
        def _():
            pair_parts(
                place_ref[0],
                weight_ref.shape[1],
                lambda span: mm(normed_ref[...], weight_ref[:, span]),
                *partial_refs[2 * chunk : 2 * chunk + 2],
            )


def mixer_output(
    local, carry, ends, tensor_place, pre, gain, weight, key_width, value_width, chunks
):
    rows, cols = local.shape
    heads = cols // value_width
    width = weight.shape[1] // 2
    gate_block = heads * (2 * key_width + value_width) // cols
    steps = rows // PACK // chunks
    whole = lambda shape: pl.BlockSpec(shape, lambda i, at: (0,) * len(shape))

    def part_spec(chunk):
        return pl.BlockSpec(
            (PACK, width), lambda i, at: (jnp.clip(i - chunk * steps, 0, steps - 1), 0)
        )

    outs = pl.pallas_call(
        functools.partial(
            output_kernel,
            heads=heads,
            key_width=key_width,
            value_width=value_width,
            chunks=chunks,
        ),
        grid_spec=pltpu.PrefetchScalarGridSpec(
            num_scalar_prefetch=1,
            grid=(rows // PACK,),
            in_specs=[
                pl.BlockSpec((PACK, cols), lambda i, at: (i, 0)),
                pl.BlockSpec((PACK, carry.shape[1]), lambda i, at: (i, 0)),
                whole(ends[0].shape),
                whole(ends[0].shape),
                whole(ends[0].shape),
                whole(ends[0].shape),
                pl.BlockSpec((PACK, cols), lambda i, at: (i, gate_block)),
                whole(gain.shape),
                whole((cols, weight.shape[1])),
            ],
            out_specs=[
                pl.BlockSpec((PACK, cols), lambda i, at: (i, 0)),
                pl.BlockSpec((PACK, cols), lambda i, at: (i, 0)),
                whole((heads, key_width, value_width)),
            ]
            + [part_spec(chunk) for chunk in range(chunks) for _ in range(2)],
        ),
        out_shape=[
            jax.ShapeDtypeStruct((rows, cols), BF),
            jax.ShapeDtypeStruct((rows, cols), BF),
            jax.ShapeDtypeStruct((heads, key_width, value_width), BF),
        ]
        + [jax.ShapeDtypeStruct((rows // chunks, width), BF)] * (chunks * 2),
        compiler_params=pltpu.CompilerParams(vmem_limit_bytes=VMEM_LIMIT),
        cost_estimate=cost(7),
        name="mixer_output",
    )(tensor_place, local, carry, *ends, pre, gain, weight)
    parts = outs[3:]
    return outs[0], outs[1], outs[2], [parts[c * 2 : c * 2 + 2] for c in range(chunks)]


def feed_kernel(place_ref, *refs, chunks):
    attn = refs[: 3 * chunks]
    cot_ref, token_ref, gain_ref, gate_ref, up_ref, down_ref = refs[3 * chunks : 3 * chunks + 6]
    outs = refs[3 * chunks + 6 :]
    middle_ref, hidden_ref, inner_ref, gate_grad_ref, up_grad_ref = outs[:5]
    out_refs, mid_refs = outs[5:9], outs[9 : 9 + 2 * chunks]
    whole_ref, kept_ref, sent_ref = outs[9 + 2 * chunks :]
    first = down_ref.shape[0] - inner_ref.shape[1]
    place = place_ref[0]
    chunk_now = pl.program_id(0) // (pl.num_programs(0) // chunks)
    for chunk in range(chunks):

        @pl.when(chunk_now == chunk)
        def _():
            pieces = [piece[...] for piece in attn[3 * chunk : 3 * chunk + 3]]
            pair_blocks(pieces, place, whole_ref)

    middle = token_ref[...].astype(F32) + whole_ref[...].astype(F32)
    middle_ref[...] = middle
    scale = lax.rsqrt(jnp.mean(middle * middle, axis=1, keepdims=True) + EPSILON)
    hidden = (middle * scale * gain_ref[...]).astype(BF)
    hidden_ref[...] = hidden
    many = inner_ref.shape[1]
    gate = mm(hidden, gate_ref[:, :many])
    up = mm(hidden, up_ref[:, :many])
    inner_grad = mm_nt(cot_ref[...], down_ref[first:, :])
    sig = sigmoid(gate)
    silu = gate * sig
    inner_ref[...] = (silu * up).astype(BF)
    gate_grad_ref[...] = (inner_grad * up * (sig * (1.0 + gate * (1.0 - sig)))).astype(BF)
    up_grad_ref[...] = (inner_grad * silu).astype(BF)
    features = whole_ref.shape[1]
    pair_parts(
        place,
        features,
        lambda span: mm_nt(gate_grad_ref[...], gate_ref[span, :many])
        + mm_nt(up_grad_ref[...], up_ref[span, :many]),
        kept_ref,
        sent_ref,
    )
    for chunk in range(chunks):

        @pl.when(chunk_now == chunk)
        def _():
            mid_refs[2 * chunk][...] = kept_ref[...]
            mid_refs[2 * chunk + 1][...] = sent_ref[...]

    width = features // 4
    for by in range(4):
        span = pl.ds(pl.multiple_of((place ^ by) * width, width), width)
        out_refs[by][...] = mm(inner_ref[...], down_ref[first:, span]).astype(BF)


def feed_forward(tensor_place, attn, cot, token, gain, feed, down, hidden):
    rows, features = cot.shape
    chunks = len(attn)
    width = features // 2
    steps = rows // PACK // chunks
    whole = lambda shape: pl.BlockSpec(shape, lambda i, at: (0,) * len(shape))
    rows_at = lambda size: pl.BlockSpec((PACK, size), lambda i, at: (i, 0))

    def part(chunk, size):
        return pl.BlockSpec(
            (PACK, size), lambda i, at: (jnp.clip(i - chunk * steps, 0, steps - 1), 0)
        )

    kept = [
        (features, F32),
        (features, BF),
        (hidden, BF),
        (hidden, BF),
        (hidden, BF),
    ] + [(width // 2, BF)] * 4
    outs = pl.pallas_call(
        functools.partial(feed_kernel, chunks=chunks),
        grid_spec=pltpu.PrefetchScalarGridSpec(
            num_scalar_prefetch=1,
            grid=(rows // PACK,),
            in_specs=[
                part(chunk, piece.shape[1]) for chunk in range(chunks) for piece in attn[chunk]
            ]
            + [rows_at(features)] * 2
            + [
                whole(gain.shape),
                pl.BlockSpec((features, feed.shape[1] // 2), lambda i, at: (0, 0)),
                pl.BlockSpec((features, feed.shape[1] // 2), lambda i, at: (0, 1)),
                whole(down.shape),
            ],
            out_specs=[rows_at(size) for size, _ in kept]
            + [part(chunk, width) for chunk in range(chunks) for _ in range(2)],
            scratch_shapes=[pltpu.VMEM((PACK, features), BF)]
            + [pltpu.VMEM((PACK, width), BF)] * 2,
        ),
        out_shape=[jax.ShapeDtypeStruct((rows, size), kind) for size, kind in kept]
        + [jax.ShapeDtypeStruct((rows // chunks, width), BF)] * (2 * chunks),
        compiler_params=pltpu.CompilerParams(vmem_limit_bytes=VMEM_LIMIT),
        cost_estimate=cost(20),
        name="feed_forward",
    )(tensor_place, *[piece for pieces in attn for piece in pieces], cot, token, gain, feed, feed, down)
    return outs[:9], [outs[9 + 2 * chunk : 11 + 2 * chunk] for chunk in range(chunks)]


def gate_back_kernel(
    place_ref, *refs, count, aliased, heads, key_width, value_width
):
    pieces = refs[:count]
    (
        middle_ref,
        cot_ref,
        ffn_gain_ref,
        weight_ref,
        mixed_ref,
        gate_ref,
        gain_ref,
        query_w_ref,
        states_ref,
    ) = refs[count : count + 9]
    (
        attn_grad_ref,
        mixed_grad_ref,
        gate_grad_ref,
        source_ref,
        own_ref,
        ffn_gain_grad_ref,
        gain_grad_ref,
        enter_grad_ref,
        whole_ref,
        middle_grad_ref,
    ) = refs[count + 9 + aliased :]
    inner = PACK // GROUP

    @pl.when(pl.program_id(0) == 0)
    def _():
        gain_grad_ref[...] = jnp.zeros_like(gain_grad_ref)
        ffn_gain_grad_ref[...] = jnp.zeros_like(ffn_gain_grad_ref)
        enter_grad_ref[...] = jnp.zeros_like(enter_grad_ref)

    pair_blocks([piece[...] for piece in pieces], place_ref[0], whole_ref)
    middle = middle_ref[...]
    scale_mid = lax.rsqrt(jnp.mean(middle * middle, axis=1, keepdims=True) + EPSILON)
    hidden_grad = whole_ref[...].astype(F32)
    unit_mid = middle * scale_mid
    ffn_gain_grad_ref[0:1, :] += jnp.sum(hidden_grad * unit_mid, axis=0, keepdims=True)
    scaled_mid = hidden_grad * ffn_gain_ref[...]
    along = jnp.mean(scaled_mid * unit_mid, axis=1, keepdims=True)
    middle_grad = cot_ref[...].astype(F32) + scale_mid * (scaled_mid - unit_mid * along)
    middle_grad_ref[...] = middle_grad
    width = own_ref.shape[1]
    own_ref[...] = middle_grad_ref[
        :, pl.ds(pl.multiple_of(place_ref[0] * width, width), width)
    ]
    attn_grad = middle_grad.astype(BF)
    attn_grad_ref[...] = attn_grad
    normed_grad = mm_nt(attn_grad, weight_ref[...])
    gain = gain_ref[...]
    for head in range(heads):
        cols = slice(head * value_width, (head + 1) * value_width)
        grad = normed_grad[:, cols]
        mixed = mixed_ref[:, cols].astype(F32)
        scale = lax.rsqrt(jnp.mean(mixed * mixed, axis=1, keepdims=True) + EPSILON)
        gate = gate_ref[:, cols]
        sig = sigmoid(gate)
        silu = gate * sig
        unit = mixed * scale
        scaled = grad * unit
        gate_grad_ref[:, cols] = (scaled * gain * (sig * (1.0 + gate * (1.0 - sig)))).astype(BF)
        gain_grad_ref[0:1, :] += jnp.sum(scaled * silu, axis=0, keepdims=True)
        unit_grad = grad * gain * silu
        mixed_grad = scale * (unit_grad - unit * jnp.mean(unit_grad * unit, axis=1, keepdims=True))
        mixed_grad = mixed_grad.astype(BF)
        mixed_grad_ref[:, cols] = mixed_grad
        total = enter_grad_ref[head]
        for b in range(inner):
            index = b * heads + head
            source = mm_tn(
                query_w_ref[index], mixed_grad[b * GROUP : (b + 1) * GROUP]
            )
            source_ref[index] = source
            total = total + mm_tn(states_ref[index, :, value_width:], source)
        enter_grad_ref[head] = total


def gate_back(
    chunk,
    chunks,
    tensor_place,
    pieces,
    middle,
    cot,
    ffn_gain,
    weight,
    mixed,
    pre,
    gain,
    query_w,
    states,
    before,
    key_width,
    value_width,
):
    rows, features = middle.shape
    width = pieces[0].shape[1]
    cols = mixed.shape[1]
    heads = cols // value_width
    gate_block = heads * (2 * key_width + value_width) // cols
    step = PACK // GROUP * heads
    steps = rows // PACK // chunks
    first = chunk * steps
    whole = lambda shape: pl.BlockSpec(shape, lambda i, at: (0,) * len(shape))
    rows_at = lambda size, col=0: pl.BlockSpec((PACK, size), lambda i, at: (first + i, col))
    blocks_at = lambda shape: pl.BlockSpec((step,) + shape, lambda i, at: (first + i, 0, 0))
    inputs = [*pieces, middle, cot, ffn_gain, weight, mixed, pre, gain, query_w, states]
    outs = pl.pallas_call(
        functools.partial(
            gate_back_kernel,
            count=len(pieces),
            aliased=len(before),
            heads=heads,
            key_width=key_width,
            value_width=value_width,
        ),
        grid_spec=pltpu.PrefetchScalarGridSpec(
            num_scalar_prefetch=1,
            grid=(steps,),
            in_specs=[
                pl.BlockSpec((PACK, piece.shape[1]), lambda i, at: (i, 0)) for piece in pieces
            ]
            + [
                rows_at(features),
                rows_at(features),
                whole(ffn_gain.shape),
                whole((cols, features)),
                rows_at(cols),
                rows_at(cols, gate_block),
                whole(gain.shape),
                blocks_at(query_w.shape[1:]),
                blocks_at(states.shape[1:]),
            ]
            + [pl.BlockSpec(memory_space=pl.ANY)] * len(before),
            out_specs=[
                rows_at(features),
                rows_at(cols),
                rows_at(cols),
                blocks_at((key_width, value_width)),
                rows_at(width),
                whole((8, features)),
                whole((8, value_width)),
                whole((heads, key_width, value_width)),
            ],
            scratch_shapes=[pltpu.VMEM((PACK, features), BF), pltpu.VMEM((PACK, features), F32)],
        ),
        out_shape=[
            jax.ShapeDtypeStruct((rows, features), BF),
            jax.ShapeDtypeStruct((rows, cols), BF),
            jax.ShapeDtypeStruct((rows, cols), BF),
            jax.ShapeDtypeStruct((rows // GROUP * heads, key_width, value_width), F32),
            jax.ShapeDtypeStruct((rows, width), F32),
            jax.ShapeDtypeStruct((8, features), F32),
            jax.ShapeDtypeStruct((8, value_width), F32),
            jax.ShapeDtypeStruct((heads, key_width, value_width), F32),
        ],
        input_output_aliases={1 + len(inputs) + i: i for i in range(len(before))},
        compiler_params=pltpu.CompilerParams(vmem_limit_bytes=VMEM_LIMIT),
        cost_estimate=cost(7),
        name="gate_back",
    )(tensor_place, *inputs, *before)
    return outs[:5], outs[5:]


def input_kernel(
    place_ref,
    pre_grad_ref,
    small_grad_ref,
    gate_grad_ref,
    weight_ref,
    token_ref,
    scale_ref,
    gain_ref,
    dot_ref,
    gain_grad_ref,
    rim_ref,
    part_ref,
    terms_ref,
):
    rows = gate_grad_ref.shape[0]
    wide = pre_grad_ref.shape[1]
    gate_wide = gate_grad_ref.shape[1]
    small_wide = small_grad_ref.shape[1]
    width = token_ref.shape[1]
    step = pl.program_id(0)

    @pl.when(step == 0)
    def _():
        dot_ref[...] = jnp.zeros_like(dot_ref)

    terms = mm_nt(pre_grad_ref[...], weight_ref[:, :wide])
    terms = terms + mm_nt(
        small_grad_ref[...], weight_ref[:, wide + gate_wide : wide + gate_wide + small_wide]
    )
    terms_ref[...] = terms
    terms_ref[:rows, :] += mm_nt(gate_grad_ref[...], weight_ref[:, wide : wide + gate_wide])
    rim_ref[...] = terms_ref[rows:, :]
    terms = terms_ref[...]
    product = terms * token_ref[...].astype(F32)
    dot_ref[...] += jnp.sum(product * gain_ref[...], axis=1, keepdims=True)
    total = jnp.sum(product * scale_ref[:, 0:1], axis=0, keepdims=True)
    gain_grad_ref[...] = jnp.broadcast_to(total, gain_grad_ref.shape)
    part_ref[...] = terms[:rows].astype(BF)


def input_terms(tensor_place, pre_grad, small_grad, gate_grad, weight, token, scale, gain, count):
    total, wide = pre_grad.shape
    rows, gate_wide = gate_grad.shape
    features, outs = weight.shape
    width = features // count
    whole = lambda shape: pl.BlockSpec(shape, lambda i, at: (0,) * len(shape))
    spot = lambda i, at: lax.rem(at[0] + i, count)
    found = pl.pallas_call(
        input_kernel,
        grid_spec=pltpu.PrefetchScalarGridSpec(
            num_scalar_prefetch=1,
            grid=(count,),
            in_specs=[
                whole(pre_grad.shape),
                whole(small_grad.shape),
                whole(gate_grad.shape),
                pl.BlockSpec((width, outs), lambda i, at: (spot(i, at), 0)),
                pl.BlockSpec((total, width), lambda i, at: (0, spot(i, at))),
                whole(scale.shape),
                pl.BlockSpec((1, width), lambda i, at: (0, spot(i, at))),
            ],
            out_specs=[
                whole((total, LANES)),
                pl.BlockSpec((8, width), lambda i, at: (0, spot(i, at))),
                pl.BlockSpec((RIM, width), lambda i, at: (0, spot(i, at))),
                pl.BlockSpec((rows, width), lambda i, at: (0, spot(i, at))),
            ],
            scratch_shapes=[pltpu.VMEM((total, width), F32)],
        ),
        out_shape=[
            jax.ShapeDtypeStruct((total, LANES), F32),
            jax.ShapeDtypeStruct((8, features), F32),
            jax.ShapeDtypeStruct((RIM, features), F32),
            jax.ShapeDtypeStruct((rows, features), BF),
        ],
        compiler_params=pltpu.CompilerParams(vmem_limit_bytes=VMEM_LIMIT),
        cost_estimate=cost(8),
        name="input_terms",
    )(tensor_place, pre_grad, small_grad, gate_grad, weight, token, scale, gain)
    return found


def conv_back(unit_grad, window, taps_ref, valid, first, width, factor, taps_grad_ref):
    conv, pieces = active_of(window, taps_ref, valid, first, width)
    sig = sigmoid(conv)
    act_grad = unit_grad
    if factor is not None:
        act = conv * sig
        scale = lax.rsqrt(jnp.sum(act * act, axis=1, keepdims=True) + EPSILON)
        along = jnp.sum(unit_grad * act, axis=1, keepdims=True)
        act_grad = (factor * scale) * (unit_grad - act * (scale * scale * along))
    conv_grad = act_grad * (sig * (1.0 + conv * (1.0 - sig)))
    for j in range(CONV):
        taps_grad_ref[j : j + 1, first : first + width] += jnp.sum(
            conv_grad * valid[:, j : j + 1] * pieces[j], axis=0, keepdims=True
        )
    return conv_grad


def true_kernel(
    small_ref,
    rate_ref,
    bias_ref,
    w_ref,
    u_ref,
    states_ref,
    enter_ref,
    true_ref,
    whole_ref,
    renewed_ref,
    *,
    heads,
    rows,
    key_width,
    value_width,
):
    inner = PACK // GROUP

    span = slice(0, PACK)
    decay_tile, _ = rates_of(small_ref[span, :], rate_ref[...], bias_ref[...])
    for head in range(heads):
        cols = slice(head * key_width, (head + 1) * key_width)
        value_at = slice(head * value_width, (head + 1) * value_width)
        decay = column_of(decay_tile, head)
        w = w_ref[span, cols]
        u = u_ref[span, value_at]
        renewed = []
        for b in range(inner):
            index = b * heads + head
            part = slice(b * GROUP, (b + 1) * GROUP)
            whole = jnp.exp(jnp.sum(decay[part], axis=0, keepdims=True))
            whole_ref[index] = jnp.broadcast_to(whole, (8, LANES))
            state = (
                states_ref[index, :, :value_width].astype(F32)
                + mm(states_ref[index, :, value_width:], enter_ref[head])
            ).astype(BF)
            true_ref[index] = state
            renewed.append((u[part].astype(F32) - mm(w[part], state)).astype(BF))
        renewed_ref[span, value_at] = jnp.concatenate(renewed, axis=0)


def mixer_true(pre, rate, bias, w, u, states, enter, heads, key_width, value_width):
    rows = pre.shape[0] - RIM
    wide = heads * (2 * key_width + value_width)
    gate_wide = heads * value_width
    count = rows // GROUP
    whole = lambda shape: pl.BlockSpec(shape, lambda i: (0,) * len(shape))
    outs = [
        ((count * heads, key_width, value_width), BF),
        ((count * heads, 8, LANES), F32),
        ((rows, heads * value_width), BF),
    ]
    given = [rate, bias, w, u, states, enter]
    rows_at = lambda width: pl.BlockSpec((PACK, width), lambda i: (i, 0))
    blocks_at = lambda shape: pl.BlockSpec(
        (PACK // GROUP * heads,) + shape, lambda i: (i, 0, 0)
    )
    return pl.pallas_call(
        functools.partial(
            true_kernel, heads=heads, rows=rows, key_width=key_width, value_width=value_width
        ),
        grid=(rows // PACK,),
        in_specs=[
            pl.BlockSpec((PACK, LANES), lambda i: (i, (wide + gate_wide) // LANES)),
            whole(rate.shape),
            whole(bias.shape),
            rows_at(w.shape[1]),
            rows_at(u.shape[1]),
            blocks_at(states.shape[1:]),
            whole(enter.shape),
        ],
        out_specs=[
            blocks_at((key_width, value_width)),
            blocks_at((8, LANES)),
            rows_at(heads * value_width),
        ],
        out_shape=[jax.ShapeDtypeStruct(shape, kind) for shape, kind in outs],
        compiler_params=pltpu.CompilerParams(vmem_limit_bytes=VMEM_LIMIT),
        cost_estimate=cost(6),
        name="mixer_true",
    )(pre, *given)


def ready_kernel(
    head_ref,
    pre_ref,
    small_ref,
    taps_ref,
    valid_ref,
    rate_ref,
    bias_ref,
    queries_ref,
    keys_ref,
    true_ref,
    renewed_ref,
    mixed_grad_ref,
    base_ref,
    key_part_ref,
    conv_grad_ref,
    taps_grad_ref,
    along_ref,
    *,
    heads,
    rows,
    key_width,
    value_width,
):
    inner = PACK // GROUP
    group = pl.program_id(0)

    @pl.when(group == 0)
    def _():
        taps_grad_ref[...] = jnp.zeros_like(taps_grad_ref)
    masks = pack_masks()
    row, col, apart, same, lower, strict = masks
    span = slice(0, PACK)
    valid = valid_ref[pl.ds(pl.multiple_of(group * PACK + RIM, RIM), PACK), :]
    decay_tile, _ = rates_of(small_ref[span, :], rate_ref[...], bias_ref[...])
    lane = lax.broadcasted_iota(jnp.int32, (PACK, LANES), 1)
    along = jnp.zeros((PACK, LANES), F32)
    for head in range(heads):
        cols = slice(head * key_width, (head + 1) * key_width)
        value_at = slice(head * value_width, (head + 1) * value_width)
        query = queries_ref[span, cols]
        key = keys_ref[span, cols]
        gam, last, fading = packed_decay(column_of(decay_tile, head), masks)
        scores = mm_nt(query, key) * fading
        renewed = renewed_ref[span, value_at]
        out_grad = mixed_grad_ref[span, value_at]
        grown_grad = []
        for b in range(inner):
            index = b * heads + head
            part = slice(b * GROUP, (b + 1) * GROUP)
            grown_grad.append(mm_nt(out_grad[part], true_ref[index]))
        base_ref[span, value_at] = mm_tn(scores, out_grad)
        scores_grad = jnp.where(lower, mm_nt(out_grad, renewed), 0.0)
        pair_grad = (scores_grad * fading).astype(BF)
        grown_grad = jnp.exp(gam) * jnp.concatenate(grown_grad, axis=0)
        query_grad = mm(pair_grad, key) + grown_grad
        along = jnp.where(
            lane == head,
            net_of(scores_grad * scores, apart)
            + jnp.sum(grown_grad * query.astype(F32), axis=1, keepdims=True),
            along,
        )
        key_part_ref[span, cols] = mm_tn(pair_grad, query)
        window = jnp.concatenate([head_ref[:, cols], pre_ref[:, cols]], axis=0)
        conv_grad_ref[span, cols] = conv_back(
            query_grad,
            window,
            taps_ref,
            valid,
            head * key_width,
            key_width,
            key_width ** (-0.5),
            taps_grad_ref,
        )
    along_ref[span, :] = along


def mixer_ready(
    pre,
    taps,
    valid,
    rate,
    bias,
    queries,
    keys,
    true,
    renewed,
    mixed_grad,
    heads,
    key_width,
    value_width,
):
    rows = pre.shape[0] - RIM
    wide = heads * (2 * key_width + value_width)
    gate_wide = heads * value_width
    key_cols = heads * key_width
    whole = lambda shape: pl.BlockSpec(shape, lambda i: (0,) * len(shape))
    outs = [
        ((rows, heads * value_width), F32),
        ((rows, key_cols), F32),
        ((rows, key_cols), F32),
        ((8, key_cols), F32),
        ((rows, LANES), F32),
    ]
    rows_at = lambda width: pl.BlockSpec((PACK, width), lambda i: (i, 0))
    head_at = lambda i: jnp.where(i == 0, rows // RIM, i * (PACK // RIM) - 1)
    return pl.pallas_call(
        functools.partial(
            ready_kernel, heads=heads, rows=rows, key_width=key_width, value_width=value_width
        ),
        grid=(rows // PACK,),
        in_specs=[
            pl.BlockSpec((RIM, key_cols), lambda i: (head_at(i), 0)),
            rows_at(key_cols),
            pl.BlockSpec((PACK, LANES), lambda i: (i, (wide + gate_wide) // LANES)),
            whole(taps.shape),
            whole(valid.shape),
            whole(rate.shape),
            whole(bias.shape),
            rows_at(key_cols),
            rows_at(key_cols),
            pl.BlockSpec((PACK // GROUP * heads,) + true.shape[1:], lambda i: (i, 0, 0)),
            rows_at(renewed.shape[1]),
            rows_at(mixed_grad.shape[1]),
        ],
        out_specs=[
            whole(shape) if shape[0] == 8 else rows_at(shape[1]) for shape, _ in outs
        ],
        out_shape=[jax.ShapeDtypeStruct(shape, kind) for shape, kind in outs],
        compiler_params=pltpu.CompilerParams(vmem_limit_bytes=VMEM_LIMIT),
        cost_estimate=cost(11),
        name="mixer_ready",
    )(
        pre,
        pre,
        pre,
        taps,
        valid,
        rate,
        bias,
        queries,
        keys,
        true,
        renewed,
        mixed_grad,
    )


def backward_kernel(
    keep_ref,
    head_ref,
    pre_ref,
    small_ref,
    taps_ref,
    valid_ref,
    rate_ref,
    bias_ref,
    keys_ref,
    inverse_ref,
    w_ref,
    u_ref,
    fold_ref,
    source_ref,
    true_ref,
    whole_ref,
    renewed_ref,
    base_ref,
    key_part_ref,
    query_conv_ref,
    query_taps_ref,
    along_ref,
    next1_ref,
    next2_ref,
    next3_ref,
    next4_ref,
    pre_grad_ref,
    small_grad_ref,
    taps_grad_ref,
    rate_grad_ref,
    later_ref,
    conv_grad_ref,
    flow_ref,
    *,
    heads,
    rows,
    key_width,
    value_width,
):
    groups = rows // PACK
    inner = PACK // GROUP
    key_cols = heads * key_width
    wide = heads * (2 * key_width + value_width)
    step = pl.program_id(0)

    @pl.when(step == 0)
    def _():
        taps_grad_ref[...] = jnp.zeros_like(taps_grad_ref)
        taps_grad_ref[:, :key_cols] = query_taps_ref[...]
        rate_grad_ref[...] = jnp.zeros_like(rate_grad_ref)
        conv_grad_ref[0:RIM, :] = jnp.zeros((RIM, wide), F32)
        conv_grad_ref[RIM + rows :, :] = jnp.zeros((RIM, wide), F32)
        conv_grad_ref[RIM : RIM + rows, :key_cols] = query_conv_ref[...]
        small_grad_ref[rows:, :] = jnp.zeros((RIM, LANES), BF)

        for head in range(heads):
            flow = next4_ref[head, :, :value_width].astype(F32)
            for near in (next3_ref, next2_ref, next1_ref):
                flow = near[head, :, :value_width].astype(F32) + mm_tn(
                    near[head, :, value_width:], flow
                )
            flow_ref[head] = flow
        for block in reversed(range(rows // GROUP)):
            for head in range(heads):
                index = block * heads + head
                flow = flow_ref[head]
                flow_low = flow.astype(BF)
                later_ref[index] = flow_low
                flow_ref[head] = keep_ref[block] * (
                    whole_ref[index, 0:1, 0:1] * flow
                    - mm_tn(fold_ref[index], flow_low)
                    + source_ref[index]
                )

    @pl.when(step > 0)
    def _():
        group = step - 1
        masks = pack_masks()
        row, col, apart, same, lower, strict = masks
        span = pl.ds(0, PACK)
        out_span = pl.ds(pl.multiple_of(group * PACK, PACK), PACK)
        small = small_ref[span, :]
        valid = valid_ref[pl.ds(pl.multiple_of(group * PACK + RIM, RIM), PACK), :]
        decay_tile, beta_tile = rates_of(small, rate_ref[...], bias_ref[...])
        lane = lax.broadcasted_iota(jnp.int32, (PACK, LANES), 1)
        small_rows = jnp.zeros((PACK, LANES), F32)
        for head in range(heads):
            decay = column_of(decay_tile, head)
            beta = column_of(beta_tile, heads + head)
            cols = slice(head * key_width, (head + 1) * key_width)
            value_at = slice(head * value_width, (head + 1) * value_width)
            key = keys_ref[span, cols]
            value = keys_ref[span, key_cols + head * value_width : key_cols + (head + 1) * value_width]
            key_f = key.astype(F32)
            gam, last, fading = packed_decay(decay, masks)
            growth = jnp.exp(gam)
            rest = jnp.exp(last - gam)
            gram = mm_nt(key, key)
            tail = (rest * key_f).astype(BF)
            w = w_ref[span, cols]
            u = u_ref[span, value_at]
            renewed = renewed_ref[span, value_at]
            renewed_grad, drops = [], []
            for b in range(inner):
                index = (group * inner + b) * heads + head
                near = b * heads + head
                flow = later_ref[index]
                renewed_grad.append(mm(tail[b * GROUP : (b + 1) * GROUP], flow))
                shared = true_ref[near].astype(F32) * flow.astype(F32)
                shared = jnp.sum(jnp.sum(shared, axis=1, keepdims=True), axis=0, keepdims=True)
                drops.append(
                    jnp.broadcast_to(shared * whole_ref[index, 0:1, 0:1], (GROUP, 1))
                )
            renewed_low = (base_ref[span, value_at] + jnp.concatenate(renewed_grad, axis=0)).astype(
                BF
            )
            tail_grad, w_grad = [], []
            for b in range(inner):
                index = (group * inner + b) * heads + head
                part = slice(b * GROUP, (b + 1) * GROUP)
                tail_grad.append(mm_nt(renewed[part], later_ref[index]))
                w_grad.append(mm_nt(renewed_low[part], true_ref[b * heads + head]))
            tail_grad = jnp.concatenate(tail_grad, axis=0)
            w_grad = -jnp.concatenate(w_grad, axis=0)
            inverse = inverse_ref[head]
            keys_grad = mm_tn(inverse, w_grad)
            values_grad = mm_tn(inverse, renewed_low)
            system_grad = jnp.where(strict, -(mm_nt(keys_grad, w) + mm_nt(values_grad, u)), 0.0)
            gram_beta = system_grad * fading
            gram_grad = (gram_beta * beta).astype(BF)
            key_grad = (
                mm(gram_grad, key)
                + mm_tn(gram_grad, key)
                + key_part_ref[span, cols]
                + beta * growth * keys_grad
                + rest * tail_grad
            )
            value_grad = beta * values_grad
            keys_dot = growth * jnp.sum(keys_grad * key_f, axis=1, keepdims=True)
            beta_grad = (
                keys_dot
                + jnp.sum(values_grad * value.astype(F32), axis=1, keepdims=True)
                + jnp.sum(gram_beta * gram, axis=1, keepdims=True)
            )
            tail_dot = rest * jnp.sum(tail_grad * key_f, axis=1, keepdims=True)
            system = jnp.where(strict, fading * beta * gram, 0.0)
            gam_grad = (
                along_ref[span, head : head + 1]
                + beta * keys_dot
                + net_of(system_grad * system, apart)
            )
            gam_grad_row = jnp.sum(
                jnp.where(apart == 0, jnp.broadcast_to(gam_grad, (PACK, PACK)), 0.0),
                axis=0,
                keepdims=True,
            )
            tail_row = jnp.sum(
                jnp.where(apart == 0, jnp.broadcast_to(tail_dot, (PACK, PACK)), 0.0),
                axis=0,
                keepdims=True,
            )
            decay_grad = jnp.sum(
                jnp.where(same, jnp.where(col >= row, gam_grad_row, tail_row), 0.0),
                axis=1,
                keepdims=True,
            ) + jnp.concatenate(drops, axis=0)
            small_rows = jnp.where(lane == head, decay_grad, small_rows)
            small_rows = jnp.where(lane == heads + head, beta_grad, small_rows)

            for first, width, unit_grad, factor in (
                (key_cols + head * key_width, key_width, key_grad, 1.0),
                (2 * key_cols + head * value_width, value_width, value_grad, None),
            ):
                window = jnp.concatenate(
                    [head_ref[:, first : first + width], pre_ref[:, first : first + width]], axis=0
                )
                conv_grad_ref[
                    pl.ds(pl.multiple_of(group * PACK + RIM, RIM), PACK), first : first + width
                ] = conv_back(
                    unit_grad, window, taps_ref, valid, first, width, factor, taps_grad_ref
                )

        raw = small + bias_ref[...]
        slope = -jnp.exp(rate_ref[...]) * sigmoid(raw)
        small_grad = jnp.where(
            lane < heads, small_rows * slope, small_rows * beta_tile * (1.0 - beta_tile)
        )
        small_grad = jnp.where(lane < 2 * heads, small_grad, 0.0)
        small_grad_ref[out_span, :] = small_grad.astype(BF)
        rate_grad_ref[0:1, :] += jnp.sum(small_rows * decay_tile, axis=0, keepdims=True)
        rate_grad_ref[1:2, :] += jnp.sum(small_grad, axis=0, keepdims=True)

    def convolve_back(start, target, count, first):
        cols = slice(first, first + LANES)
        window = conv_grad_ref[pl.ds(start, count + RIM), cols]
        flags = valid_ref[pl.ds(start, count + RIM), :]
        total = None
        for j in range(CONV):
            term = window * (flags[:, j : j + 1] * taps_ref[j : j + 1, cols])
            shift = CONV - 1 - j
            if shift:
                term = pltpu.roll(term, count + RIM - shift, 0)
            total = term if total is None else total + term
        pre_grad_ref[pl.ds(target, count), cols] = total[:count].astype(BF)

    @pl.when(step == groups)
    def _():
        def spread(group, _):
            base = pl.multiple_of(group * PACK, PACK)
            for first in range(0, wide, LANES):
                convolve_back(pl.multiple_of(base + RIM, RIM), base, PACK, first)
            return 0

        lax.fori_loop(0, groups, spread, 0)
        for first in range(0, wide, LANES):
            convolve_back(0, rows, RIM, first)


def mixer_backward(
    keep,
    pre,
    taps,
    valid,
    rate,
    bias,
    keys,
    inverse,
    w,
    u,
    fold,
    source,
    found,
    nexts,
    heads,
    key_width,
    value_width,
):
    rows = pre.shape[0] - RIM
    wide = heads * (2 * key_width + value_width)
    gate_wide = heads * value_width
    count = rows // GROUP
    whole = lambda shape: pl.BlockSpec(shape, lambda i: (0,) * len(shape))
    outs = [
        ((rows + RIM, wide), BF),
        ((rows + RIM, LANES), BF),
        ((8, wide), F32),
        ((8, LANES), F32),
    ]
    groups = rows // PACK
    step = PACK // GROUP * heads
    at = lambda i: jnp.maximum(i - 1, 0)
    rows_at = lambda width: pl.BlockSpec((PACK, width), lambda i: (at(i), 0))
    blocks_at = lambda many, shape: pl.BlockSpec((many,) + shape, lambda i: (at(i), 0, 0))
    true, whole_decays, renewed, base, key_part, query_conv, query_taps, along = found
    head_at = lambda i: jnp.where(at(i) == 0, rows // RIM, at(i) * (PACK // RIM) - 1)
    return pl.pallas_call(
        functools.partial(
            backward_kernel, heads=heads, rows=rows, key_width=key_width, value_width=value_width
        ),
        grid=(groups + 1,),
        in_specs=[
            pl.BlockSpec(memory_space=pltpu.SMEM),
            pl.BlockSpec((RIM, wide), lambda i: (head_at(i), 0)),
            rows_at(wide),
            pl.BlockSpec((PACK, LANES), lambda i: (at(i), (wide + gate_wide) // LANES)),
            whole(taps.shape),
            whole(valid.shape),
            whole(rate.shape),
            whole(bias.shape),
            rows_at(keys.shape[1]),
            blocks_at(heads, inverse.shape[1:]),
            rows_at(w.shape[1]),
            rows_at(u.shape[1]),
            whole(fold.shape),
            whole(source.shape),
            blocks_at(step, true.shape[1:]),
            whole(whole_decays.shape),
            rows_at(renewed.shape[1]),
            rows_at(base.shape[1]),
            rows_at(key_part.shape[1]),
            whole(query_conv.shape),
            whole(query_taps.shape),
            rows_at(along.shape[1]),
        ]
        + [whole(near.shape) for near in nexts],
        out_specs=[whole(shape) for shape, _ in outs],
        out_shape=[jax.ShapeDtypeStruct(shape, kind) for shape, kind in outs],
        scratch_shapes=[
            pltpu.VMEM((count * heads, key_width, value_width), BF),
            pltpu.VMEM((rows + 2 * RIM, wide), F32),
            pltpu.VMEM((heads, key_width, value_width), F32),
        ],
        compiler_params=pltpu.CompilerParams(vmem_limit_bytes=VMEM_LIMIT),
        cost_estimate=cost(25),
        name="mixer_backward",
    )(keep, pre, pre, pre, taps, valid, rate, bias, keys, inverse, w, u, fold, source, *found, *nexts)


def spread_into(piece, whole_shape, start, axis_number):
    return lax.dynamic_update_slice_in_dim(jnp.zeros(whole_shape, F32), piece, start, axis_number)


def lane_row(values):
    return jnp.pad(values, (0, LANES - values.shape[0]))[None, :]


def per_device(
    tokens,
    cotangent,
    lengths,
    norm_gain,
    query_weight,
    key_weight,
    value_weight,
    outgate_weight,
    alpha_weight,
    beta_weight,
    output_weight,
    conv_query,
    conv_key,
    conv_value,
    log_rate,
    step_bias,
    out_gain,
    ffn_gain,
    gate_weight,
    up_weight,
    down_weight,
):
    rows, slice_width = tokens.shape
    count = lax.axis_size("tensor")
    full_width = slice_width * count
    tensor_place = lax.axis_index("tensor")
    tensor_array = tensor_place.astype(jnp.int32)[None]
    place = lax.axis_index(FH)
    key_cols = query_weight.shape[1]
    value_cols = value_weight.shape[1]
    heads = alpha_weight.shape[1]
    key_width = key_cols // heads
    value_width = value_cols // heads
    wide = 2 * key_cols + value_cols
    reach = LONGEST // rows

    rim_slice = shifted(tokens[rows - RIM :], FH, 1)
    token_pieces = rotations(jnp.concatenate([tokens, rim_slice], axis=0), "tensor")
    small_shard = jnp.pad(
        jnp.concatenate([alpha_weight, beta_weight], axis=1), ((0, 0), (0, 2 * LANES - 2 * heads))
    )
    in_full = weight_rows(
        jnp.concatenate(
            [query_weight, key_weight, value_weight, outgate_weight, small_shard], axis=1
        ),
        0,
    )
    hidden = gate_weight.shape[1]
    room = ((0, 0), (0, padded(hidden) - hidden))
    down_full = weight_rows(jnp.concatenate([output_weight, down_weight], axis=0), 1)
    feed_full = weight_rows(
        jnp.concatenate([jnp.pad(gate_weight, room), jnp.pad(up_weight, room)], axis=1), 0
    )

    starts = jnp.cumsum(lengths) - lengths
    places = place * rows + jnp.arange(rows, dtype=jnp.int32)
    latest = jnp.max(jnp.where(starts[None, :] <= places[:, None], starts[None, :], 0), axis=1)
    tap_index = jnp.arange(8, dtype=jnp.int32)
    valid = ((places - latest)[:, None] >= CONV - 1 - tap_index[None, :]).astype(F32)
    valid_padded = jnp.pad(valid, ((RIM, RIM), (0, 0)))
    block_first = place * rows + jnp.arange(rows // GROUP, dtype=jnp.int32) * GROUP
    keep = 1.0 - jnp.any(block_first[:, None] == starts[None, :], axis=1).astype(F32)
    taps = jnp.concatenate(
        [
            lax.dynamic_slice_in_dim(conv_query, tensor_place * key_cols, key_cols, 1),
            lax.dynamic_slice_in_dim(conv_key, tensor_place * key_cols, key_cols, 1),
            lax.dynamic_slice_in_dim(conv_value, tensor_place * value_cols, value_cols, 1),
        ],
        axis=1,
    )
    rate = lane_row(lax.dynamic_slice_in_dim(log_rate, tensor_place * heads, heads))
    bias = lane_row(lax.dynamic_slice_in_dim(step_bias, tensor_place * heads, heads))
    gain_row = out_gain[None, :]
    norm_row = norm_gain[None, :]
    ffn_row = ffn_gain[None, :]

    token_rows, hidden_in, scale_in, pre = project(
        tensor_array, token_pieces, norm_row, in_full
    )
    cot_held, *_ = lax.optimization_barrier(
        (cotangent, down_full, feed_full, valid, keep, taps, rate, bias, *token_pieces[1:])
    )
    cot_rows = lax.all_gather(cot_held, "tensor", axis=1, tiled=True)

    keys, inverse, w, u, fold, states, end = mixer_forward(
        pre, keep, taps, valid, rate, bias, heads, key_width, value_width
    )
    queries, query_w, local, carry = mixer_query(
        pre, taps, valid, rate, bias, keys, w, u, states, heads, key_width, value_width
    )
    ends = [shifted(end, FH, by) for by in range(1, reach + 1)]
    ends[0], cot_rows = lax.optimization_barrier((ends[0], cot_rows))
    mixed, normed, enter, attn_parts = mixer_output(
        local,
        carry,
        ends,
        tensor_array,
        pre,
        gain_row,
        down_full,
        key_width,
        value_width,
        CHUNKS,
    )

    settled = mixer_true(pre, rate, bias, w, u, states, enter, heads, key_width, value_width)
    halves = [
        pair_half(*parts, settled if chunk == 0 else None) for chunk, parts in enumerate(attn_parts)
    ]
    attn_chunks = [pair_gather(pair_rest(*half).astype(BF)) for half in halves]
    true, whole_decays, renewed = settled
    kept, mid_parts = feed_forward(
        tensor_array, attn_chunks, cot_rows, token_rows, ffn_row, feed_full, down_full, hidden
    )
    middle, hidden_mid, inner_act, gate_grad, up_grad, *out_parts = kept
    back_kept, sums = (), []
    feed_local = weight_grads(
        (hidden_mid, gate_grad), (hidden_mid, up_grad), (cot_rows, inner_act)
    )
    halves = [
        pair_half(*parts, feed_local if chunk == 0 else None)
        for chunk, parts in enumerate(mid_parts)
    ]
    mid_chunks = [pair_gather(pair_rest(*half).astype(BF)) for half in halves]
    feed_grads = owners(feed_local)
    for chunk in range(CHUNKS):
        back_kept, found = gate_back(
            chunk,
            CHUNKS,
            tensor_array,
            mid_chunks[chunk],
            middle,
            cot_rows,
            ffn_row,
            down_full,
            mixed,
            pre,
            gain_row,
            query_w,
            states,
            back_kept,
            key_width,
            value_width,
        )
        sums.append(found)
    attn_grad, mixed_grad, outgate_grad, source, middle_grad_own = back_kept
    ffn_gain_grad, out_gain_grad, enter_grad = [sum(group[1:], group[0]) for group in zip(*sums)]

    enter_low = jnp.concatenate([enter_grad.astype(BF), end[:, :, value_width:]], axis=2)
    nexts = [shifted(enter_low, FH, -by) for by in range(1, reach + 1)]
    attn_held, feed_grads = lax.optimization_barrier((attn_grad, feed_grads))
    out_local = weight_grads((attn_held, normed), (hidden_in, outgate_grad))
    out_sums = lax.psum_scatter(out_local, FH, scatter_dimension=0, tiled=True)
    mixed_held, out_held = lax.optimization_barrier((mixed_grad, out_parts, out_local))[:2]
    found = mixer_ready(
        pre,
        taps,
        valid_padded,
        rate,
        bias,
        queries,
        keys,
        true,
        renewed,
        mixed_held,
        heads,
        key_width,
        value_width,
    )
    found = [true, whole_decays, renewed, *found]
    output_terms = out_held[0].astype(F32)
    for by in (1, 2, 3):
        output_terms = output_terms + paired(out_held[by], by).astype(F32)
    middle_own = lax.dynamic_slice_in_dim(middle, tensor_place * slice_width, slice_width, 1)
    output_rows = (middle_own + output_terms).astype(BF)
    pre_grad, small_grad, taps_grad, rate_grad = mixer_backward(
        keep,
        pre,
        taps,
        valid_padded,
        rate,
        bias,
        keys,
        inverse,
        w,
        u,
        fold,
        source,
        found,
        nexts,
        heads,
        key_width,
        value_width,
    )

    in_dot, norm_gain_grad, rim_terms, in_part = input_terms(
        tensor_array, pre_grad, small_grad, outgate_grad, in_full, token_rows, scale_in, norm_row, count
    )
    out_grads = out_sums.astype(F32)
    in_grad = lax.psum_scatter(in_part, "tensor", scatter_dimension=1, tiled=True).astype(F32)
    late_local = weight_grads((hidden_in, pre_grad), (hidden_in, small_grad))
    late_half, late_grads = owners_by_steps(late_local)
    rim = shifted(jnp.concatenate([rim_terms, in_dot[rows:]], axis=1), FH, -1)
    in_dot = in_dot[:rows, 0] + jnp.pad(rim[:, full_width], (rows - RIM, 0))
    rim_blocks = [
        lax.dynamic_slice_in_dim(
            rim, lax.rem(tensor_place + by, count) * slice_width, slice_width, 1
        ).reshape(-1)
        for by in range(count)
    ]

    own_gain_grad = lax.dynamic_slice_in_dim(
        ffn_gain_grad[0], tensor_place * slice_width, slice_width
    )
    pieces = (
        spread_into(taps_grad[:CONV, :key_cols], conv_query.shape, tensor_place * key_cols, 1),
        spread_into(
            taps_grad[:CONV, key_cols : 2 * key_cols], conv_key.shape, tensor_place * key_cols, 1
        ),
        spread_into(
            taps_grad[:CONV, 2 * key_cols :], conv_value.shape, tensor_place * value_cols, 1
        ),
        out_gain_grad[0],
        norm_gain_grad[0],
        spread_into(own_gain_grad, ffn_gain.shape, tensor_place * slice_width, 0),
        spread_into(rate_grad[0, :heads], log_rate.shape, tensor_place * heads, 0),
        spread_into(rate_grad[1, :heads], step_bias.shape, tensor_place * heads, 0),
    )
    flat = jnp.concatenate([piece.reshape(-1) for piece in pieces])
    flat = jnp.pad(flat, (0, -flat.size % (8 * LANES))).reshape(-1, LANES)
    flat = lax.optimization_barrier((flat, late_half))[0]
    flat = total_batches(flat).reshape(-1)
    joined = scattered(
        [jnp.concatenate([flat, in_dot, block]).reshape(-1, LANES) for block in rim_blocks], "tensor"
    ).reshape(-1)
    small, at = [], 0
    for piece in pieces:
        small.append(joined[at : at + piece.size].reshape(piece.shape))
        at += piece.size
    in_dot = joined[flat.size : flat.size + rows]
    rim_grad = joined[flat.size + rows :].reshape(RIM, slice_width)

    norm_slice = lax.dynamic_slice_in_dim(norm_gain, tensor_place * slice_width, slice_width)
    in_grad = in_grad + jnp.pad(rim_grad, ((rows - RIM, 0), (0, 0)))
    scale = scale_in[:rows, :1]
    tokens_grad = (
        middle_grad_own
        + scale * (in_grad * norm_slice)
        - tokens.astype(F32) * (scale * scale * scale * in_dot[:, None] / full_width)
    )

    return (
        output_rows,
        tokens_grad,
        late_grads[:, :key_cols],
        late_grads[:, key_cols : 2 * key_cols],
        late_grads[:, 2 * key_cols : wide],
        out_grads[:, value_cols:],
        late_grads[:, wide : wide + heads],
        late_grads[:, wide + heads : wide + 2 * heads],
        out_grads[:, :value_cols].T,
        feed_grads[:, :hidden],
        feed_grads[:, padded(hidden) : padded(hidden) + hidden],
        feed_grads[:, 2 * padded(hidden) : 2 * padded(hidden) + hidden].T,
        small[0],
        small[1],
        small[2],
        small[6],
        small[7],
        small[3],
        small[4],
        small[5],
    )


def solution(mesh):
    in_specs = (
        P(FH, "tensor"),
        P(FH, "tensor"),
        P(),
        P(),
        P("fsdp", "tensor"),
        P("fsdp", "tensor"),
        P("fsdp", "tensor"),
        P("fsdp", "tensor"),
        P("fsdp", "tensor"),
        P("fsdp", "tensor"),
        P("tensor", "fsdp"),
        P(),
        P(),
        P(),
        P(),
        P(),
        P(),
        P(),
        P("fsdp", "tensor"),
        P("fsdp", "tensor"),
        P("tensor", "fsdp"),
    )
    out_specs = (
        P(FH, "tensor"),
        P(FH, "tensor"),
        P(FH, "tensor"),
        P(FH, "tensor"),
        P(FH, "tensor"),
        P(FH, "tensor"),
        P(FH, "tensor"),
        P(FH, "tensor"),
        P("tensor", FH),
        P(FH, "tensor"),
        P(FH, "tensor"),
        P("tensor", FH),
        P(),
        P(),
        P(),
        P(),
        P(),
        P(),
        P(),
        P(),
    )
    return jax.shard_map(
        per_device, mesh=mesh, in_specs=in_specs, out_specs=out_specs, check_vma=False
    )
```

```python
import functools

import jax
import jax.numpy as jnp
from jax import lax
from jax.experimental import pallas as pl
from jax.experimental.pallas import tpu as pltpu
from jax.sharding import PartitionSpec as P

CONV = 4
GROUP = 64
RIM = 16
PACK = 256
LANES = 128
LONGEST = 4096
EPSILON = 1e-06
FH = ("fsdp", "heads")
ALL = ("fsdp", "heads", "tensor")
BF = jnp.bfloat16
F32 = jnp.float32
VMEM_LIMIT = 56 * 1024 * 1024
INVERSE_PASSES = 1
CHUNKS = 2
SIDES = 4


def cost(micros):
    return pl.CostEstimate(flops=int(micros * 1e9), bytes_accessed=int(micros * 3e6), transcendentals=0)


def shifted(shard, axis, by):
    devices = lax.axis_size(axis)
    pairs = [(i, i + by) for i in range(devices) if 0 <= i + by < devices]
    return lax.ppermute(shard, axis, pairs)


def dot_on(left, right, left_dim, right_dim):
    return lax.dot_general(
        left.astype(BF),
        right.astype(BF),
        (((left_dim,), (right_dim,)), ((), ())),
        preferred_element_type=F32,
    )


def mm(left, right):
    return dot_on(left, right, 1, 0)


def mm_tn(left, right):
    return dot_on(left, right, 0, 0)


def mm_nt(left, right):
    return dot_on(left, right, 1, 1)


def mm_fine(left, right):
    if INVERSE_PASSES == 1:
        return mm(left, right)
    left_high, right_high = left.astype(BF), right.astype(BF)
    left_low = left - left_high.astype(F32)
    right_low = right - right_high.astype(F32)
    return mm(left_high, right_high) + mm(left_low, right_high) + mm(left_high, right_low)


def sigmoid(value):
    return 1.0 / (1.0 + jnp.exp(-value))


def softplus(value):
    return jnp.maximum(value, 0.0) + jnp.log(1.0 + jnp.exp(-jnp.abs(value)))


def window_taps(window, rows):
    total = window.shape[0]
    return [pltpu.roll(window, total - (RIM - CONV + 1 + j), 0)[:rows] for j in range(CONV)]


def pack_masks():
    row = lax.broadcasted_iota(jnp.int32, (PACK, PACK), 0)
    col = lax.broadcasted_iota(jnp.int32, (PACK, PACK), 1)
    apart = row ^ col
    same = apart < GROUP
    return row, col, apart, same, same & (row >= col), same & (row > col)


def packed_decay(decay, masks):
    row, col, apart, same, lower, strict = masks
    spread = jnp.broadcast_to(decay, (PACK, PACK))
    decay_row = jnp.sum(jnp.where(apart == 0, spread, 0.0), axis=0, keepdims=True)
    gam_row = jnp.sum(jnp.where(same & (row <= col), spread, 0.0), axis=0, keepdims=True)
    spread_row = jnp.broadcast_to(decay_row, (PACK, PACK))
    gam = jnp.sum(jnp.where(lower, spread_row, 0.0), axis=1, keepdims=True)
    last = jnp.sum(jnp.where(same, spread_row, 0.0), axis=1, keepdims=True)
    fading = jnp.where(lower, jnp.exp(jnp.where(lower, gam - gam_row, 0.0)), 0.0)
    return gam, last, fading


def rates_of(small, rate, bias):
    decay_tile = -jnp.exp(rate) * softplus(small + bias)
    return decay_tile, sigmoid(small)


def load_window(pre_ref, group, first, width, rows):
    start = group * PACK
    before = jnp.where(group == 0, rows, start - RIM)
    head = pre_ref[pl.ds(pl.multiple_of(before, RIM), RIM), first : first + width]
    body = pre_ref[pl.ds(pl.multiple_of(start, PACK), PACK), first : first + width]
    return jnp.concatenate([head, body], axis=0)


def active_of(window, taps_ref, valid, first, width):
    pieces = window_taps(window, PACK)
    conv = None
    for j in range(CONV):
        term = pieces[j] * taps_ref[j : j + 1, first : first + width] * valid[:, j : j + 1]
        conv = term if conv is None else conv + term
    return conv, pieces


def net_of(changes, apart):
    column = jnp.sum(changes, axis=0, keepdims=True)
    column = jnp.where(apart == 0, jnp.broadcast_to(column, changes.shape), 0.0)
    return jnp.sum(changes - column, axis=1, keepdims=True)


def column_of(tile, lane):
    return tile[:, lane : lane + 1].astype(BF).astype(F32)


def forward_kernel(
    keep_ref,
    pre_ref,
    small_ref,
    taps_ref,
    valid_ref,
    rate_ref,
    bias_ref,
    keys_ref,
    inverse_ref,
    w_ref,
    u_ref,
    fold_ref,
    states_ref,
    ends_ref,
    fresh_ref,
    last_ref,
    joint_ref,
    *,
    heads,
    rows,
    key_width,
    value_width,
):
    groups = rows // PACK
    inner = PACK // GROUP
    key_cols = heads * key_width

    def solve(step, _):
        masks = pack_masks()
        row, col, apart, same, lower, strict = masks
        items = []
        for side in range(SIDES):
            group = step * SIDES + side
            span = pl.ds(pl.multiple_of(group * PACK, PACK), PACK)
            valid = valid_ref[span, :]
            decay_tile, beta_tile = rates_of(small_ref[span, :], rate_ref[...], bias_ref[...])
            for head in range(heads):
                decay = column_of(decay_tile, head)
                beta = column_of(beta_tile, heads + head)
                first = key_cols + head * key_width
                window = load_window(pre_ref, group, first, key_width, rows)
                conv, _ = active_of(window, taps_ref, valid, first, key_width)
                act = conv * sigmoid(conv)
                scale = lax.rsqrt(jnp.sum(act * act, axis=1, keepdims=True) + EPSILON)
                key = (act * scale).astype(BF)
                gam, last, fading = packed_decay(decay, masks)
                gram = mm_nt(key, key)
                system = jnp.where(strict, fading * beta * gram, 0.0)
                inverse = jnp.where(apart == 0, 1.0, 0.0) - jnp.where(apart == 1, system, 0.0)
                items.append([beta, key, gam, last, system, inverse, group, span, valid, head])
        level = 1
        while (1 << level) < GROUP:
            parts = [
                mm_fine(jnp.where((apart >> level) == 1, item[4], 0.0), item[5]) for item in items
            ]
            steps = [mm_fine(item[5], part) for item, part in zip(items, parts)]
            for item, step_of in zip(items, steps):
                item[5] = item[5] - step_of
            level += 1
        for beta, key, gam, last, system, inverse, group, span, valid, head in items:
            keys_ref[span, head * key_width : (head + 1) * key_width] = key
            cols = slice(head * value_width, (head + 1) * value_width)
            first = 2 * key_cols + head * value_width
            window = load_window(pre_ref, group, first, value_width, rows)
            conv, _ = active_of(window, taps_ref, valid, first, value_width)
            value = (conv * sigmoid(conv)).astype(BF)
            keys_ref[span, key_cols + head * value_width : key_cols + (head + 1) * value_width] = (
                value
            )
            key_f = key.astype(F32)
            inverse_low = inverse.astype(BF)
            inverse_ref[group * heads + head] = inverse_low
            w_low = mm(inverse_low, beta * jnp.exp(gam) * key_f).astype(BF)
            u_low = mm(inverse_low, beta * value.astype(F32)).astype(BF)
            w_ref[span, head * key_width : (head + 1) * key_width] = w_low
            u_ref[span, cols] = u_low
            tail = jnp.exp(last - gam) * key_f
            block_of = lax.broadcasted_iota(jnp.int32, (PACK, 1), 0) // GROUP
            whole = jnp.exp(last)
            for b in range(inner):
                index = (group * inner + b) * heads + head
                tail_b = jnp.where(block_of == b, tail, 0.0).astype(BF)
                fold_ref[index] = mm_tn(tail_b, w_low).astype(BF)
                fresh_ref[index] = mm_tn(tail_b, u_low)
                last_ref[index] = jnp.broadcast_to(
                    whole[b * GROUP : b * GROUP + 1], (8, LANES)
                )
        return 0

    lax.fori_loop(0, groups // SIDES, solve, 0)

    unit = jnp.where(
        lax.broadcasted_iota(jnp.int32, (key_width, key_width), 0)
        == lax.broadcasted_iota(jnp.int32, (key_width, key_width), 1),
        1.0,
        0.0,
    )
    for head in range(heads):
        joint_ref[head, :, :value_width] = jnp.zeros((key_width, value_width), F32)
        joint_ref[head, :, value_width:] = unit
    for block in range(rows // GROUP):
        for head in range(heads):
            index = block * heads + head
            joint = joint_ref[head] * keep_ref[block]
            joint_low = joint.astype(BF)
            states_ref[index] = joint_low
            fresh = last_ref[index, 0:1, 0:1] * joint - mm(fold_ref[index], joint_low)
            joint_ref[head, :, :value_width] = fresh[:, :value_width] + fresh_ref[index]
            joint_ref[head, :, value_width:] = fresh[:, value_width:]
    ends_ref[...] = joint_ref[...].astype(BF)


def mixer_forward(pre, keep, taps, valid, rate, bias, heads, key_width, value_width):
    rows = pre.shape[0] - RIM
    wide = heads * (2 * key_width + value_width)
    gate_wide = heads * value_width
    count = rows // GROUP
    packs = rows // PACK
    joint_width = key_width + value_width
    whole = lambda shape: pl.BlockSpec(shape, lambda i: (0,) * len(shape))
    outs = [
        ((rows, wide - heads * key_width), BF),
        ((packs * heads, PACK, PACK), BF),
        ((rows, heads * key_width), BF),
        ((rows, heads * value_width), BF),
        ((count * heads, key_width, key_width), BF),
        ((count * heads, key_width, joint_width), BF),
        ((heads, key_width, joint_width), BF),
    ]
    return pl.pallas_call(
        functools.partial(
            forward_kernel, heads=heads, rows=rows, key_width=key_width, value_width=value_width
        ),
        grid=(1,),
        in_specs=[
            pl.BlockSpec(memory_space=pltpu.SMEM),
            pl.BlockSpec((rows + RIM, wide), lambda i: (0, 0)),
            pl.BlockSpec((rows + RIM, LANES), lambda i: (0, (wide + gate_wide) // LANES)),
            whole(taps.shape),
            whole(valid.shape),
            whole(rate.shape),
            whole(bias.shape),
        ],
        out_specs=[whole(shape) for shape, _ in outs],
        out_shape=[jax.ShapeDtypeStruct(shape, kind) for shape, kind in outs],
        scratch_shapes=[
            pltpu.VMEM((count * heads, key_width, value_width), F32),
            pltpu.VMEM((count * heads, 8, LANES), F32),
            pltpu.VMEM((heads, key_width, joint_width), F32),
        ],
        compiler_params=pltpu.CompilerParams(vmem_limit_bytes=VMEM_LIMIT),
        cost_estimate=cost(20),
        name="mixer_forward",
    )(keep, pre, pre, taps, valid, rate, bias)


def query_kernel(
    head_ref,
    pre_ref,
    small_ref,
    taps_ref,
    valid_ref,
    rate_ref,
    bias_ref,
    keys_ref,
    w_ref,
    u_ref,
    states_ref,
    queries_ref,
    query_w_ref,
    local_ref,
    carry_ref,
    *,
    heads,
    rows,
    key_width,
    value_width,
):
    inner = PACK // GROUP

    masks = pack_masks()
    span = slice(0, PACK)
    valid = valid_ref[span, :]
    decay_tile, _ = rates_of(small_ref[span, :], rate_ref[...], bias_ref[...])
    for head in range(heads):
        cols = slice(head * key_width, (head + 1) * key_width)
        value_at = slice(head * value_width, (head + 1) * value_width)
        window = jnp.concatenate([head_ref[:, cols], pre_ref[:, cols]], axis=0)
        conv, _ = active_of(window, taps_ref, valid, head * key_width, key_width)
        act = conv * sigmoid(conv)
        scale = lax.rsqrt(jnp.sum(act * act, axis=1, keepdims=True) + EPSILON)
        query = (act * (scale * key_width ** (-0.5))).astype(BF)
        queries_ref[span, cols] = query
        gam, last, fading = packed_decay(column_of(decay_tile, head), masks)
        scores = (mm_nt(query, keys_ref[span, cols]) * fading).astype(BF)
        query_w = (
            jnp.exp(gam) * query.astype(F32) - mm(scores, w_ref[span, cols])
        ).astype(BF)
        start = mm(scores, u_ref[span, value_at])
        local, carry = [], []
        for b in range(inner):
            index = b * heads + head
            part = slice(b * GROUP, (b + 1) * GROUP)
            query_w_ref[index] = query_w[part]
            moved = mm(query_w[part], states_ref[index])
            local.append(moved[:, :value_width])
            carry.append(moved[:, value_width:])
        local_ref[span, value_at] = start + jnp.concatenate(local, axis=0)
        carry_ref[span, cols] = jnp.concatenate(carry, axis=0).astype(BF)


def mixer_query(pre, taps, valid, rate, bias, keys, w, u, states, heads, key_width, value_width):
    rows = pre.shape[0] - RIM
    wide = heads * (2 * key_width + value_width)
    gate_wide = heads * value_width
    whole = lambda shape: pl.BlockSpec(shape, lambda i: (0,) * len(shape))
    outs = [
        ((rows, heads * key_width), BF),
        ((rows // GROUP * heads, GROUP, key_width), BF),
        ((rows, heads * value_width), F32),
        ((rows, heads * key_width), BF),
    ]
    rows_at = lambda width: pl.BlockSpec((PACK, width), lambda i: (i, 0))
    blocks_at = lambda shape: pl.BlockSpec(
        (PACK // GROUP * heads,) + shape, lambda i: (i, 0, 0)
    )
    head_at = lambda i: jnp.where(i == 0, rows // RIM, i * (PACK // RIM) - 1)
    return pl.pallas_call(
        functools.partial(
            query_kernel, heads=heads, rows=rows, key_width=key_width, value_width=value_width
        ),
        grid=(rows // PACK,),
        in_specs=[
            pl.BlockSpec((RIM, heads * key_width), lambda i: (head_at(i), 0)),
            rows_at(heads * key_width),
            pl.BlockSpec((PACK, LANES), lambda i: (i, (wide + gate_wide) // LANES)),
            whole(taps.shape),
            rows_at(valid.shape[1]),
            whole(rate.shape),
            whole(bias.shape),
            rows_at(heads * key_width),
            rows_at(w.shape[1]),
            rows_at(u.shape[1]),
            blocks_at(states.shape[1:]),
        ],
        out_specs=[
            blocks_at(shape[1:]) if len(shape) == 3 else rows_at(shape[1]) for shape, _ in outs
        ],
        out_shape=[jax.ShapeDtypeStruct(shape, kind) for shape, kind in outs],
        compiler_params=pltpu.CompilerParams(vmem_limit_bytes=VMEM_LIMIT),
        cost_estimate=cost(10),
        name="mixer_query",
    )(pre, pre, pre, taps, valid, rate, bias, keys, w, u, states)


def rotated(shard, axis, by):
    devices = lax.axis_size(axis)
    return lax.ppermute(shard, axis, [(i, (i + by) % devices) for i in range(devices)])


def rotations(shard, axis):
    moved = [rotated(shard, axis, by) for by in reversed(range(1, lax.axis_size(axis)))]
    return [shard] + moved[::-1]


def scattered(pieces, axis):
    total = pieces[0].astype(F32)
    for by in range(1, lax.axis_size(axis)):
        total = total + rotated(pieces[by], axis, by).astype(F32)
    return total


def axis_total(values, axis):
    return scattered([values] * lax.axis_size(axis), axis)


def paired(shard, by):
    devices = lax.axis_size("tensor")
    return lax.ppermute(shard, "tensor", [(i, i ^ by) for i in range(devices)])


def pair_half(kept, sent, beside=None):
    width = kept.shape[1] // 2
    near = paired(sent, 1)
    if beside is not None:
        near = lax.optimization_barrier((near, beside))[0]
    other = (kept[:, width:].astype(F32) + near[:, width:].astype(F32)).astype(BF)
    return kept[:, :width].astype(F32) + near[:, :width].astype(F32), other


def pair_rest(own, other):
    return own + paired(other, 2).astype(F32)


def pair_gather(total):
    far = paired(total, 2)
    return [total, far, paired(jnp.concatenate([total, far], axis=1), 1)]


def pair_blocks(pieces, place, whole_ref):
    own, far, near = pieces
    width = whole_ref.shape[1] // 4
    for by, piece in ((0, own), (2, far), (1, near[:, :width]), (3, near[:, width:])):
        whole_ref[:, pl.ds(pl.multiple_of((place ^ by) * width, width), width)] = piece


def pair_parts(place, whole_width, compute, kept_ref, sent_ref):
    width = whole_width // 4
    for by, ref, col in ((1, sent_ref, 0), (3, sent_ref, 1), (0, kept_ref, 0), (2, kept_ref, 1)):
        span = pl.ds(pl.multiple_of((place ^ by) * width, width), width)
        ref[:, col * width : (col + 1) * width] = compute(span).astype(BF)


def swapped(shard):
    return lax.ppermute(shard, "fsdp", [(0, 1), (1, 0)])


def weight_rows(shard, axis):
    return lax.all_gather(shard, "fsdp", axis=axis, tiled=True)


def owners(grad):
    return lax.psum_scatter(grad, FH, scatter_dimension=0, tiled=True).astype(F32)


def owners_by_steps(grad):
    if lax.axis_size("fsdp") != 2:
        return grad, owners(grad)
    half = grad.shape[0] // 2
    core = lax.axis_index("fsdp")
    mine = lax.dynamic_slice_in_dim(grad, core * half, half)
    other = swapped(lax.dynamic_slice_in_dim(grad, (1 - core) * half, half))
    grad = (mine.astype(F32) + other.astype(F32)).astype(BF)
    count = lax.axis_size("heads")
    rows = half // count
    spot = lax.axis_index("heads")
    return grad, scattered(
        [
            lax.dynamic_slice_in_dim(grad, lax.rem(spot + by, count) * rows, rows)
            for by in range(count)
        ],
        "heads",
    )


def padded(width):
    return -(-width // LANES) * LANES


def weight_kernel(*refs, rows):
    out_ref = refs[-1]
    at = 0
    for index, many in enumerate(rows):
        left, right = refs[2 * index], refs[2 * index + 1]
        width = right.shape[1]
        part = mm_tn(left[...], right[...]).astype(BF)
        out_ref[:, at : at + width] = part
        if width < padded(width):
            out_ref[:, at + width : at + padded(width)] = jnp.zeros(
                (part.shape[0], padded(width) - width), BF
            )
        at += padded(width)


def weight_grads(*pairs):
    features = pairs[0][0].shape[1]
    total = sum(padded(right.shape[1]) for _, right in pairs)
    specs, args = [], []
    for left, right in pairs:
        many = right.shape[0]
        specs.append(pl.BlockSpec((many, PACK), lambda i: (0, i)))
        specs.append(pl.BlockSpec(right.shape, lambda i: (0, 0)))
        args += [left, right]
    return pl.pallas_call(
        functools.partial(weight_kernel, rows=[right.shape[0] for _, right in pairs]),
        grid=(features // PACK,),
        in_specs=specs,
        out_specs=pl.BlockSpec((PACK, total), lambda i: (i, 0)),
        out_shape=jax.ShapeDtypeStruct((features, total), BF),
        compiler_params=pltpu.CompilerParams(vmem_limit_bytes=VMEM_LIMIT),
        cost_estimate=cost(5),
        name="weight_grads",
    )(*args)


def total_batches(values):
    if lax.axis_size("fsdp") == 2:
        values = values + swapped(values)
    else:
        values = lax.psum(values, "fsdp")
    return axis_total(values, "heads")


def feature_blocks(pieces, place, whole_ref):
    count = len(pieces)
    width = whole_ref.shape[1] // count
    for by, piece in enumerate(pieces):
        at = lax.rem(place + count - by, count) * width
        whole_ref[:, pl.ds(pl.multiple_of(at, width), width)] = piece


def project_kernel(place_ref, *refs, count):
    pieces = refs[:count]
    gain_ref, weight_ref, token_ref, hidden_ref, scale_ref, pre_ref = refs[count:]
    rows = pieces[0].shape[0] - RIM

    @pl.when(pl.program_id(0) == 0)
    def _():
        feature_blocks([piece[...] for piece in pieces], place_ref[0], token_ref)

        def norm(start, many):
            span = pl.ds(start, many)
            values = token_ref[span, :].astype(F32)
            scale = lax.rsqrt(jnp.mean(values * values, axis=1, keepdims=True) + EPSILON)
            hidden_ref[span, :] = (values * scale * gain_ref[...]).astype(BF)
            scale_ref[span, :] = jnp.broadcast_to(scale, (many, LANES))

        for start in range(0, rows, PACK):
            norm(start, PACK)
        norm(rows, RIM)

    pre_ref[...] = mm(hidden_ref[...], weight_ref[...])


def project(tensor_place, pieces, gain, weight):
    total = pieces[0].shape[0]
    features, outs = weight.shape
    count = len(pieces)
    tile = 2 * LANES
    whole = lambda shape: pl.BlockSpec(shape, lambda i, at: (0,) * len(shape))
    return pl.pallas_call(
        functools.partial(project_kernel, count=count),
        grid_spec=pltpu.PrefetchScalarGridSpec(
            num_scalar_prefetch=1,
            grid=(outs // tile,),
            in_specs=[whole(piece.shape) for piece in pieces]
            + [whole(gain.shape), pl.BlockSpec((features, tile), lambda i, at: (0, i))],
            out_specs=[
                whole((total, features)),
                whole((total, features)),
                whole((total, LANES)),
                pl.BlockSpec((total, tile), lambda i, at: (0, i)),
            ],
        ),
        out_shape=[
            jax.ShapeDtypeStruct((total, features), BF),
            jax.ShapeDtypeStruct((total, features), BF),
            jax.ShapeDtypeStruct((total, LANES), F32),
            jax.ShapeDtypeStruct((total, outs), F32),
        ],
        compiler_params=pltpu.CompilerParams(vmem_limit_bytes=VMEM_LIMIT),
        cost_estimate=cost(8),
        name="project",
    )(tensor_place, *pieces, gain, weight)


def output_kernel(
    place_ref,
    local_ref,
    carry_ref,
    end1_ref,
    end2_ref,
    end3_ref,
    end4_ref,
    gate_ref,
    gain_ref,
    weight_ref,
    mixed_ref,
    normed_ref,
    enter_ref,
    *partial_refs,
    heads,
    key_width,
    value_width,
    chunks,
):
    step = pl.program_id(0)

    @pl.when(step == 0)
    def _():
        for head in range(heads):
            state = end4_ref[head, :, :value_width].astype(F32)
            for end in (end3_ref, end2_ref, end1_ref):
                state = end[head, :, :value_width].astype(F32) + mm(
                    end[head, :, value_width:], state
                )
            enter_ref[head] = state.astype(BF)

    for head in range(heads):
        cols = slice(head * value_width, (head + 1) * value_width)
        mixed = local_ref[:, cols] + mm(
            carry_ref[:, head * key_width : (head + 1) * key_width], enter_ref[head]
        )
        mixed_low = mixed.astype(BF)
        mixed_ref[:, cols] = mixed_low
        mixed = mixed_low.astype(F32)
        scale = lax.rsqrt(jnp.mean(mixed * mixed, axis=1, keepdims=True) + EPSILON)
        gate = gate_ref[:, cols]
        normed = mixed * scale * gain_ref[...] * (gate * sigmoid(gate))
        normed_ref[:, cols] = normed.astype(BF)
    steps = pl.num_programs(0) // chunks
    for chunk in range(chunks):

        @pl.when(step // steps == chunk)
        def _():
            pair_parts(
                place_ref[0],
                weight_ref.shape[1],
                lambda span: mm(normed_ref[...], weight_ref[:, span]),
                *partial_refs[2 * chunk : 2 * chunk + 2],
            )


def mixer_output(
    local, carry, ends, tensor_place, pre, gain, weight, key_width, value_width, chunks
):
    rows, cols = local.shape
    heads = cols // value_width
    width = weight.shape[1] // 2
    gate_block = heads * (2 * key_width + value_width) // cols
    steps = rows // PACK // chunks
    whole = lambda shape: pl.BlockSpec(shape, lambda i, at: (0,) * len(shape))

    def part_spec(chunk):
        return pl.BlockSpec(
            (PACK, width), lambda i, at: (jnp.clip(i - chunk * steps, 0, steps - 1), 0)
        )

    outs = pl.pallas_call(
        functools.partial(
            output_kernel,
            heads=heads,
            key_width=key_width,
            value_width=value_width,
            chunks=chunks,
        ),
        grid_spec=pltpu.PrefetchScalarGridSpec(
            num_scalar_prefetch=1,
            grid=(rows // PACK,),
            in_specs=[
                pl.BlockSpec((PACK, cols), lambda i, at: (i, 0)),
                pl.BlockSpec((PACK, carry.shape[1]), lambda i, at: (i, 0)),
                whole(ends[0].shape),
                whole(ends[0].shape),
                whole(ends[0].shape),
                whole(ends[0].shape),
                pl.BlockSpec((PACK, cols), lambda i, at: (i, gate_block)),
                whole(gain.shape),
                whole((cols, weight.shape[1])),
            ],
            out_specs=[
                pl.BlockSpec((PACK, cols), lambda i, at: (i, 0)),
                pl.BlockSpec((PACK, cols), lambda i, at: (i, 0)),
                whole((heads, key_width, value_width)),
            ]
            + [part_spec(chunk) for chunk in range(chunks) for _ in range(2)],
        ),
        out_shape=[
            jax.ShapeDtypeStruct((rows, cols), BF),
            jax.ShapeDtypeStruct((rows, cols), BF),
            jax.ShapeDtypeStruct((heads, key_width, value_width), BF),
        ]
        + [jax.ShapeDtypeStruct((rows // chunks, width), BF)] * (chunks * 2),
        compiler_params=pltpu.CompilerParams(vmem_limit_bytes=VMEM_LIMIT),
        cost_estimate=cost(7),
        name="mixer_output",
    )(tensor_place, local, carry, *ends, pre, gain, weight)
    parts = outs[3:]
    return outs[0], outs[1], outs[2], [parts[c * 2 : c * 2 + 2] for c in range(chunks)]


def feed_kernel(place_ref, *refs, chunks):
    attn = refs[: 3 * chunks]
    cot_ref, token_ref, gain_ref, gate_ref, up_ref, down_ref = refs[3 * chunks : 3 * chunks + 6]
    outs = refs[3 * chunks + 6 :]
    middle_ref, hidden_ref, inner_ref, gate_grad_ref, up_grad_ref = outs[:5]
    out_refs, mid_refs = outs[5:9], outs[9 : 9 + 2 * chunks]
    whole_ref, kept_ref, sent_ref = outs[9 + 2 * chunks :]
    first = down_ref.shape[0] - inner_ref.shape[1]
    place = place_ref[0]
    chunk_now = pl.program_id(0) // (pl.num_programs(0) // chunks)
    for chunk in range(chunks):

        @pl.when(chunk_now == chunk)
        def _():
            pieces = [piece[...] for piece in attn[3 * chunk : 3 * chunk + 3]]
            pair_blocks(pieces, place, whole_ref)

    middle = token_ref[...].astype(F32) + whole_ref[...].astype(F32)
    middle_ref[...] = middle
    scale = lax.rsqrt(jnp.mean(middle * middle, axis=1, keepdims=True) + EPSILON)
    hidden = (middle * scale * gain_ref[...]).astype(BF)
    hidden_ref[...] = hidden
    many = inner_ref.shape[1]
    gate = mm(hidden, gate_ref[:, :many])
    up = mm(hidden, up_ref[:, :many])
    inner_grad = mm_nt(cot_ref[...], down_ref[first:, :])
    sig = sigmoid(gate)
    silu = gate * sig
    inner_ref[...] = (silu * up).astype(BF)
    gate_grad_ref[...] = (inner_grad * up * (sig * (1.0 + gate * (1.0 - sig)))).astype(BF)
    up_grad_ref[...] = (inner_grad * silu).astype(BF)
    features = whole_ref.shape[1]
    pair_parts(
        place,
        features,
        lambda span: mm_nt(gate_grad_ref[...], gate_ref[span, :many])
        + mm_nt(up_grad_ref[...], up_ref[span, :many]),
        kept_ref,
        sent_ref,
    )
    for chunk in range(chunks):

        @pl.when(chunk_now == chunk)
        def _():
            mid_refs[2 * chunk][...] = kept_ref[...]
            mid_refs[2 * chunk + 1][...] = sent_ref[...]

    width = features // 4
    for by in range(4):
        span = pl.ds(pl.multiple_of((place ^ by) * width, width), width)
        out_refs[by][...] = mm(inner_ref[...], down_ref[first:, span]).astype(BF)


def feed_forward(tensor_place, attn, cot, token, gain, feed, down, hidden):
    rows, features = cot.shape
    chunks = len(attn)
    width = features // 2
    step_rows = rows // chunks
    steps = 1
    whole = lambda shape: pl.BlockSpec(shape, lambda i, at: (0,) * len(shape))
    rows_at = lambda size: pl.BlockSpec((step_rows, size), lambda i, at: (i, 0))

    def part(chunk, size):
        return pl.BlockSpec(
            (step_rows, size), lambda i, at: (jnp.clip(i - chunk * steps, 0, steps - 1), 0)
        )

    kept = [
        (features, F32),
        (features, BF),
        (hidden, BF),
        (hidden, BF),
        (hidden, BF),
    ] + [(width // 2, BF)] * 4
    outs = pl.pallas_call(
        functools.partial(feed_kernel, chunks=chunks),
        grid_spec=pltpu.PrefetchScalarGridSpec(
            num_scalar_prefetch=1,
            grid=(chunks,),
            in_specs=[
                part(chunk, piece.shape[1]) for chunk in range(chunks) for piece in attn[chunk]
            ]
            + [rows_at(features)] * 2
            + [
                whole(gain.shape),
                pl.BlockSpec((features, feed.shape[1] // 2), lambda i, at: (0, 0)),
                pl.BlockSpec((features, feed.shape[1] // 2), lambda i, at: (0, 1)),
                whole(down.shape),
            ],
            out_specs=[rows_at(size) for size, _ in kept]
            + [part(chunk, width) for chunk in range(chunks) for _ in range(2)],
            scratch_shapes=[pltpu.VMEM((step_rows, features), BF)]
            + [pltpu.VMEM((step_rows, width), BF)] * 2,
        ),
        out_shape=[jax.ShapeDtypeStruct((rows, size), kind) for size, kind in kept]
        + [jax.ShapeDtypeStruct((rows // chunks, width), BF)] * (2 * chunks),
        compiler_params=pltpu.CompilerParams(vmem_limit_bytes=VMEM_LIMIT),
        cost_estimate=cost(20),
        name="feed_forward",
    )(tensor_place, *[piece for pieces in attn for piece in pieces], cot, token, gain, feed, feed, down)
    return outs[:9], [outs[9 + 2 * chunk : 11 + 2 * chunk] for chunk in range(chunks)]


def gate_back_kernel(
    place_ref, *refs, count, aliased, heads, key_width, value_width
):
    pieces = refs[:count]
    (
        middle_ref,
        cot_ref,
        ffn_gain_ref,
        weight_ref,
        mixed_ref,
        gate_ref,
        gain_ref,
        query_w_ref,
        states_ref,
    ) = refs[count : count + 9]
    (
        attn_grad_ref,
        mixed_grad_ref,
        gate_grad_ref,
        source_ref,
        own_ref,
        ffn_gain_grad_ref,
        gain_grad_ref,
        enter_grad_ref,
        whole_ref,
        middle_grad_ref,
    ) = refs[count + 9 + aliased :]
    inner = PACK // GROUP

    @pl.when(pl.program_id(0) == 0)
    def _():
        gain_grad_ref[...] = jnp.zeros_like(gain_grad_ref)
        ffn_gain_grad_ref[...] = jnp.zeros_like(ffn_gain_grad_ref)
        enter_grad_ref[...] = jnp.zeros_like(enter_grad_ref)

    pair_blocks([piece[...] for piece in pieces], place_ref[0], whole_ref)
    middle = middle_ref[...]
    scale_mid = lax.rsqrt(jnp.mean(middle * middle, axis=1, keepdims=True) + EPSILON)
    hidden_grad = whole_ref[...].astype(F32)
    unit_mid = middle * scale_mid
    ffn_gain_grad_ref[0:1, :] += jnp.sum(hidden_grad * unit_mid, axis=0, keepdims=True)
    scaled_mid = hidden_grad * ffn_gain_ref[...]
    along = jnp.mean(scaled_mid * unit_mid, axis=1, keepdims=True)
    middle_grad = cot_ref[...].astype(F32) + scale_mid * (scaled_mid - unit_mid * along)
    middle_grad_ref[...] = middle_grad
    width = own_ref.shape[1]
    own_ref[...] = middle_grad_ref[
        :, pl.ds(pl.multiple_of(place_ref[0] * width, width), width)
    ]
    attn_grad = middle_grad.astype(BF)
    attn_grad_ref[...] = attn_grad
    normed_grad = mm_nt(attn_grad, weight_ref[...])
    gain = gain_ref[...]
    for head in range(heads):
        cols = slice(head * value_width, (head + 1) * value_width)
        grad = normed_grad[:, cols]
        mixed = mixed_ref[:, cols].astype(F32)
        scale = lax.rsqrt(jnp.mean(mixed * mixed, axis=1, keepdims=True) + EPSILON)
        gate = gate_ref[:, cols]
        sig = sigmoid(gate)
        silu = gate * sig
        unit = mixed * scale
        scaled = grad * unit
        gate_grad_ref[:, cols] = (scaled * gain * (sig * (1.0 + gate * (1.0 - sig)))).astype(BF)
        gain_grad_ref[0:1, :] += jnp.sum(scaled * silu, axis=0, keepdims=True)
        unit_grad = grad * gain * silu
        mixed_grad = scale * (unit_grad - unit * jnp.mean(unit_grad * unit, axis=1, keepdims=True))
        mixed_grad = mixed_grad.astype(BF)
        mixed_grad_ref[:, cols] = mixed_grad
        total = enter_grad_ref[head]
        for b in range(inner):
            index = b * heads + head
            source = mm_tn(
                query_w_ref[index], mixed_grad[b * GROUP : (b + 1) * GROUP]
            )
            source_ref[index] = source
            total = total + mm_tn(states_ref[index, :, value_width:], source)
        enter_grad_ref[head] = total


def gate_back(
    chunk,
    chunks,
    tensor_place,
    pieces,
    middle,
    cot,
    ffn_gain,
    weight,
    mixed,
    pre,
    gain,
    query_w,
    states,
    before,
    key_width,
    value_width,
):
    rows, features = middle.shape
    width = pieces[0].shape[1]
    cols = mixed.shape[1]
    heads = cols // value_width
    gate_block = heads * (2 * key_width + value_width) // cols
    step = PACK // GROUP * heads
    steps = rows // PACK // chunks
    first = chunk * steps
    whole = lambda shape: pl.BlockSpec(shape, lambda i, at: (0,) * len(shape))
    rows_at = lambda size, col=0: pl.BlockSpec((PACK, size), lambda i, at: (first + i, col))
    blocks_at = lambda shape: pl.BlockSpec((step,) + shape, lambda i, at: (first + i, 0, 0))
    inputs = [*pieces, middle, cot, ffn_gain, weight, mixed, pre, gain, query_w, states]
    outs = pl.pallas_call(
        functools.partial(
            gate_back_kernel,
            count=len(pieces),
            aliased=len(before),
            heads=heads,
            key_width=key_width,
            value_width=value_width,
        ),
        grid_spec=pltpu.PrefetchScalarGridSpec(
            num_scalar_prefetch=1,
            grid=(steps,),
            in_specs=[
                pl.BlockSpec((PACK, piece.shape[1]), lambda i, at: (i, 0)) for piece in pieces
            ]
            + [
                rows_at(features),
                rows_at(features),
                whole(ffn_gain.shape),
                whole((cols, features)),
                rows_at(cols),
                rows_at(cols, gate_block),
                whole(gain.shape),
                blocks_at(query_w.shape[1:]),
                blocks_at(states.shape[1:]),
            ]
            + [pl.BlockSpec(memory_space=pl.ANY)] * len(before),
            out_specs=[
                rows_at(features),
                rows_at(cols),
                rows_at(cols),
                blocks_at((key_width, value_width)),
                rows_at(width),
                whole((8, features)),
                whole((8, value_width)),
                whole((heads, key_width, value_width)),
            ],
            scratch_shapes=[pltpu.VMEM((PACK, features), BF), pltpu.VMEM((PACK, features), F32)],
        ),
        out_shape=[
            jax.ShapeDtypeStruct((rows, features), BF),
            jax.ShapeDtypeStruct((rows, cols), BF),
            jax.ShapeDtypeStruct((rows, cols), BF),
            jax.ShapeDtypeStruct((rows // GROUP * heads, key_width, value_width), F32),
            jax.ShapeDtypeStruct((rows, width), F32),
            jax.ShapeDtypeStruct((8, features), F32),
            jax.ShapeDtypeStruct((8, value_width), F32),
            jax.ShapeDtypeStruct((heads, key_width, value_width), F32),
        ],
        input_output_aliases={1 + len(inputs) + i: i for i in range(len(before))},
        compiler_params=pltpu.CompilerParams(vmem_limit_bytes=VMEM_LIMIT),
        cost_estimate=cost(7),
        name="gate_back",
    )(tensor_place, *inputs, *before)
    return outs[:5], outs[5:]


def input_kernel(
    place_ref,
    pre_grad_ref,
    small_grad_ref,
    gate_grad_ref,
    weight_ref,
    token_ref,
    scale_ref,
    gain_ref,
    dot_ref,
    gain_grad_ref,
    rim_ref,
    part_ref,
    terms_ref,
):
    rows = gate_grad_ref.shape[0]
    wide = pre_grad_ref.shape[1]
    gate_wide = gate_grad_ref.shape[1]
    small_wide = small_grad_ref.shape[1]
    width = token_ref.shape[1]
    step = pl.program_id(0)

    @pl.when(step == 0)
    def _():
        dot_ref[...] = jnp.zeros_like(dot_ref)

    terms = mm_nt(pre_grad_ref[...], weight_ref[:, :wide])
    terms = terms + mm_nt(
        small_grad_ref[...], weight_ref[:, wide + gate_wide : wide + gate_wide + small_wide]
    )
    terms_ref[...] = terms
    terms_ref[:rows, :] += mm_nt(gate_grad_ref[...], weight_ref[:, wide : wide + gate_wide])
    rim_ref[...] = terms_ref[rows:, :]
    terms = terms_ref[...]
    product = terms * token_ref[...].astype(F32)
    dot_ref[...] += jnp.sum(product * gain_ref[...], axis=1, keepdims=True)
    total = jnp.sum(product * scale_ref[:, 0:1], axis=0, keepdims=True)
    gain_grad_ref[...] = jnp.broadcast_to(total, gain_grad_ref.shape)
    part_ref[...] = terms[:rows].astype(BF)


def input_terms(tensor_place, pre_grad, small_grad, gate_grad, weight, token, scale, gain, count):
    total, wide = pre_grad.shape
    rows, gate_wide = gate_grad.shape
    features, outs = weight.shape
    width = features // count
    whole = lambda shape: pl.BlockSpec(shape, lambda i, at: (0,) * len(shape))
    spot = lambda i, at: lax.rem(at[0] + i, count)
    found = pl.pallas_call(
        input_kernel,
        grid_spec=pltpu.PrefetchScalarGridSpec(
            num_scalar_prefetch=1,
            grid=(count,),
            in_specs=[
                whole(pre_grad.shape),
                whole(small_grad.shape),
                whole(gate_grad.shape),
                pl.BlockSpec((width, outs), lambda i, at: (spot(i, at), 0)),
                pl.BlockSpec((total, width), lambda i, at: (0, spot(i, at))),
                whole(scale.shape),
                pl.BlockSpec((1, width), lambda i, at: (0, spot(i, at))),
            ],
            out_specs=[
                whole((total, LANES)),
                pl.BlockSpec((8, width), lambda i, at: (0, spot(i, at))),
                pl.BlockSpec((RIM, width), lambda i, at: (0, spot(i, at))),
                pl.BlockSpec((rows, width), lambda i, at: (0, spot(i, at))),
            ],
            scratch_shapes=[pltpu.VMEM((total, width), F32)],
        ),
        out_shape=[
            jax.ShapeDtypeStruct((total, LANES), F32),
            jax.ShapeDtypeStruct((8, features), F32),
            jax.ShapeDtypeStruct((RIM, features), F32),
            jax.ShapeDtypeStruct((rows, features), BF),
        ],
        compiler_params=pltpu.CompilerParams(vmem_limit_bytes=VMEM_LIMIT),
        cost_estimate=cost(8),
        name="input_terms",
    )(tensor_place, pre_grad, small_grad, gate_grad, weight, token, scale, gain)
    return found


def conv_back(unit_grad, window, taps_ref, valid, first, width, factor, taps_grad_ref):
    conv, pieces = active_of(window, taps_ref, valid, first, width)
    sig = sigmoid(conv)
    act_grad = unit_grad
    if factor is not None:
        act = conv * sig
        scale = lax.rsqrt(jnp.sum(act * act, axis=1, keepdims=True) + EPSILON)
        along = jnp.sum(unit_grad * act, axis=1, keepdims=True)
        act_grad = (factor * scale) * (unit_grad - act * (scale * scale * along))
    conv_grad = act_grad * (sig * (1.0 + conv * (1.0 - sig)))
    for j in range(CONV):
        taps_grad_ref[j : j + 1, first : first + width] += jnp.sum(
            conv_grad * valid[:, j : j + 1] * pieces[j], axis=0, keepdims=True
        )
    return conv_grad


def true_kernel(
    small_ref,
    rate_ref,
    bias_ref,
    w_ref,
    u_ref,
    states_ref,
    enter_ref,
    true_ref,
    whole_ref,
    renewed_ref,
    *,
    heads,
    rows,
    key_width,
    value_width,
):
    inner = PACK // GROUP

    span = slice(0, PACK)
    decay_tile, _ = rates_of(small_ref[span, :], rate_ref[...], bias_ref[...])
    for head in range(heads):
        cols = slice(head * key_width, (head + 1) * key_width)
        value_at = slice(head * value_width, (head + 1) * value_width)
        decay = column_of(decay_tile, head)
        w = w_ref[span, cols]
        u = u_ref[span, value_at]
        renewed = []
        for b in range(inner):
            index = b * heads + head
            part = slice(b * GROUP, (b + 1) * GROUP)
            whole = jnp.exp(jnp.sum(decay[part], axis=0, keepdims=True))
            whole_ref[index] = jnp.broadcast_to(whole, (8, LANES))
            state = (
                states_ref[index, :, :value_width].astype(F32)
                + mm(states_ref[index, :, value_width:], enter_ref[head])
            ).astype(BF)
            true_ref[index] = state
            renewed.append((u[part].astype(F32) - mm(w[part], state)).astype(BF))
        renewed_ref[span, value_at] = jnp.concatenate(renewed, axis=0)


def mixer_true(pre, rate, bias, w, u, states, enter, heads, key_width, value_width):
    rows = pre.shape[0] - RIM
    wide = heads * (2 * key_width + value_width)
    gate_wide = heads * value_width
    count = rows // GROUP
    whole = lambda shape: pl.BlockSpec(shape, lambda i: (0,) * len(shape))
    outs = [
        ((count * heads, key_width, value_width), BF),
        ((count * heads, 8, LANES), F32),
        ((rows, heads * value_width), BF),
    ]
    given = [rate, bias, w, u, states, enter]
    rows_at = lambda width: pl.BlockSpec((PACK, width), lambda i: (i, 0))
    blocks_at = lambda shape: pl.BlockSpec(
        (PACK // GROUP * heads,) + shape, lambda i: (i, 0, 0)
    )
    return pl.pallas_call(
        functools.partial(
            true_kernel, heads=heads, rows=rows, key_width=key_width, value_width=value_width
        ),
        grid=(rows // PACK,),
        in_specs=[
            pl.BlockSpec((PACK, LANES), lambda i: (i, (wide + gate_wide) // LANES)),
            whole(rate.shape),
            whole(bias.shape),
            rows_at(w.shape[1]),
            rows_at(u.shape[1]),
            blocks_at(states.shape[1:]),
            whole(enter.shape),
        ],
        out_specs=[
            blocks_at((key_width, value_width)),
            blocks_at((8, LANES)),
            rows_at(heads * value_width),
        ],
        out_shape=[jax.ShapeDtypeStruct(shape, kind) for shape, kind in outs],
        compiler_params=pltpu.CompilerParams(vmem_limit_bytes=VMEM_LIMIT),
        cost_estimate=cost(6),
        name="mixer_true",
    )(pre, *given)


def ready_kernel(
    head_ref,
    pre_ref,
    small_ref,
    taps_ref,
    valid_ref,
    rate_ref,
    bias_ref,
    queries_ref,
    keys_ref,
    true_ref,
    renewed_ref,
    mixed_grad_ref,
    base_ref,
    key_part_ref,
    conv_grad_ref,
    taps_grad_ref,
    along_ref,
    *,
    heads,
    rows,
    key_width,
    value_width,
):
    inner = PACK // GROUP
    group = pl.program_id(0)

    @pl.when(group == 0)
    def _():
        taps_grad_ref[...] = jnp.zeros_like(taps_grad_ref)
    masks = pack_masks()
    row, col, apart, same, lower, strict = masks
    span = slice(0, PACK)
    valid = valid_ref[pl.ds(pl.multiple_of(group * PACK + RIM, RIM), PACK), :]
    decay_tile, _ = rates_of(small_ref[span, :], rate_ref[...], bias_ref[...])
    lane = lax.broadcasted_iota(jnp.int32, (PACK, LANES), 1)
    along = jnp.zeros((PACK, LANES), F32)
    for head in range(heads):
        cols = slice(head * key_width, (head + 1) * key_width)
        value_at = slice(head * value_width, (head + 1) * value_width)
        query = queries_ref[span, cols]
        key = keys_ref[span, cols]
        gam, last, fading = packed_decay(column_of(decay_tile, head), masks)
        scores = mm_nt(query, key) * fading
        renewed = renewed_ref[span, value_at]
        out_grad = mixed_grad_ref[span, value_at]
        grown_grad = []
        for b in range(inner):
            index = b * heads + head
            part = slice(b * GROUP, (b + 1) * GROUP)
            grown_grad.append(mm_nt(out_grad[part], true_ref[index]))
        base_ref[span, value_at] = mm_tn(scores, out_grad)
        scores_grad = jnp.where(lower, mm_nt(out_grad, renewed), 0.0)
        pair_grad = (scores_grad * fading).astype(BF)
        grown_grad = jnp.exp(gam) * jnp.concatenate(grown_grad, axis=0)
        query_grad = mm(pair_grad, key) + grown_grad
        along = jnp.where(
            lane == head,
            net_of(scores_grad * scores, apart)
            + jnp.sum(grown_grad * query.astype(F32), axis=1, keepdims=True),
            along,
        )
        key_part_ref[span, cols] = mm_tn(pair_grad, query)
        window = jnp.concatenate([head_ref[:, cols], pre_ref[:, cols]], axis=0)
        conv_grad_ref[span, cols] = conv_back(
            query_grad,
            window,
            taps_ref,
            valid,
            head * key_width,
            key_width,
            key_width ** (-0.5),
            taps_grad_ref,
        )
    along_ref[span, :] = along


def mixer_ready(
    pre,
    taps,
    valid,
    rate,
    bias,
    queries,
    keys,
    true,
    renewed,
    mixed_grad,
    heads,
    key_width,
    value_width,
):
    rows = pre.shape[0] - RIM
    wide = heads * (2 * key_width + value_width)
    gate_wide = heads * value_width
    key_cols = heads * key_width
    whole = lambda shape: pl.BlockSpec(shape, lambda i: (0,) * len(shape))
    outs = [
        ((rows, heads * value_width), F32),
        ((rows, key_cols), F32),
        ((rows, key_cols), F32),
        ((8, key_cols), F32),
        ((rows, LANES), F32),
    ]
    rows_at = lambda width: pl.BlockSpec((PACK, width), lambda i: (i, 0))
    head_at = lambda i: jnp.where(i == 0, rows // RIM, i * (PACK // RIM) - 1)
    return pl.pallas_call(
        functools.partial(
            ready_kernel, heads=heads, rows=rows, key_width=key_width, value_width=value_width
        ),
        grid=(rows // PACK,),
        in_specs=[
            pl.BlockSpec((RIM, key_cols), lambda i: (head_at(i), 0)),
            rows_at(key_cols),
            pl.BlockSpec((PACK, LANES), lambda i: (i, (wide + gate_wide) // LANES)),
            whole(taps.shape),
            whole(valid.shape),
            whole(rate.shape),
            whole(bias.shape),
            rows_at(key_cols),
            rows_at(key_cols),
            pl.BlockSpec((PACK // GROUP * heads,) + true.shape[1:], lambda i: (i, 0, 0)),
            rows_at(renewed.shape[1]),
            rows_at(mixed_grad.shape[1]),
        ],
        out_specs=[
            whole(shape) if shape[0] == 8 else rows_at(shape[1]) for shape, _ in outs
        ],
        out_shape=[jax.ShapeDtypeStruct(shape, kind) for shape, kind in outs],
        compiler_params=pltpu.CompilerParams(vmem_limit_bytes=VMEM_LIMIT),
        cost_estimate=cost(11),
        name="mixer_ready",
    )(
        pre,
        pre,
        pre,
        taps,
        valid,
        rate,
        bias,
        queries,
        keys,
        true,
        renewed,
        mixed_grad,
    )


def backward_kernel(
    keep_ref,
    head_ref,
    pre_ref,
    small_ref,
    taps_ref,
    valid_ref,
    rate_ref,
    bias_ref,
    keys_ref,
    inverse_ref,
    w_ref,
    u_ref,
    fold_ref,
    source_ref,
    true_ref,
    whole_ref,
    renewed_ref,
    base_ref,
    key_part_ref,
    query_conv_ref,
    query_taps_ref,
    along_ref,
    next1_ref,
    next2_ref,
    next3_ref,
    next4_ref,
    pre_grad_ref,
    small_grad_ref,
    taps_grad_ref,
    rate_grad_ref,
    later_ref,
    conv_grad_ref,
    flow_ref,
    *,
    heads,
    rows,
    key_width,
    value_width,
):
    groups = rows // PACK
    inner = PACK // GROUP
    key_cols = heads * key_width
    wide = heads * (2 * key_width + value_width)
    step = pl.program_id(0)

    @pl.when(step == 0)
    def _():
        taps_grad_ref[...] = jnp.zeros_like(taps_grad_ref)
        taps_grad_ref[:, :key_cols] = query_taps_ref[...]
        rate_grad_ref[...] = jnp.zeros_like(rate_grad_ref)
        conv_grad_ref[0:RIM, :] = jnp.zeros((RIM, wide), F32)
        conv_grad_ref[RIM + rows :, :] = jnp.zeros((RIM, wide), F32)
        conv_grad_ref[RIM : RIM + rows, :key_cols] = query_conv_ref[...]
        small_grad_ref[rows:, :] = jnp.zeros((RIM, LANES), BF)

        for head in range(heads):
            flow = next4_ref[head, :, :value_width].astype(F32)
            for near in (next3_ref, next2_ref, next1_ref):
                flow = near[head, :, :value_width].astype(F32) + mm_tn(
                    near[head, :, value_width:], flow
                )
            flow_ref[head] = flow
        for block in reversed(range(rows // GROUP)):
            for head in range(heads):
                index = block * heads + head
                flow = flow_ref[head]
                flow_low = flow.astype(BF)
                later_ref[index] = flow_low
                flow_ref[head] = keep_ref[block] * (
                    whole_ref[index, 0:1, 0:1] * flow
                    - mm_tn(fold_ref[index], flow_low)
                    + source_ref[index]
                )

    @pl.when(step > 0)
    def _():
        group = step - 1
        masks = pack_masks()
        row, col, apart, same, lower, strict = masks
        span = pl.ds(0, PACK)
        out_span = pl.ds(pl.multiple_of(group * PACK, PACK), PACK)
        small = small_ref[span, :]
        valid = valid_ref[pl.ds(pl.multiple_of(group * PACK + RIM, RIM), PACK), :]
        decay_tile, beta_tile = rates_of(small, rate_ref[...], bias_ref[...])
        lane = lax.broadcasted_iota(jnp.int32, (PACK, LANES), 1)
        small_rows = jnp.zeros((PACK, LANES), F32)
        for head in range(heads):
            decay = column_of(decay_tile, head)
            beta = column_of(beta_tile, heads + head)
            cols = slice(head * key_width, (head + 1) * key_width)
            value_at = slice(head * value_width, (head + 1) * value_width)
            key = keys_ref[span, cols]
            value = keys_ref[span, key_cols + head * value_width : key_cols + (head + 1) * value_width]
            key_f = key.astype(F32)
            gam, last, fading = packed_decay(decay, masks)
            growth = jnp.exp(gam)
            rest = jnp.exp(last - gam)
            gram = mm_nt(key, key)
            tail = (rest * key_f).astype(BF)
            w = w_ref[span, cols]
            u = u_ref[span, value_at]
            renewed = renewed_ref[span, value_at]
            renewed_grad, drops = [], []
            for b in range(inner):
                index = (group * inner + b) * heads + head
                near = b * heads + head
                flow = later_ref[index]
                renewed_grad.append(mm(tail[b * GROUP : (b + 1) * GROUP], flow))
                shared = true_ref[near].astype(F32) * flow.astype(F32)
                shared = jnp.sum(jnp.sum(shared, axis=1, keepdims=True), axis=0, keepdims=True)
                drops.append(
                    jnp.broadcast_to(shared * whole_ref[index, 0:1, 0:1], (GROUP, 1))
                )
            renewed_low = (base_ref[span, value_at] + jnp.concatenate(renewed_grad, axis=0)).astype(
                BF
            )
            tail_grad, w_grad = [], []
            for b in range(inner):
                index = (group * inner + b) * heads + head
                part = slice(b * GROUP, (b + 1) * GROUP)
                tail_grad.append(mm_nt(renewed[part], later_ref[index]))
                w_grad.append(mm_nt(renewed_low[part], true_ref[b * heads + head]))
            tail_grad = jnp.concatenate(tail_grad, axis=0)
            w_grad = -jnp.concatenate(w_grad, axis=0)
            inverse = inverse_ref[head]
            keys_grad = mm_tn(inverse, w_grad)
            values_grad = mm_tn(inverse, renewed_low)
            system_grad = jnp.where(strict, -(mm_nt(keys_grad, w) + mm_nt(values_grad, u)), 0.0)
            gram_beta = system_grad * fading
            gram_grad = (gram_beta * beta).astype(BF)
            key_grad = (
                mm(gram_grad, key)
                + mm_tn(gram_grad, key)
                + key_part_ref[span, cols]
                + beta * growth * keys_grad
                + rest * tail_grad
            )
            value_grad = beta * values_grad
            keys_dot = growth * jnp.sum(keys_grad * key_f, axis=1, keepdims=True)
            beta_grad = (
                keys_dot
                + jnp.sum(values_grad * value.astype(F32), axis=1, keepdims=True)
                + jnp.sum(gram_beta * gram, axis=1, keepdims=True)
            )
            tail_dot = rest * jnp.sum(tail_grad * key_f, axis=1, keepdims=True)
            system = jnp.where(strict, fading * beta * gram, 0.0)
            gam_grad = (
                along_ref[span, head : head + 1]
                + beta * keys_dot
                + net_of(system_grad * system, apart)
            )
            gam_grad_row = jnp.sum(
                jnp.where(apart == 0, jnp.broadcast_to(gam_grad, (PACK, PACK)), 0.0),
                axis=0,
                keepdims=True,
            )
            tail_row = jnp.sum(
                jnp.where(apart == 0, jnp.broadcast_to(tail_dot, (PACK, PACK)), 0.0),
                axis=0,
                keepdims=True,
            )
            decay_grad = jnp.sum(
                jnp.where(same, jnp.where(col >= row, gam_grad_row, tail_row), 0.0),
                axis=1,
                keepdims=True,
            ) + jnp.concatenate(drops, axis=0)
            small_rows = jnp.where(lane == head, decay_grad, small_rows)
            small_rows = jnp.where(lane == heads + head, beta_grad, small_rows)

            for first, width, unit_grad, factor in (
                (key_cols + head * key_width, key_width, key_grad, 1.0),
                (2 * key_cols + head * value_width, value_width, value_grad, None),
            ):
                window = jnp.concatenate(
                    [head_ref[:, first : first + width], pre_ref[:, first : first + width]], axis=0
                )
                conv_grad_ref[
                    pl.ds(pl.multiple_of(group * PACK + RIM, RIM), PACK), first : first + width
                ] = conv_back(
                    unit_grad, window, taps_ref, valid, first, width, factor, taps_grad_ref
                )

        raw = small + bias_ref[...]
        slope = -jnp.exp(rate_ref[...]) * sigmoid(raw)
        small_grad = jnp.where(
            lane < heads, small_rows * slope, small_rows * beta_tile * (1.0 - beta_tile)
        )
        small_grad = jnp.where(lane < 2 * heads, small_grad, 0.0)
        small_grad_ref[out_span, :] = small_grad.astype(BF)
        rate_grad_ref[0:1, :] += jnp.sum(small_rows * decay_tile, axis=0, keepdims=True)
        rate_grad_ref[1:2, :] += jnp.sum(small_grad, axis=0, keepdims=True)

    def convolve_back(start, target, count, first):
        cols = slice(first, first + LANES)
        window = conv_grad_ref[pl.ds(start, count + RIM), cols]
        flags = valid_ref[pl.ds(start, count + RIM), :]
        total = None
        for j in range(CONV):
            term = window * (flags[:, j : j + 1] * taps_ref[j : j + 1, cols])
            shift = CONV - 1 - j
            if shift:
                term = pltpu.roll(term, count + RIM - shift, 0)
            total = term if total is None else total + term
        pre_grad_ref[pl.ds(target, count), cols] = total[:count].astype(BF)

    @pl.when(step == groups)
    def _():
        def spread(group, _):
            base = pl.multiple_of(group * PACK, PACK)
            for first in range(0, wide, LANES):
                convolve_back(pl.multiple_of(base + RIM, RIM), base, PACK, first)
            return 0

        lax.fori_loop(0, groups, spread, 0)
        for first in range(0, wide, LANES):
            convolve_back(0, rows, RIM, first)


def mixer_backward(
    keep,
    pre,
    taps,
    valid,
    rate,
    bias,
    keys,
    inverse,
    w,
    u,
    fold,
    source,
    found,
    nexts,
    heads,
    key_width,
    value_width,
):
    rows = pre.shape[0] - RIM
    wide = heads * (2 * key_width + value_width)
    gate_wide = heads * value_width
    count = rows // GROUP
    whole = lambda shape: pl.BlockSpec(shape, lambda i: (0,) * len(shape))
    outs = [
        ((rows + RIM, wide), BF),
        ((rows + RIM, LANES), BF),
        ((8, wide), F32),
        ((8, LANES), F32),
    ]
    groups = rows // PACK
    step = PACK // GROUP * heads
    at = lambda i: jnp.maximum(i - 1, 0)
    rows_at = lambda width: pl.BlockSpec((PACK, width), lambda i: (at(i), 0))
    blocks_at = lambda many, shape: pl.BlockSpec((many,) + shape, lambda i: (at(i), 0, 0))
    true, whole_decays, renewed, base, key_part, query_conv, query_taps, along = found
    head_at = lambda i: jnp.where(at(i) == 0, rows // RIM, at(i) * (PACK // RIM) - 1)
    return pl.pallas_call(
        functools.partial(
            backward_kernel, heads=heads, rows=rows, key_width=key_width, value_width=value_width
        ),
        grid=(groups + 1,),
        in_specs=[
            pl.BlockSpec(memory_space=pltpu.SMEM),
            pl.BlockSpec((RIM, wide), lambda i: (head_at(i), 0)),
            rows_at(wide),
            pl.BlockSpec((PACK, LANES), lambda i: (at(i), (wide + gate_wide) // LANES)),
            whole(taps.shape),
            whole(valid.shape),
            whole(rate.shape),
            whole(bias.shape),
            rows_at(keys.shape[1]),
            blocks_at(heads, inverse.shape[1:]),
            rows_at(w.shape[1]),
            rows_at(u.shape[1]),
            whole(fold.shape),
            whole(source.shape),
            blocks_at(step, true.shape[1:]),
            whole(whole_decays.shape),
            rows_at(renewed.shape[1]),
            rows_at(base.shape[1]),
            rows_at(key_part.shape[1]),
            whole(query_conv.shape),
            whole(query_taps.shape),
            rows_at(along.shape[1]),
        ]
        + [whole(near.shape) for near in nexts],
        out_specs=[whole(shape) for shape, _ in outs],
        out_shape=[jax.ShapeDtypeStruct(shape, kind) for shape, kind in outs],
        scratch_shapes=[
            pltpu.VMEM((count * heads, key_width, value_width), BF),
            pltpu.VMEM((rows + 2 * RIM, wide), F32),
            pltpu.VMEM((heads, key_width, value_width), F32),
        ],
        compiler_params=pltpu.CompilerParams(vmem_limit_bytes=VMEM_LIMIT),
        cost_estimate=cost(25),
        name="mixer_backward",
    )(keep, pre, pre, pre, taps, valid, rate, bias, keys, inverse, w, u, fold, source, *found, *nexts)


def spread_into(piece, whole_shape, start, axis_number):
    return lax.dynamic_update_slice_in_dim(jnp.zeros(whole_shape, F32), piece, start, axis_number)


def lane_row(values):
    return jnp.pad(values, (0, LANES - values.shape[0]))[None, :]


def per_device(
    tokens,
    cotangent,
    lengths,
    norm_gain,
    query_weight,
    key_weight,
    value_weight,
    outgate_weight,
    alpha_weight,
    beta_weight,
    output_weight,
    conv_query,
    conv_key,
    conv_value,
    log_rate,
    step_bias,
    out_gain,
    ffn_gain,
    gate_weight,
    up_weight,
    down_weight,
):
    rows, slice_width = tokens.shape
    count = lax.axis_size("tensor")
    full_width = slice_width * count
    tensor_place = lax.axis_index("tensor")
    tensor_array = tensor_place.astype(jnp.int32)[None]
    place = lax.axis_index(FH)
    key_cols = query_weight.shape[1]
    value_cols = value_weight.shape[1]
    heads = alpha_weight.shape[1]
    key_width = key_cols // heads
    value_width = value_cols // heads
    wide = 2 * key_cols + value_cols
    reach = LONGEST // rows

    rim_slice = shifted(tokens[rows - RIM :], FH, 1)
    token_pieces = rotations(jnp.concatenate([tokens, rim_slice], axis=0), "tensor")
    small_shard = jnp.pad(
        jnp.concatenate([alpha_weight, beta_weight], axis=1), ((0, 0), (0, 2 * LANES - 2 * heads))
    )
    in_full = weight_rows(
        jnp.concatenate(
            [query_weight, key_weight, value_weight, outgate_weight, small_shard], axis=1
        ),
        0,
    )
    hidden = gate_weight.shape[1]
    room = ((0, 0), (0, padded(hidden) - hidden))
    down_full = weight_rows(jnp.concatenate([output_weight, down_weight], axis=0), 1)
    feed_full = weight_rows(
        jnp.concatenate([jnp.pad(gate_weight, room), jnp.pad(up_weight, room)], axis=1), 0
    )

    starts = jnp.cumsum(lengths) - lengths
    places = place * rows + jnp.arange(rows, dtype=jnp.int32)
    latest = jnp.max(jnp.where(starts[None, :] <= places[:, None], starts[None, :], 0), axis=1)
    tap_index = jnp.arange(8, dtype=jnp.int32)
    valid = ((places - latest)[:, None] >= CONV - 1 - tap_index[None, :]).astype(F32)
    valid_padded = jnp.pad(valid, ((RIM, RIM), (0, 0)))
    block_first = place * rows + jnp.arange(rows // GROUP, dtype=jnp.int32) * GROUP
    keep = 1.0 - jnp.any(block_first[:, None] == starts[None, :], axis=1).astype(F32)
    taps = jnp.concatenate(
        [
            lax.dynamic_slice_in_dim(conv_query, tensor_place * key_cols, key_cols, 1),
            lax.dynamic_slice_in_dim(conv_key, tensor_place * key_cols, key_cols, 1),
            lax.dynamic_slice_in_dim(conv_value, tensor_place * value_cols, value_cols, 1),
        ],
        axis=1,
    )
    rate = lane_row(lax.dynamic_slice_in_dim(log_rate, tensor_place * heads, heads))
    bias = lane_row(lax.dynamic_slice_in_dim(step_bias, tensor_place * heads, heads))
    gain_row = out_gain[None, :]
    norm_row = norm_gain[None, :]
    ffn_row = ffn_gain[None, :]

    token_rows, hidden_in, scale_in, pre = project(
        tensor_array, token_pieces, norm_row, in_full
    )
    cot_held, *_ = lax.optimization_barrier(
        (cotangent, down_full, feed_full, valid, keep, taps, rate, bias, *token_pieces[1:])
    )
    cot_rows = lax.all_gather(cot_held, "tensor", axis=1, tiled=True)

    keys, inverse, w, u, fold, states, end = mixer_forward(
        pre, keep, taps, valid, rate, bias, heads, key_width, value_width
    )
    queries, query_w, local, carry = mixer_query(
        pre, taps, valid, rate, bias, keys, w, u, states, heads, key_width, value_width
    )
    ends = [shifted(end, FH, by) for by in range(1, reach + 1)]
    ends[0], cot_rows = lax.optimization_barrier((ends[0], cot_rows))
    mixed, normed, enter, attn_parts = mixer_output(
        local,
        carry,
        ends,
        tensor_array,
        pre,
        gain_row,
        down_full,
        key_width,
        value_width,
        CHUNKS,
    )

    settled = mixer_true(pre, rate, bias, w, u, states, enter, heads, key_width, value_width)
    halves = [
        pair_half(*parts, settled if chunk == 0 else None) for chunk, parts in enumerate(attn_parts)
    ]
    attn_chunks = [pair_gather(pair_rest(*half).astype(BF)) for half in halves]
    true, whole_decays, renewed = settled
    kept, mid_parts = feed_forward(
        tensor_array, attn_chunks, cot_rows, token_rows, ffn_row, feed_full, down_full, hidden
    )
    middle, hidden_mid, inner_act, gate_grad, up_grad, *out_parts = kept
    back_kept, sums = (), []
    feed_local = weight_grads(
        (hidden_mid, gate_grad), (hidden_mid, up_grad), (cot_rows, inner_act)
    )
    halves = [
        pair_half(*parts, feed_local if chunk == 0 else None)
        for chunk, parts in enumerate(mid_parts)
    ]
    mid_chunks = [pair_gather(pair_rest(*half).astype(BF)) for half in halves]
    feed_grads = owners(feed_local)
    for chunk in range(CHUNKS):
        back_kept, found = gate_back(
            chunk,
            CHUNKS,
            tensor_array,
            mid_chunks[chunk],
            middle,
            cot_rows,
            ffn_row,
            down_full,
            mixed,
            pre,
            gain_row,
            query_w,
            states,
            back_kept,
            key_width,
            value_width,
        )
        sums.append(found)
    attn_grad, mixed_grad, outgate_grad, source, middle_grad_own = back_kept
    ffn_gain_grad, out_gain_grad, enter_grad = [sum(group[1:], group[0]) for group in zip(*sums)]

    enter_low = jnp.concatenate([enter_grad.astype(BF), end[:, :, value_width:]], axis=2)
    nexts = [shifted(enter_low, FH, -by) for by in range(1, reach + 1)]
    attn_held, feed_grads = lax.optimization_barrier((attn_grad, feed_grads))
    out_local = weight_grads((attn_held, normed), (hidden_in, outgate_grad))
    out_sums = lax.psum_scatter(out_local, FH, scatter_dimension=0, tiled=True)
    mixed_held, out_held = lax.optimization_barrier((mixed_grad, out_parts, out_local))[:2]
    found = mixer_ready(
        pre,
        taps,
        valid_padded,
        rate,
        bias,
        queries,
        keys,
        true,
        renewed,
        mixed_held,
        heads,
        key_width,
        value_width,
    )
    found = [true, whole_decays, renewed, *found]
    output_terms = out_held[0].astype(F32)
    for by in (1, 2, 3):
        output_terms = output_terms + paired(out_held[by], by).astype(F32)
    middle_own = lax.dynamic_slice_in_dim(middle, tensor_place * slice_width, slice_width, 1)
    output_rows = (middle_own + output_terms).astype(BF)
    pre_grad, small_grad, taps_grad, rate_grad = mixer_backward(
        keep,
        pre,
        taps,
        valid_padded,
        rate,
        bias,
        keys,
        inverse,
        w,
        u,
        fold,
        source,
        found,
        nexts,
        heads,
        key_width,
        value_width,
    )

    in_dot, norm_gain_grad, rim_terms, in_part = input_terms(
        tensor_array, pre_grad, small_grad, outgate_grad, in_full, token_rows, scale_in, norm_row, count
    )
    out_grads = out_sums.astype(F32)
    in_grad = lax.psum_scatter(in_part, "tensor", scatter_dimension=1, tiled=True).astype(F32)
    late_local = weight_grads((hidden_in, pre_grad), (hidden_in, small_grad))
    late_half, late_grads = owners_by_steps(late_local)
    rim = shifted(jnp.concatenate([rim_terms, in_dot[rows:]], axis=1), FH, -1)
    in_dot = in_dot[:rows, 0] + jnp.pad(rim[:, full_width], (rows - RIM, 0))
    rim_blocks = [
        lax.dynamic_slice_in_dim(
            rim, lax.rem(tensor_place + by, count) * slice_width, slice_width, 1
        ).reshape(-1)
        for by in range(count)
    ]

    own_gain_grad = lax.dynamic_slice_in_dim(
        ffn_gain_grad[0], tensor_place * slice_width, slice_width
    )
    pieces = (
        spread_into(taps_grad[:CONV, :key_cols], conv_query.shape, tensor_place * key_cols, 1),
        spread_into(
            taps_grad[:CONV, key_cols : 2 * key_cols], conv_key.shape, tensor_place * key_cols, 1
        ),
        spread_into(
            taps_grad[:CONV, 2 * key_cols :], conv_value.shape, tensor_place * value_cols, 1
        ),
        out_gain_grad[0],
        norm_gain_grad[0],
        spread_into(own_gain_grad, ffn_gain.shape, tensor_place * slice_width, 0),
        spread_into(rate_grad[0, :heads], log_rate.shape, tensor_place * heads, 0),
        spread_into(rate_grad[1, :heads], step_bias.shape, tensor_place * heads, 0),
    )
    flat = jnp.concatenate([piece.reshape(-1) for piece in pieces])
    flat = jnp.pad(flat, (0, -flat.size % (8 * LANES))).reshape(-1, LANES)
    flat = lax.optimization_barrier((flat, late_half))[0]
    flat = total_batches(flat).reshape(-1)
    joined = scattered(
        [jnp.concatenate([flat, in_dot, block]).reshape(-1, LANES) for block in rim_blocks], "tensor"
    ).reshape(-1)
    small, at = [], 0
    for piece in pieces:
        small.append(joined[at : at + piece.size].reshape(piece.shape))
        at += piece.size
    in_dot = joined[flat.size : flat.size + rows]
    rim_grad = joined[flat.size + rows :].reshape(RIM, slice_width)

    norm_slice = lax.dynamic_slice_in_dim(norm_gain, tensor_place * slice_width, slice_width)
    in_grad = in_grad + jnp.pad(rim_grad, ((rows - RIM, 0), (0, 0)))
    scale = scale_in[:rows, :1]
    tokens_grad = (
        middle_grad_own
        + scale * (in_grad * norm_slice)
        - tokens.astype(F32) * (scale * scale * scale * in_dot[:, None] / full_width)
    )

    return (
        output_rows,
        tokens_grad,
        late_grads[:, :key_cols],
        late_grads[:, key_cols : 2 * key_cols],
        late_grads[:, 2 * key_cols : wide],
        out_grads[:, value_cols:],
        late_grads[:, wide : wide + heads],
        late_grads[:, wide + heads : wide + 2 * heads],
        out_grads[:, :value_cols].T,
        feed_grads[:, :hidden],
        feed_grads[:, padded(hidden) : padded(hidden) + hidden],
        feed_grads[:, 2 * padded(hidden) : 2 * padded(hidden) + hidden].T,
        small[0],
        small[1],
        small[2],
        small[6],
        small[7],
        small[3],
        small[4],
        small[5],
    )


def solution(mesh):
    in_specs = (
        P(FH, "tensor"),
        P(FH, "tensor"),
        P(),
        P(),
        P("fsdp", "tensor"),
        P("fsdp", "tensor"),
        P("fsdp", "tensor"),
        P("fsdp", "tensor"),
        P("fsdp", "tensor"),
        P("fsdp", "tensor"),
        P("tensor", "fsdp"),
        P(),
        P(),
        P(),
        P(),
        P(),
        P(),
        P(),
        P("fsdp", "tensor"),
        P("fsdp", "tensor"),
        P("tensor", "fsdp"),
    )
    out_specs = (
        P(FH, "tensor"),
        P(FH, "tensor"),
        P(FH, "tensor"),
        P(FH, "tensor"),
        P(FH, "tensor"),
        P(FH, "tensor"),
        P(FH, "tensor"),
        P(FH, "tensor"),
        P("tensor", FH),
        P(FH, "tensor"),
        P(FH, "tensor"),
        P("tensor", FH),
        P(),
        P(),
        P(),
        P(),
        P(),
        P(),
        P(),
        P(),
    )
    return jax.shard_map(
        per_device, mesh=mesh, in_specs=in_specs, out_specs=out_specs, check_vma=False
    )
```
